512 devices in a mesh: dp: 64 (over z, x_lo, core), tensor: 8 (over y, x_hi).
Axes of the slice: x: 4 (x_hi: 2, x_lo: 2; x = x_hi * 2 + x_lo), y: 4, z: 16, core: 2. Of those that a mesh axis runs over, the one named last changes fastest.
Arguments:
- activations: bfloat16 [32768, 1024], P('dp', 'tensor'), may hold values from -16 to 16
- cotangent: bfloat16 [32768, 2, 1024], P('dp'), may hold values from -16 to 16
- weight: bfloat16 [1024, 2, 1024], P('tensor'), may hold values from -0.125 to 0.125
- owners: int32 [3], replicated, may hold values from 0 to 63
- worker_group: int32 [64], replicated, may hold values from 0 to 1, as said below
- basis_a: bfloat16 [64, 1024, 1024], P('dp', None, 'tensor'), may hold values from -0.1875 to 0.1875
- values_a: bfloat16 [64, 1024], P('dp', 'tensor'), may hold values from 0.0099487305 to 0.29882812
- basis_g: bfloat16 [64, 2, 1024, 1024], P('dp', None, None, 'tensor'), may hold values from -0.1875 to 0.1875
- values_g: bfloat16 [64, 2, 1024], P('dp', None, 'tensor'), may hold values from 0.0099487305 to 0.29882812
Outputs:
- grad_input: bfloat16 [32768, 1024], P('dp', 'tensor')
- factor_a: float32 [1024, 1024], P('dp', 'tensor')
- factor_g: float32 [1024, 2, 1024], P('dp', None, 'tensor')
- preconditioned: bfloat16 [1024, 2, 1024], P(None, None, 'tensor')
- worker_block: bfloat16 [64, 1024, 1024], P('dp', None, 'tensor')
The draws below stay inside these ranges and needn't reach their ends.
Inputs may be any that keep to these rules, and one draw needn't show every extreme that they name: `worker_group`: each of the 2 groups holds at least one replica.
All inputs are finite; a program needn't handle non-finite values.
Results may differ from the reference program's by a relative error of at most 0.01.
Values may be sent and summed in bfloat16 or wider, within the bound.
No kernel may reach another device: no remote copies, remote signals or barrier semaphores. Data moves between devices by JAX's collectives and lax.ppermute only.
A program may use at most 64 MiB of HBM per device.

```python
import math
import jax
import jax.numpy as jnp

BLK = 1024
NO = 2
TOKENS = 32768
N_DP = 64


def draw_worker_group(key, part):
    key = jax.random.fold_in(key, 7)
    first_key, second_key = jax.random.split(key)
    base_groups = jax.random.randint(first_key, (N_DP,), 0, NO)
    shuffled = jax.random.permutation(second_key, N_DP)
    return base_groups.at[shuffled[:NO]].set(jnp.arange(NO, dtype=jnp.int32)).astype(jnp.int32)


def strengthened(drawn, stream_key, source, target, blocks, factor):
    owner, partner = [(jnp.arange(drawn.shape[dim]) // (drawn.shape[dim] // blocks)).reshape([-1 if axis == dim else 1 for axis in range(drawn.ndim)]) for dim in (source, target)]
    chosen = jax.random.permutation(stream_key, blocks)[partner]
    strong = (owner == chosen) | (owner == (partner + blocks // 2) % blocks)
    return jnp.where(strong, factor * drawn, drawn)


def steps_of(own_key, extent, cuts, low, largest):
    level, own = 1.0, jax.random.fold_in(own_key, 6)
    for position, parts in cuts:
        draws = jnp.exp(jax.random.uniform(jax.random.fold_in(own, position), (parts,), jnp.float32, low / len(cuts), largest / len(cuts)))
        level = level * jnp.repeat(draws, extent[position] // parts).reshape([-1 if axis == position else 1 for axis in range(len(extent))])
    return level


def bell_draw(stream_key, extent, scale, bound, pieces=(), held_as=jnp.bfloat16):
    drawn = scale * jax.random.normal(stream_key, extent, jnp.float32)
    if pieces:
        drawn = drawn * steps_of(stream_key, extent, pieces, -0.22, 0.18)
    return jnp.clip(drawn, -bound, bound).astype(held_as)


def bell_draw_with(own_key, extent, spread, reach, shards, heavy, kind=jnp.bfloat16):
    entries = spread * jax.random.normal(own_key, extent, jnp.float32)
    if shards:
        entries = entries * steps_of(own_key, extent, shards, -0.22, 0.18)
    return jnp.clip(strengthened(entries, jax.random.fold_in(own_key, 3), *heavy), -reach, reach).astype(kind)


def setup_inputs(seed: int = 0) -> dict:
    key_of = jax.random.split(jax.random.key(seed), 10)
    activations = bell_draw_with(key_of[0], (TOKENS, BLK), 1.0, 16.0, ((0, 64), (1, 8)), (0, 1, 64, 4.0))
    cotangent = bell_draw_with(key_of[1], (TOKENS, NO, BLK), 1.0, 16.0, ((0, 64),), (0, 2, 64, 4.0))
    weight = bell_draw(key_of[2], (BLK, NO, BLK), (NO * BLK) ** -0.5, 0.125, ((0, 8),))
    owners = jax.random.randint(key_of[3], (NO + 1,), 0, N_DP).astype(jnp.int32)
    worker_group = draw_worker_group(jax.random.fold_in(key_of[9], 71), 0)
    basis_a = bell_draw(key_of[5], (N_DP, BLK, BLK), BLK ** -0.5, 0.1875, ((0, 64), (2, 8)))
    values_a = jnp.clip(jnp.exp(math.log(0.29882812) - 3.4024236 * jax.random.uniform(key_of[6], (N_DP, BLK), jnp.float32) ** steps_of(key_of[6], (N_DP, BLK), ((0, 64), (1, 8)), -0.2, 0.2)), 0.0099487305, 0.29882812).astype(jnp.bfloat16)
    basis_g = bell_draw(key_of[7], (N_DP, NO, BLK, BLK), BLK ** -0.5, 0.1875, ((0, 64), (3, 8)))
    values_g = jnp.clip(jnp.exp(math.log(0.29882812) - 3.4024236 * jax.random.uniform(key_of[8], (N_DP, NO, BLK), jnp.float32) ** steps_of(key_of[8], (N_DP, NO, BLK), ((0, 64), (2, 8)), -0.2, 0.2)), 0.0099487305, 0.29882812).astype(jnp.bfloat16)
    return dict(activations=activations, cotangent=cotangent, weight=weight, owners=owners, worker_group=worker_group, basis_a=basis_a, values_a=values_a, basis_g=basis_g, values_g=values_g)


damping = 1e-3


def reference(activations, cotangent, weight, owners, worker_group, basis_a, values_a, basis_g, values_g):
    flat_cot = cotangent.reshape(TOKENS, NO * BLK)
    flat_weight = weight.reshape(BLK, NO * BLK)
    grad_input = jnp.dot(flat_cot, flat_weight.T, preferred_element_type=jnp.float32).astype(jnp.bfloat16)
    gradient = jnp.dot(activations.T, flat_cot, preferred_element_type=jnp.float32) / TOKENS
    gradient = gradient.astype(jnp.bfloat16).reshape(BLK, NO, BLK)
    factor_a = jnp.dot(activations.T, activations, preferred_element_type=jnp.float32) / TOKENS
    factor_g = jnp.stack([jnp.dot(cotangent[:, block_index].T, cotangent[:, block_index], preferred_element_type=jnp.float32) / TOKENS for block_index in range(NO)], 1)
    whole_a = basis_a[owners[0]]
    eigen_a = values_a[owners[0]].astype(jnp.float32)
    results = []
    for block_index in range(NO):
        whole_g = basis_g[owners[1 + block_index], block_index]
        eigen_g = values_g[owners[1 + block_index], block_index].astype(jnp.float32)
        rotated = jnp.dot(whole_a.T, gradient[:, block_index], preferred_element_type=jnp.float32).astype(jnp.bfloat16)
        spectral = jnp.dot(rotated, whole_g, preferred_element_type=jnp.float32)
        scaled = (spectral / (eigen_a[:, None] * eigen_g[None, :] + damping)).astype(jnp.bfloat16)
        mixed = jnp.dot(scaled, whole_g.T, preferred_element_type=jnp.float32).astype(jnp.bfloat16)
        results.append(jnp.dot(whole_a, mixed, preferred_element_type=jnp.float32).astype(jnp.bfloat16))
    preconditioned = jnp.stack(results, 1)
    worker_block = jnp.transpose(jnp.take(preconditioned, worker_group, axis=1), (1, 0, 2))
    return grad_input, factor_a, factor_g, preconditioned, worker_block
```

```python
import jax
import jax.numpy as jnp
from jax import lax
from jax.sharding import Mesh, PartitionSpec as P

damping = 0.001
f32 = jnp.float32
bf16 = jnp.bfloat16


def exchange(array, axis):
    return lax.all_to_all(array, axis, 0, 0, tiled=True)


def swap(array, axis):
    return lax.ppermute(array, axis, [(0, 1), (1, 0)])


def pick(array, index, axis=0):
    return lax.dynamic_index_in_dim(array, index, axis, keepdims=False)


def add(left, right):
    return (left.astype(f32) + right.astype(f32)).astype(bf16)


def rows(array):
    return array.reshape(-1, array.shape[-1])


def cut(array, sizes):
    out, start = [], 0
    for size in sizes:
        out.append(lax.slice_in_dim(array, start, start + size, axis=array.ndim - 2))
        start += size
    return out


def repeat(array, count):
    return jnp.broadcast_to(array[None], (count,) + array.shape)


def local(act, cot, weight, owners, worker_group, basis_a, values_a, basis_g, values_g):
    tok, slab = act.shape
    blocks, full = cot.shape[1:]
    nz, nt = lax.axis_size("z"), lax.axis_size("t")
    z, xl, core, t = (lax.axis_index(name) for name in ("z", "xl", "c", "t"))
    scale = 1.0 / (tok * nz * 4)
    group = full // (nz * 4)
    half = full // 2
    piece = slab // 2

    owner_z, owner_x, owner_c = owners // 4, (owners // 2) % 2, owners % 2
    here_c, here_x = owner_c == core, owner_x == xl
    j_own = 1 + xl

    whole_act = exchange(jnp.broadcast_to(act[None], (nt, tok, slab)).reshape(nt * tok, slab), "t")
    whole_act = whole_act.reshape(nt, tok, slab)

    grad = jnp.einsum("tjb,ta->jba", cot, act, preferred_element_type=f32) * scale
    grad = grad.astype(bf16).reshape(blocks, nt, 2, piece, slab)
    own_cols = lax.dynamic_slice_in_dim(cot, t * slab, slab, 2)
    g_term = jnp.einsum("tja,tjb->jab", cot, own_cols, preferred_element_type=f32) * scale
    g_term = g_term.astype(bf16).reshape(blocks, nz, 2, 2, group, slab)

    qa = basis_a[0].reshape(2, half, slab)
    qg = basis_g[0].reshape(blocks, 2, half, slab)
    vals = jnp.concatenate(
        [values_a.reshape(1, slab), values_g.reshape(blocks, slab), jnp.zeros((5, slab), bf16)], 0
    )

    def for_core(index):
        return (
            pick(grad, index, 2).reshape(-1, slab),
            pick(g_term, index, 3).reshape(-1, slab),
            pick(qa, index, 0),
            pick(qg, index, 1).reshape(-1, slab),
        )

    sent = for_core(1 - core)
    mine = for_core(core)
    sizes = [part.shape[0] for part in sent]
    got = swap(jnp.concatenate(sent + (vals,), 0), "c")
    got_grad, got_g, got_qa, got_qg, got_vals = cut(got, sizes + [8])
    grad = add(mine[0], got_grad).reshape(blocks, nt * piece, slab)
    g_term = add(mine[1], got_g).reshape(blocks, nz, 2, group, slab)
    qa = jnp.where(here_c[0], mine[2], got_qa)
    qg = jnp.where(here_c[1:, None, None], mine[3].reshape(blocks, half, slab), got_qg.reshape(blocks, half, slab))
    flags = lambda here: jnp.concatenate([here, jnp.zeros((5,), here.dtype)])[:, None]
    vals = jnp.where(flags(here_c), vals, got_vals)

    def for_x(index):
        return (
            pick(grad, index),
            pick(g_term, index, 2).reshape(-1, slab),
            pick(qg, index),
        )

    sent = for_x(1 - xl)
    mine = for_x(xl)
    sizes = [part.shape[0] for part in sent]
    got = swap(jnp.concatenate(sent + (qa, vals), 0), "xl")
    got_grad, got_g, got_qg, got_qa, got_vals = cut(got, sizes + [half, 8])
    grad = add(mine[0], got_grad)
    g_term = add(mine[1], got_g).reshape(blocks, nz, group, slab)
    qg = jnp.where(pick(here_x, j_own), mine[2], got_qg)
    qa = jnp.where(here_x[0], qa, got_qa)
    vals = jnp.where(flags(here_x), vals, got_vals)

    per = half // nz
    sent = jnp.concatenate(
        [
            grad.reshape(nz, per, slab),
            g_term.transpose(1, 0, 2, 3).reshape(nz, blocks * group, slab),
            qa.reshape(nz, per, slab),
            qg.reshape(nz, per, slab),
            repeat(vals, nz),
        ],
        1,
    )
    got = exchange(sent, "z")
    got_grad, got_g, got_qa, got_qg, got_vals = cut(got, [per, blocks * group, per, per, 8])
    grad = jnp.sum(got_grad.astype(f32), 0).astype(bf16)
    factor_g = jnp.sum(got_g.astype(f32), 0).reshape(blocks, group, slab).transpose(1, 0, 2)
    qa = pick(got_qa, owner_z[0])
    qg = pick(got_qg, pick(owner_z, j_own))
    vals = jnp.stack(
        [pick(got_vals[:, 0], owner_z[0])]
        + [pick(got_vals[:, 1 + j], owner_z[1 + j]) for j in range(blocks)]
        + [jnp.zeros((slab,), bf16)] * 5,
        0,
    )

    a_term = jnp.einsum("ntf,tb->nfb", whole_act, act, preferred_element_type=f32) * scale
    a_term = a_term.astype(bf16).reshape(nz, 2, 2, group, slab)
    got = swap(pick(a_term, 1 - core, 2), "c")
    a_term = add(pick(a_term, core, 2), got)
    got = swap(pick(a_term, 1 - xl, 1), "xl")
    a_term = add(pick(a_term, xl, 1), got)

    sent = jnp.concatenate([repeat(jnp.concatenate([grad, qa, qg], 0), nz), a_term], 1)
    got = exchange(sent, "z")
    got_grad, got_qa, got_qg, got_a = cut(got, [per, per, per, group])
    factor_a = jnp.sum(got_a.astype(f32), 0)
    grad, qa, qg = rows(got_grad), rows(got_qa), rows(got_qg)

    sent = jnp.concatenate(
        [grad.reshape(nt, piece, slab), repeat(qa, nt), repeat(vals, nt)], 1
    )
    got = lax.all_gather(exchange(sent, "t"), "c", axis=0)
    grad, qa, vals = cut(got, [piece, half, 8])
    vals = vals[0].transpose(1, 0, 2).reshape(8, full).astype(f32)
    grad = grad.transpose(0, 2, 1, 3).reshape(slab, full)
    qa = qa.transpose(0, 2, 1, 3).reshape(full, full)
    qa_cols = lax.dynamic_slice_in_dim(qa, core * half, half, 1)
    rotated = lax.dot_general(
        qa_cols, grad, (((0,), (1,)), ((), ())), preferred_element_type=f32
    ).astype(bf16)

    sent = jnp.concatenate([rotated.reshape(nt, piece, slab), repeat(qg, nt)], 1)
    got_rot, got_qg = cut(exchange(sent, "t"), [piece, half])
    qg = lax.all_gather(got_qg, "c", axis=0).transpose(0, 2, 1, 3).reshape(full, full)
    rotated = got_rot.transpose(1, 0, 2).reshape(piece, full)
    spectral = jnp.dot(rotated, qg, preferred_element_type=f32)
    la = lax.dynamic_slice_in_dim(vals[0], core * half + t * piece, piece, 0)
    lg = pick(vals, j_own)
    scaled = (spectral / (la[:, None] * lg[None, :] + damping)).astype(bf16)
    mixed = lax.dot_general(
        scaled, qg, (((1,), (1,)), ((), ())), preferred_element_type=f32
    ).astype(bf16)

    sent = mixed.reshape(piece, nt, slab).transpose(1, 0, 2)
    got = exchange(repeat(sent, blocks).reshape(blocks * nt, piece, slab), ("xl", "t"))
    got = lax.all_gather(got.reshape(blocks, nt * piece, slab), "c", axis=0)
    mixed = got.transpose(0, 2, 1, 3).reshape(full, blocks * slab)
    pre = jnp.dot(qa, mixed, preferred_element_type=f32).astype(bf16).reshape(full, blocks, slab)
    worker = pick(pre, worker_group[(z * 2 + xl) * 2 + core], 1)[None]

    grad_input = lax.dot_general(
        cot, weight, (((1, 2), (1, 2)), ((), ())), preferred_element_type=f32
    ).astype(bf16)
    return grad_input, factor_a, factor_g, pre, worker


def solution(mesh):
    dp, tensor = mesh.devices.shape
    fine = Mesh(mesh.devices.reshape(dp // 4, 2, 2, tensor), ("z", "xl", "c", "t"))
    dp = ("z", "xl", "c")
    return jax.shard_map(
        local,
        mesh=fine,
        in_specs=(
            P(dp, "t"),
            P(dp, None, None),
            P("t", None, None),
            P(),
            P(),
            P(dp, None, "t"),
            P(dp, "t"),
            P(dp, None, None, "t"),
            P(dp, None, "t"),
        ),
        out_specs=(
            P(dp, "t"),
            P(dp, "t"),
            P(dp, None, "t"),
            P(None, None, "t"),
            P(dp, None, "t"),
        ),
        check_vma=False,
    )
```

```python
import functools

import jax
import jax.numpy as jnp
from jax import lax
from jax.experimental import pallas as pl
from jax.experimental.pallas import tpu as pltpu
from jax.sharding import Mesh, PartitionSpec as P

damping = 0.001
f32 = jnp.float32
bf16 = jnp.bfloat16
VALS = 16

Z, XL, CORE, T, OWNER, GROUP = 0, 1, 2, 3, 4, 7


def exchange(array, axis):
    return lax.all_to_all(array, axis, 0, 0, tiled=True)


def swap(array, axis):
    return lax.ppermute(array, axis, [(0, 1), (1, 0)])


def call(body, outs, info, *args, scratch=(), flops=0):
    bytes_all = sum(a.size * a.dtype.itemsize for a in args) + sum(
        o.size * o.dtype.itemsize for o in outs
    )
    return pl.pallas_call(
        body,
        out_shape=outs,
        in_specs=[pl.BlockSpec(memory_space=pltpu.SMEM)]
        + [pl.BlockSpec(memory_space=pltpu.VMEM)] * len(args),
        out_specs=[pl.BlockSpec(memory_space=pltpu.VMEM)] * len(outs),
        scratch_shapes=list(scratch),
        compiler_params=pltpu.CompilerParams(vmem_limit_bytes=40 * 1024 * 1024),
        cost_estimate=pl.CostEstimate(flops=flops, bytes_accessed=bytes_all, transcendentals=0),
    )(info, *args)


def out(shape, dtype=bf16):
    return jax.ShapeDtypeStruct(shape, dtype)


def dot(left, right, dims=((1,), (0,))):
    return lax.dot_general(left, right, (dims, ((), ())), preferred_element_type=f32)


def value_rows(flags, own, other):
    place = lax.broadcasted_iota(jnp.int32, own.shape, 0)
    take = jnp.zeros(own.shape, jnp.int32)
    for row, flag in enumerate(flags):
        take = jnp.where(place == row, flag.astype(jnp.int32), take)
    return jnp.where(take > 0, own.astype(f32), other.astype(f32)).astype(bf16)


def pack_bases(info, ba, bg, vals, sent):
    half = ba.shape[0] // 2
    start = pl.multiple_of((1 - info[CORE]) * half, half)
    sent[0:half] = ba[pl.ds(start, half)]
    for j in range(bg.shape[0]):
        sent[(1 + j) * half : (2 + j) * half] = bg[j, pl.ds(start, half)]
    sent[(1 + bg.shape[0]) * half :] = vals[...]


def select_core(info, ba, bg, vals, got, sent):
    half = ba.shape[0] // 2
    nz, _, slab = sent.shape
    per = half // nz
    core = info[CORE]
    start = pl.multiple_of(core * half, half)
    count = 1 + bg.shape[0]
    flags = [info[OWNER + i] % 2 == core for i in range(count)]
    for i in range(count):
        span = slice(i * per, (i + 1) * per)

        @pl.when(flags[i])
        def _():
            own = ba[pl.ds(start, half)] if i == 0 else bg[i - 1, pl.ds(start, half)]
            sent[:, span] = own.reshape(nz, per, slab)

        @pl.when(jnp.logical_not(flags[i]))
        def _():
            sent[:, span] = got[i * half : (i + 1) * half].reshape(nz, per, slab)

    chosen = value_rows(flags, vals[...], got[count * half :])
    for k in range(nz):
        sent[k, count * per :] = chosen


def select_z(info, got, sent, keep):
    per = (got.shape[1] - VALS) // 3
    xl = info[XL]
    source = [info[OWNER + i] // 4 for i in range(3)]

    def part(i):
        return got[source[i], i * per : (i + 1) * per]

    chosen = got[source[0], 3 * per :]
    for i in (1, 2):
        other = got[source[i], 3 * per :]
        place = lax.broadcasted_iota(jnp.int32, chosen.shape, 0)
        chosen = jnp.where(place == i, other.astype(f32), chosen.astype(f32)).astype(bf16)
    for ref in (sent, keep):
        ref[0:per] = part(0)
        ref[2 * per :] = chosen

    @pl.when(xl == 0)
    def _():
        keep[per : 2 * per] = part(1)
        sent[per : 2 * per] = part(2)

    @pl.when(xl == 1)
    def _():
        keep[per : 2 * per] = part(2)
        sent[per : 2 * per] = part(1)


def terms(info, x0, x1, act, own0, own1, sent, keep, packed):
    _, _, nz, height, slab = packed.shape
    full = x0.shape[1]
    nt = full // slab
    per = full // 2 // nz
    group = (height - per) // 2
    scale = 1.0 / (x0.shape[0] * nz * 4)
    for j, (x, own) in enumerate(((x0, own0), (x1, own1))):
        right = jnp.concatenate([act[...], own[...]], 1)
        both = dot(x[...], right, ((0,), (0,))) * scale
        grad = both[:, :slab].reshape(nt, 2, slab // 2, slab)
        cov = both[:, slab:].reshape(nz, 2, 2, group, slab)
        for c in range(2):
            packed[c, j, :, 0:per] = grad[:, c].reshape(nz, per, slab)
            for xl in range(2):
                packed[c, xl, :, per + j * group : per + (j + 1) * group] = cov[:, xl, c]
    core = info[CORE]
    sent[...] = packed[1 - core].astype(bf16)
    keep[...] = packed[core]


def add_core(info, keep, got, sent, rest):
    xl = info[XL]
    sent[...] = (keep[1 - xl] + got[1 - xl].astype(f32)).astype(bf16)
    rest[...] = keep[xl] + got[xl].astype(f32)


def pack_z(info, keep, got, base, other, sent, vals):
    nz, height, slab = keep.shape
    per = (base.shape[0] - VALS) // 2
    xl = info[XL]
    sent[:, 0:height] = (keep[...] + got[...].astype(f32)).astype(bf16)
    here = [(info[OWNER + i] // 2) % 2 == xl for i in range(3)]
    flag_a = here[0]
    flag_g = (info[OWNER + 1 + xl] // 2) % 2 == xl
    for i, flag in enumerate((flag_a, flag_g)):
        span = slice(i * per, (i + 1) * per)
        place = slice(height + i * per, height + (i + 1) * per)

        @pl.when(flag)
        def _():
            for k in range(nz):
                sent[k, place] = base[span]

        @pl.when(jnp.logical_not(flag))
        def _():
            for k in range(nz):
                sent[k, place] = other[span]

    vals[...] = value_rows(here, base[2 * per :], other[2 * per :])


def reduce_z(info, got, a_keep, a_got, sent, factor_g, qa, qg):
    nz, _, slab = got.shape
    half = qa.shape[0]
    per = half // nz
    group = factor_g.shape[1]
    total = got[0, 0 : per + 2 * group].astype(f32)
    for k in range(1, nz):
        total = total + got[k, 0 : per + 2 * group].astype(f32)
    grad = total[0:per].astype(bf16)
    for j in range(2):
        factor_g[j] = total[per + j * group : per + (j + 1) * group]
    for k in range(nz):
        sent[k, 0:per] = grad
    sent[:, per:] = (a_keep[...] + a_got[...].astype(f32)).astype(bf16)
    start = per + 2 * group
    qa[...] = got[:, start : start + per].reshape(half, slab)
    qg[...] = got[:, start + per : start + 2 * per].reshape(half, slab)


def pack_t(info, got, qa, vals, sent, factor_a):
    nz, _, slab = got.shape
    half = qa.shape[0]
    per = half // nz
    nt = sent.shape[0]
    piece = half // nt
    sent[:, 0:piece] = got[:, 0:per].reshape(half, slab).reshape(nt, piece, slab)
    for k in range(nt):
        sent[k, piece : piece + half] = qa[...]
        sent[k, piece + half :] = vals[...]
    total = got[0, per:].astype(f32)
    for k in range(1, nz):
        total = total + got[k, per:].astype(f32)
    factor_a[...] = total


def rotate(info, own, other, qg, sent, grad):
    nt, _, slab = own.shape
    half = qg.shape[0]
    piece = half // nt
    core = info[CORE]
    mine = pl.multiple_of(core * piece, piece)
    theirs = pl.multiple_of((1 - core) * piece, piece)
    for k in range(nt):
        grad[pl.ds(mine, piece), k * slab : (k + 1) * slab] = own[k, 0:piece]
        grad[pl.ds(theirs, piece), k * slab : (k + 1) * slab] = other[k, 0:piece]
    near = grad[:, pl.ds(pl.multiple_of(core * half, half), half)]
    far = grad[:, pl.ds(pl.multiple_of((1 - core) * half, half), half)]
    for i in range(nt // 2):
        k = core * (nt // 2) + i
        turned = dot(near, own[k, piece : piece + half]) + dot(far, other[k, piece : piece + half])
        turned = turned.T.astype(bf16)
        sent[2 * i, 0:piece] = turned[0:piece]
        sent[2 * i + 1, 0:piece] = turned[piece:]
    for k in range(nt):
        sent[k, piece:] = qg[...]


def scale_rows(info, own, other, gathered, sent, rot, scaled, column):
    nt, height, slab = own.shape
    piece = sent.shape[2]
    half = height - piece
    core, xl, t = info[CORE], info[XL], info[T]
    first = gathered.shape[1] - VALS
    row = gathered[core * (nt // 2) + t // 2, first:].astype(f32)[0:1]
    column[...] = jnp.broadcast_to(row, (slab, slab)).T
    la = column[pl.ds(pl.multiple_of((t % 2) * piece, piece), piece)]
    for k in range(nt):
        rot[:, k * slab : (k + 1) * slab] = own[k, 0:piece]
    near = rot[:, pl.ds(pl.multiple_of(core * half, half), half)]
    far = rot[:, pl.ds(pl.multiple_of((1 - core) * half, half), half)]
    for k in range(nt):
        spectral = dot(near, own[k, piece:]) + dot(far, other[k, piece:])
        values = gathered[k, first:].astype(f32)
        lg = jnp.where(xl == 0, values[1:2], values[2:3])
        scaled[k] = (spectral / (la * lg + damping)).astype(bf16)
    for side, ref in ((core, own), (1 - core, other)):
        mixed = dot(scaled[0], ref[0, piece:], ((1,), (1,)))
        for k in range(1, nt):
            mixed = mixed + dot(scaled[k], ref[k, piece:], ((1,), (1,)))
        mixed = mixed.astype(bf16)
        for i in range(nt // 2):
            for copy in range(2):
                sent[copy, side * (nt // 2) + i] = mixed[:, i * slab : (i + 1) * slab]


def finish(info, own, other, own_mixed, other_mixed, pre, worker):
    blocks, nt, piece, slab = own_mixed.shape
    half = pre.shape[1] // 2
    core = info[CORE]
    for side, ref in ((core, own), (1 - core, other)):
        total = jnp.zeros((half, blocks * slab), f32)
        for part, mixed in ((core, own_mixed), (1 - core, other_mixed)):
            for i in range(nt // 2):
                right = jnp.concatenate(
                    [mixed[j, 2 * i : 2 * i + 2].reshape(2 * piece, slab) for j in range(blocks)], 1
                )
                total = total + dot(ref[part * (nt // 2) + i, piece : piece + half], right)
        total = total.astype(bf16)
        place = pl.ds(pl.multiple_of(side * half, half), half)
        for j in range(blocks):
            pre[j, place] = total[:, j * slab : (j + 1) * slab]

        @pl.when(info[GROUP] == 0)
        def _():
            worker[0, place] = total[:, :slab]

        @pl.when(info[GROUP] == 1)
        def _():
            worker[0, place] = total[:, slab:]


def local(act, cot, weight, owners, worker_group, basis_a, values_a, basis_g, values_g):
    tok, slab = act.shape
    blocks, full = cot.shape[1:]
    nz, nt = lax.axis_size("z"), lax.axis_size("t")
    z, xl, core, t = (lax.axis_index(name) for name in ("z", "xl", "c", "t"))
    group = full // (nz * 4)
    half, piece = full // 2, slab // 2
    per = half // nz
    height = per + blocks * group
    replica = (z * 2 + xl) * 2 + core
    info = jnp.concatenate(
        [
            jnp.stack([z, xl, core, t]).astype(jnp.int32),
            owners,
            lax.dynamic_slice_in_dim(worker_group, replica, 1),
        ]
    )

    ba, bg = basis_a[0], basis_g[0]
    vals = jnp.concatenate([values_a, values_g[0], jnp.zeros((VALS - 3, slab), bf16)], 0)
    (sent,) = call(pack_bases, [out((3 * half + VALS, slab))], info, ba, bg, vals)
    got = swap(sent, "c")
    (sent,) = call(select_core, [out((nz, 3 * per + VALS, slab))], info, ba, bg, vals, got)
    got_bases = exchange(sent, "z")

    whole_act = lax.all_gather(act, "t", axis=1, tiled=True)

    x0, x1 = cot[:, 0], cot[:, 1]
    own0 = lax.dynamic_slice_in_dim(x0, t * slab, slab, 1)
    own1 = lax.dynamic_slice_in_dim(x1, t * slab, slab, 1)
    block = (2, nz, height, slab)
    sent, keep = call(
        terms,
        [out(block), out(block, f32)],
        info,
        x0,
        x1,
        act,
        own0,
        own1,
        scratch=[pltpu.VMEM((2,) + block, f32)],
        flops=8 * tok * full * slab,
    )
    got = swap(sent, "c")
    sent, keep = call(add_core, [out(block[1:]), out(block[1:], f32)], info, keep, got)
    got = swap(sent, "xl")

    shape = (2 * per + VALS, slab)
    base_sent, base_keep = call(select_z, [out(shape), out(shape)], info, got_bases)
    base_got = swap(base_sent, "xl")

    sent, vals = call(
        pack_z,
        [out((nz, height + 2 * per, slab)), out((VALS, slab))],
        info,
        keep,
        got,
        base_keep,
        base_got,
    )
    got = exchange(sent, "z")

    scale = 1.0 / (tok * nz * 4)
    a_term = dot(whole_act, act, ((0,), (0,))) * scale
    a_term = a_term.reshape(nz, 2, 2, group, slab)
    pick = functools.partial(lax.dynamic_index_in_dim, keepdims=False)
    a_got = swap(pick(a_term, 1 - core, 2).astype(bf16), "c")
    a_term = pick(a_term, core, 2) + a_got.astype(f32)
    a_got = swap(pick(a_term, 1 - xl, 1).astype(bf16), "xl")
    a_keep = pick(a_term, xl, 1)

    sent, factor_g, qa, qg = call(
        reduce_z,
        [out((nz, per + group, slab)), out((blocks, group, slab), f32), out((half, slab)), out((half, slab))],
        info,
        got,
        a_keep,
        a_got,
    )
    got = exchange(sent, "z")
    sent, factor_a = call(
        pack_t,
        [out((nt, piece + half + VALS, slab)), out((group, slab), f32)],
        info,
        got,
        qa,
        vals,
    )
    own = exchange(sent, "t")
    other = swap(own, "c")
    (sent,) = call(
        rotate,
        [out((nt, piece + half, slab))],
        info,
        own,
        other,
        qg,
        scratch=[pltpu.VMEM((slab, full), bf16)],
        flops=2 * slab * full * half,
    )
    own_rows = exchange(sent, "t")
    other_rows = swap(own_rows, "c")
    (sent,) = call(
        scale_rows,
        [out((blocks, nt, piece, slab))],
        info,
        own_rows,
        other_rows,
        own,
        scratch=[
            pltpu.VMEM((piece, full), bf16),
            pltpu.VMEM((nt, piece, slab), bf16),
            pltpu.VMEM((slab, slab), f32),
        ],
        flops=4 * piece * full * full,
    )
    own_mixed = exchange(sent.reshape(blocks * nt, piece, slab), ("xl", "t"))
    own_mixed = own_mixed.reshape(blocks, nt, piece, slab)
    other_mixed = swap(own_mixed, "c")
    pre, worker = call(
        finish,
        [out((blocks, full, slab)), out((1, full, slab))],
        info,
        own,
        other,
        own_mixed,
        other_mixed,
        flops=4 * full * full * slab,
    )

    grad_input = (dot(x0, weight[:, 0], ((1,), (1,))) + dot(x1, weight[:, 1], ((1,), (1,)))).astype(
        bf16
    )
    return (
        grad_input,
        factor_a,
        factor_g.transpose(1, 0, 2),
        pre.transpose(1, 0, 2),
        worker,
    )


def solution(mesh):
    dp, tensor = mesh.devices.shape
    fine = Mesh(mesh.devices.reshape(dp // 4, 2, 2, tensor), ("z", "xl", "c", "t"))
    dp = ("z", "xl", "c")
    return jax.shard_map(
        local,
        mesh=fine,
        in_specs=(
            P(dp, "t"),
            P(dp, None, None),
            P("t", None, None),
            P(),
            P(),
            P(dp, None, "t"),
            P(dp, "t"),
            P(dp, None, None, "t"),
            P(dp, None, "t"),
        ),
        out_specs=(
            P(dp, "t"),
            P(dp, "t"),
            P(dp, None, "t"),
            P(None, None, "t"),
            P(dp, None, "t"),
        ),
        check_vma=False,
    )
```

```python
import functools

import jax
import jax.numpy as jnp
from jax import lax
from jax.experimental import pallas as pl
from jax.experimental.pallas import tpu as pltpu
from jax.sharding import Mesh, PartitionSpec as P

damping = 0.001
f32 = jnp.float32
bf16 = jnp.bfloat16
VALS = 16


def exchange(array, axis):
    return lax.all_to_all(array, axis, 0, 0, tiled=True)


def swap(array, axis):
    return lax.ppermute(array, axis, [(0, 1), (1, 0)])


def across(array, axis, step):
    pairs = [(i, i ^ step) for i in range(lax.axis_size(axis))]
    return lax.ppermute(array, axis, pairs)


def call(body, outs, scalars, args, places=None, scratch=(), flops=0):
    bytes_all = sum(a.size * a.dtype.itemsize for a in args) + sum(
        o.size * o.dtype.itemsize for o in outs
    )
    places = places or [pltpu.VMEM] * len(args)
    return pl.pallas_call(
        body,
        out_shape=outs,
        in_specs=[pl.BlockSpec(memory_space=pltpu.SMEM)] * len(scalars)
        + [pl.BlockSpec(memory_space=place) for place in places],
        out_specs=[pl.BlockSpec(memory_space=pltpu.VMEM)] * len(outs),
        scratch_shapes=list(scratch),
        compiler_params=pltpu.CompilerParams(vmem_limit_bytes=40 * 1024 * 1024),
        cost_estimate=pl.CostEstimate(flops=flops, bytes_accessed=bytes_all, transcendentals=0),
    )(*scalars, *args)


def out(shape, dtype=bf16):
    return jax.ShapeDtypeStruct(shape, dtype)


def dot(left, right, dims=((1,), (0,))):
    return lax.dot_general(left, right, (dims, ((), ())), preferred_element_type=f32)


def value_rows(flags, own, other):
    place = lax.broadcasted_iota(jnp.int32, own.shape, 0)
    take = jnp.zeros(own.shape, jnp.int32)
    for row, flag in enumerate(flags):
        take = jnp.where(place == row, flag.astype(jnp.int32), take)
    return jnp.where(take > 0, own.astype(f32), other.astype(f32)).astype(bf16)


def choose(flag, ref, place, own, other):
    @pl.when(flag)
    def _():
        ref[place] = own()

    @pl.when(jnp.logical_not(flag))
    def _():
        ref[place] = other()


def pack_bases(ba, bg, va, vg, sent, keep, sem):
    half = ba.shape[1] // 2
    core = lax.axis_index("c")
    place = lax.broadcasted_iota(jnp.int32, (VALS, ba.shape[2]), 0)
    vals = jnp.where(place == 0, va[...].astype(f32), 0.0)
    for j in range(2):
        row = vg[0].astype(f32)[j : j + 1]
        vals = jnp.where(place == 1 + j, row, vals)
    copies = []
    for side, (ref, who) in enumerate(((sent, 1 - core), (keep, core))):
        rows = pl.ds(pl.multiple_of(who * half, half), half)
        for i in range(3):
            source = ba.at[0, rows] if i == 0 else bg.at[0, i - 1, rows]
            copies.append(
                pltpu.make_async_copy(source, ref.at[i * half : (i + 1) * half], sem.at[side, i])
            )
            copies[-1].start()
    sent[3 * half :] = vals.astype(bf16)
    keep[3 * half :] = vals.astype(bf16)
    for copy in copies:
        copy.wait()


def select_core(owners, own, got, sent, keep):
    half = (own.shape[0] - VALS) // 3
    core, xl = lax.axis_index("c"), lax.axis_index("xl")
    flags = [owners[i] % 2 == core for i in range(3)]

    def fill(ref, slot, i):
        start = pl.multiple_of(i * half, half)
        choose(
            owners[i] % 2 == core,
            ref,
            slice(slot * half, (slot + 1) * half),
            lambda: own[pl.ds(start, half)],
            lambda: got[pl.ds(start, half)],
        )

    vals = value_rows(flags, own[3 * half :], got[3 * half :])
    for ref, block in ((sent, 2 - xl), (keep, 1 + xl)):
        fill(ref, 0, 0)
        fill(ref, 1, block)
        ref[2 * half :] = vals


def select_x(owners, own, got, sent):
    nz, _, slab = sent.shape
    half = (own.shape[0] - VALS) // 2
    per = half // nz
    xl = lax.axis_index("xl")
    here = [(owners[i] // 2) % 2 == xl for i in range(3)]
    flags = (here[0], (owners[1 + xl] // 2) % 2 == xl)
    for i, flag in enumerate(flags):
        rows = slice(i * half, (i + 1) * half)
        choose(
            flag,
            sent,
            (slice(None), slice(i * per, (i + 1) * per)),
            lambda: own[rows].reshape(nz, per, slab),
            lambda: got[rows].reshape(nz, per, slab),
        )
    vals = value_rows(here, own[2 * half :], got[2 * half :])
    for k in range(nz):
        sent[k, 2 * per :] = vals


def terms(cot, act, sent, keep, packed, flat):
    _, _, nz, height, slab = packed.shape
    tok, blocks, full = cot.shape
    nt = full // slab
    per = full // 2 // nz
    group = (height - per) // 2
    scale = 1.0 / (tok * nz * 4)
    flat[...] = cot[...].reshape(tok, blocks * full)
    t = lax.axis_index("t")
    for j in range(2):
        own = flat[:, pl.ds(pl.multiple_of(j * full + t * slab, slab), slab)]
        right = jnp.concatenate([act[...], own], 1)
        both = dot(flat[:, j * full : (j + 1) * full], right, ((0,), (0,))) * scale
        grad = both[:, :slab].reshape(nt, 2, slab // 2, slab)
        cov = both[:, slab:].reshape(nz, 2, 2, group, slab)
        for c in range(2):
            packed[c, j, :, 0:per] = grad[:, c].reshape(nz, per, slab)
            for xl in range(2):
                packed[c, xl, :, per + j * group : per + (j + 1) * group] = cov[:, xl, c]
    core = lax.axis_index("c")
    sent[...] = packed[1 - core].astype(bf16)
    keep[...] = packed[core]


def add_core(keep, got, sent, rest):
    xl = lax.axis_index("xl")
    sent[...] = (keep[1 - xl] + got[1 - xl].astype(f32)).astype(bf16)
    rest[...] = keep[xl] + got[xl].astype(f32)


def pack_z(owners, keep, got, bases, sent, vals, cov):
    nz, height, slab = keep.shape
    per = (bases.shape[1] - VALS) // 2
    xl = lax.axis_index("xl")
    source = [owners[i] // 4 for i in range(3)]
    sent[:, 0:per] = (keep[:, 0:per] + got[:, 0:per].astype(f32)).astype(bf16)
    cov[...] = keep[:, per:] + got[:, per:].astype(f32)
    for i, src in enumerate((source[0], owners[1 + xl] // 4)):
        part = bases[src, i * per : (i + 1) * per]
        for k in range(nz):
            sent[k, (1 + i) * per : (2 + i) * per] = part
    chosen = bases[source[0], 2 * per :].astype(f32)
    place = lax.broadcasted_iota(jnp.int32, chosen.shape, 0)
    for i in (1, 2):
        chosen = jnp.where(place == i, bases[source[i], 2 * per :].astype(f32), chosen)
    vals[...] = chosen.astype(bf16)


def reduce_z(got, sent, bases):
    nz, height, slab = got.shape
    per = height // 3
    total = got[0, 0:per].astype(f32)
    for k in range(1, nz):
        total = total + got[k, 0:per].astype(f32)
    total = total.astype(bf16)
    for k in range(nz):
        sent[k] = total
    half = nz * per
    bases[0:half] = got[:, per : 2 * per].reshape(half, slab)
    bases[half:] = got[:, 2 * per :].reshape(half, slab)


def stack_bases(*refs):
    pieces, whole = refs[:-1], refs[-1]
    t = lax.axis_index("t")
    for k, piece in enumerate(pieces):
        whole[t ^ k] = piece[...]


def pack_t(got, vals, sent):
    nz, per, slab = got.shape
    nt, height, _ = sent.shape[1:]
    piece = height - VALS
    grad = got[...].reshape(nz * per, slab).reshape(nt, piece, slab)
    for c in range(2):
        sent[c, :, 0:piece] = grad
        for k in range(nt):
            sent[c, k, piece:] = vals[...]


def rotate(got, own, other, sent, grad):
    nt, height, slab = own.shape
    half = height // 2
    piece = half // nt
    core = lax.axis_index("c")
    for c in range(2):
        for k in range(nt):
            grad[c * piece : (c + 1) * piece, k * slab : (k + 1) * slab] = got[c, k, 0:piece]
    near = grad[:, pl.ds(pl.multiple_of(core * half, half), half)]
    far = grad[:, pl.ds(pl.multiple_of((1 - core) * half, half), half)]
    for i in range(nt // 2):
        k = core * (nt // 2) + i
        turned = dot(near, own[k, 0:half]) + dot(far, other[k, 0:half])
        turned = turned.T.astype(bf16)
        sent[2 * i] = turned[0:piece]
        sent[2 * i + 1] = turned[piece:]


def scale_rows(rows, own, other, got, sent, rot, scaled, column):
    nt, piece, slab = rows.shape
    half = own.shape[1] // 2
    core, xl, t = lax.axis_index("c"), lax.axis_index("xl"), lax.axis_index("t")
    row = got[0, core * (nt // 2) + t // 2, piece:].astype(f32)[0:1]
    column[...] = jnp.broadcast_to(row, (slab, slab)).T
    la = column[pl.ds(pl.multiple_of((t % 2) * piece, piece), piece)]
    for k in range(nt):
        rot[:, k * slab : (k + 1) * slab] = rows[k]
    near = rot[:, pl.ds(pl.multiple_of(core * half, half), half)]
    far = rot[:, pl.ds(pl.multiple_of((1 - core) * half, half), half)]
    for k in range(nt):
        spectral = dot(near, own[k, half:]) + dot(far, other[k, half:])
        values = got[0, k, piece:].astype(f32)
        lg = jnp.where(xl == 0, values[1:2], values[2:3])
        scaled[k] = (spectral / (la * lg + damping)).astype(bf16)
    for side, ref in ((core, own), (1 - core, other)):
        mixed = dot(scaled[0], ref[0, half:], ((1,), (1,)))
        for k in range(1, nt):
            mixed = mixed + dot(scaled[k], ref[k, half:], ((1,), (1,)))
        mixed = mixed.astype(bf16)
        for i in range(nt // 2):
            for copy in range(2):
                sent[copy, side * (nt // 2) + i] = mixed[:, i * slab : (i + 1) * slab]


def finish(groups, own, other, own_mixed, other_mixed, pre, worker):
    blocks, nt, piece, slab = own_mixed.shape
    half = own.shape[1] // 2
    core = lax.axis_index("c")
    replica = (lax.axis_index("z") * 2 + lax.axis_index("xl")) * 2 + core
    group = groups[replica]
    for side, ref in ((core, own), (1 - core, other)):
        total = jnp.zeros((half, blocks * slab), f32)
        for part, mixed in ((core, own_mixed), (1 - core, other_mixed)):
            for i in range(nt // 2):
                right = jnp.concatenate(
                    [mixed[j, 2 * i : 2 * i + 2].reshape(2 * piece, slab) for j in range(blocks)], 1
                )
                total = total + dot(ref[part * (nt // 2) + i, 0:half], right)
        total = total.astype(bf16)
        place = pl.ds(pl.multiple_of(side * half, half), half)
        pre[place] = total.reshape(half, blocks, slab)
        choose(
            group == 0,
            worker,
            (0, place),
            lambda: total[:, :slab],
            lambda: total[:, slab:],
        )


def input_grad(cot, weight, grad):
    tok, blocks, full = cot.shape
    left = cot[...].reshape(tok, blocks * full)
    right = weight[...].reshape(weight.shape[0], blocks * full)
    grad[...] = dot(left, right, ((1,), (1,))).astype(bf16)


def input_factor(whole, act, sent, keep, packed):
    nz, _, _, group, slab = packed.shape
    scale = 1.0 / (act.shape[0] * nz * 4)
    packed[...] = (dot(whole[...], act[...], ((0,), (0,))) * scale).reshape(packed.shape)
    core = lax.axis_index("c")
    sent[...] = packed[:, :, 1 - core].astype(bf16)
    keep[...] = packed[:, :, core]


def input_factor_core(keep, got, sent, rest):
    xl = lax.axis_index("xl")
    sent[...] = (keep[:, 1 - xl] + got[:, 1 - xl].astype(f32)).astype(bf16)
    rest[...] = keep[:, xl] + got[:, xl].astype(f32)


def pack_factors(cov, keep, got, sent):
    group = keep.shape[1]
    sent[:, 0 : 2 * group] = cov[...].astype(bf16)
    sent[:, 2 * group :] = (keep[...] + got[...].astype(f32)).astype(bf16)


def local(act, cot, weight, owners, worker_group, basis_a, values_a, basis_g, values_g):
    tok, slab = act.shape
    blocks, full = cot.shape[1:]
    nz, nt = lax.axis_size("z"), lax.axis_size("t")
    group = full // (nz * 4)
    half, piece = full // 2, slab // 2
    per = half // nz
    height = per + blocks * group

    shape = (3 * half + VALS, slab)
    sent, keep = call(
        pack_bases,
        [out(shape), out(shape)],
        [],
        [basis_a, basis_g, values_a, values_g],
        [pl.ANY, pl.ANY, pltpu.VMEM, pltpu.VMEM],
        scratch=[pltpu.SemaphoreType.DMA((2, 3))],
    )
    got = swap(sent, "c")
    shape = (2 * half + VALS, slab)
    sent, keep = call(select_core, [out(shape), out(shape)], [owners], [keep, got])
    got = swap(sent, "xl")
    (sent,) = call(select_x, [out((nz, 2 * per + VALS, slab))], [owners], [keep, got])
    got_bases = exchange(sent, "z")

    whole_act = lax.all_gather(act, "t", axis=1, tiled=True)

    block = (2, nz, height, slab)
    sent, keep = call(
        terms,
        [out(block), out(block, f32)],
        [],
        [cot, act],
        scratch=[pltpu.VMEM((2,) + block, f32), pltpu.VMEM((tok, blocks * full), bf16)],
        flops=8 * tok * full * slab,
    )
    got = swap(sent, "c")
    sent, keep = call(add_core, [out(block[1:]), out(block[1:], f32)], [], [keep, got])
    got = swap(sent, "xl")

    sent, vals, cov = call(
        pack_z,
        [out((nz, 3 * per, slab)), out((VALS, slab)), out((nz, 2 * group, slab), f32)],
        [owners],
        [keep, got, got_bases],
    )
    got = exchange(sent, "z")

    block = (nz, 2, group, slab)
    sent, keep = call(
        input_factor,
        [out(block), out(block, f32)],
        [],
        [whole_act, act],
        scratch=[pltpu.VMEM((nz, 2, 2, group, slab), f32)],
        flops=2 * tok * full * slab,
    )
    a_got = swap(sent, "c")
    block = (nz, group, slab)
    sent, keep = call(input_factor_core, [out(block), out(block, f32)], [], [keep, a_got])
    a_got = swap(sent, "xl")
    (sent,) = call(pack_factors, [out((nz, 3 * group, slab))], [], [cov, keep, a_got])
    factors = lax.psum_scatter(sent, "z", scatter_dimension=0, tiled=False).astype(f32)
    factor_g = factors[: 2 * group].reshape(blocks, group, slab).transpose(1, 0, 2)
    factor_a = factors[2 * group :]

    sent, bases = call(
        reduce_z, [out((nz, per, slab)), out((2 * half, slab))], [], [got]
    )
    got = exchange(sent, "z")
    pieces = [bases] + [across(bases, "t", k) for k in range(1, nt)]
    (own,) = call(stack_bases, [out((nt, 2 * half, slab))], [], pieces)
    other = swap(own, "c")

    (sent,) = call(pack_t, [out((2, nt, piece + VALS, slab))], [], [got, vals])
    columns = exchange(sent.reshape(2 * nt, piece + VALS, slab), ("c", "t"))
    columns = columns.reshape(2, nt, piece + VALS, slab)
    (sent,) = call(
        rotate,
        [out((nt, piece, slab))],
        [],
        [columns, own, other],
        scratch=[pltpu.VMEM((slab, full), bf16)],
        flops=2 * slab * full * half,
    )
    rows = exchange(sent, "t")
    (sent,) = call(
        scale_rows,
        [out((blocks, nt, piece, slab))],
        [],
        [rows, own, other, columns],
        scratch=[
            pltpu.VMEM((piece, full), bf16),
            pltpu.VMEM((nt, piece, slab), bf16),
            pltpu.VMEM((slab, slab), f32),
        ],
        flops=4 * piece * full * full,
    )
    own_mixed = exchange(sent.reshape(blocks * nt, piece, slab), ("xl", "t"))
    own_mixed = own_mixed.reshape(blocks, nt, piece, slab)
    other_mixed = swap(own_mixed, "c")
    pre, worker = call(
        finish,
        [out((full, blocks, slab)), out((1, full, slab))],
        [worker_group],
        [own, other, own_mixed, other_mixed],
        flops=4 * full * full * slab,
    )

    (grad_input,) = call(
        input_grad, [out((tok, slab))], [], [cot, weight], flops=4 * tok * full * slab
    )
    return grad_input, factor_a, factor_g, pre, worker


def solution(mesh):
    dp, tensor = mesh.devices.shape
    fine = Mesh(mesh.devices.reshape(dp // 4, 2, 2, tensor), ("z", "xl", "c", "t"))
    dp = ("z", "xl", "c")
    return jax.shard_map(
        local,
        mesh=fine,
        in_specs=(
            P(dp, "t"),
            P(dp, None, None),
            P("t", None, None),
            P(),
            P(),
            P(dp, None, "t"),
            P(dp, "t"),
            P(dp, None, None, "t"),
            P(dp, None, "t"),
        ),
        out_specs=(
            P(dp, "t"),
            P(dp, "t"),
            P(dp, None, "t"),
            P(None, None, "t"),
            P(dp, None, "t"),
        ),
        check_vma=False,
    )
```

```python
import functools

import jax
import jax.numpy as jnp
from jax import lax
from jax.experimental import pallas as pl
from jax.experimental.pallas import tpu as pltpu
from jax.sharding import Mesh, PartitionSpec as P

damping = 0.001
f32 = jnp.float32
bf16 = jnp.bfloat16
VALS = 16


def exchange(array, axis):
    return lax.all_to_all(array, axis, 0, 0, tiled=True)


def swap(array, axis):
    return lax.ppermute(array, axis, [(0, 1), (1, 0)])


def across(array, axis, step):
    pairs = [(i, i ^ step) for i in range(lax.axis_size(axis))]
    return lax.ppermute(array, axis, pairs)


def call(body, outs, scalars, args, places=None, scratch=(), flops=0):
    bytes_all = sum(a.size * a.dtype.itemsize for a in args) + sum(
        o.size * o.dtype.itemsize for o in outs
    )
    places = places or [pltpu.VMEM] * len(args)
    return pl.pallas_call(
        body,
        out_shape=outs,
        in_specs=[pl.BlockSpec(memory_space=pltpu.SMEM)] * len(scalars)
        + [pl.BlockSpec(memory_space=place) for place in places],
        out_specs=[pl.BlockSpec(memory_space=pltpu.VMEM)] * len(outs),
        scratch_shapes=list(scratch),
        compiler_params=pltpu.CompilerParams(vmem_limit_bytes=40 * 1024 * 1024),
        cost_estimate=pl.CostEstimate(flops=flops, bytes_accessed=bytes_all, transcendentals=0),
    )(*scalars, *args)


def out(shape, dtype=bf16):
    return jax.ShapeDtypeStruct(shape, dtype)


def dot(left, right, dims=((1,), (0,))):
    return lax.dot_general(left, right, (dims, ((), ())), preferred_element_type=f32)


def value_rows(flags, own, other):
    place = lax.broadcasted_iota(jnp.int32, own.shape, 0)
    take = jnp.zeros(own.shape, jnp.int32)
    for row, flag in enumerate(flags):
        take = jnp.where(place == row, flag.astype(jnp.int32), take)
    return jnp.where(take > 0, own.astype(f32), other.astype(f32)).astype(bf16)


def choose(flag, ref, place, own, other):
    @pl.when(flag)
    def _():
        ref[place] = own()

    @pl.when(jnp.logical_not(flag))
    def _():
        ref[place] = other()


def pack_bases(ba, bg, va, vg, sent, keep, sem):
    half = ba.shape[1] // 2
    core = lax.axis_index("c")
    place = lax.broadcasted_iota(jnp.int32, (VALS, ba.shape[2]), 0)
    vals = jnp.where(place == 0, va[...].astype(f32), 0.0)
    for j in range(2):
        row = vg[0].astype(f32)[j : j + 1]
        vals = jnp.where(place == 1 + j, row, vals)
    copies = []
    for side, (ref, who) in enumerate(((sent, 1 - core), (keep, core))):
        rows = pl.ds(pl.multiple_of(who * half, half), half)
        for i in range(3):
            source = ba.at[0, rows] if i == 0 else bg.at[0, i - 1, rows]
            copies.append(
                pltpu.make_async_copy(source, ref.at[i * half : (i + 1) * half], sem.at[side, i])
            )
            copies[-1].start()
    sent[3 * half :] = vals.astype(bf16)
    keep[3 * half :] = vals.astype(bf16)
    for copy in copies:
        copy.wait()


def select_core(owners, own, got, sent, keep):
    half = (own.shape[0] - VALS) // 3
    core, xl = lax.axis_index("c"), lax.axis_index("xl")
    flags = [owners[i] % 2 == core for i in range(3)]

    def fill(ref, slot, i):
        start = pl.multiple_of(i * half, half)
        choose(
            owners[i] % 2 == core,
            ref,
            slice(slot * half, (slot + 1) * half),
            lambda: own[pl.ds(start, half)],
            lambda: got[pl.ds(start, half)],
        )

    vals = value_rows(flags, own[3 * half :], got[3 * half :])
    for ref, block in ((sent, 2 - xl), (keep, 1 + xl)):
        fill(ref, 0, 0)
        fill(ref, 1, block)
        ref[2 * half :] = vals


def select_x(owners, own, got, sent):
    nz, _, slab = sent.shape
    half = (own.shape[0] - VALS) // 2
    per = half // nz
    xl = lax.axis_index("xl")
    here = [(owners[i] // 2) % 2 == xl for i in range(3)]
    flags = (here[0], (owners[1 + xl] // 2) % 2 == xl)
    for i, flag in enumerate(flags):
        rows = slice(i * half, (i + 1) * half)
        choose(
            flag,
            sent,
            (slice(None), slice(i * per, (i + 1) * per)),
            lambda: own[rows].reshape(nz, per, slab),
            lambda: got[rows].reshape(nz, per, slab),
        )
    vals = value_rows(here, own[2 * half :], got[2 * half :])
    for k in range(nz):
        sent[k, 2 * per :] = vals


def terms(cot, act, sent, keep, packed, flat):
    _, _, nz, height, slab = packed.shape
    tok, blocks, full = cot.shape
    nt = full // slab
    per = full // 2 // nz
    group = (height - per) // 2
    scale = 1.0 / (tok * nz * 4)
    flat[...] = cot[...].reshape(tok, blocks * full)
    t = lax.axis_index("t")
    for j in range(2):
        own = flat[:, pl.ds(pl.multiple_of(j * full + t * slab, slab), slab)]
        right = jnp.concatenate([act[...], own], 1)
        both = dot(flat[:, j * full : (j + 1) * full], right, ((0,), (0,))) * scale
        grad = both[:, :slab].reshape(nt, 2, slab // 2, slab)
        cov = both[:, slab:].reshape(nz, 2, 2, group, slab)
        for c in range(2):
            packed[c, j, :, 0:per] = grad[:, c].reshape(nz, per, slab)
            for xl in range(2):
                packed[c, xl, :, per + j * group : per + (j + 1) * group] = cov[:, xl, c]
    core = lax.axis_index("c")
    sent[...] = packed[1 - core].astype(bf16)
    keep[...] = packed[core]


def add_core(keep, got, sent, rest):
    xl = lax.axis_index("xl")
    sent[...] = (keep[1 - xl] + got[1 - xl].astype(f32)).astype(bf16)
    rest[...] = keep[xl] + got[xl].astype(f32)


def pack_z(owners, keep, got, bases, sent, vals):
    nz, height, slab = keep.shape
    per = (bases.shape[1] - VALS) // 2
    xl = lax.axis_index("xl")
    source = [owners[i] // 4 for i in range(3)]
    sent[:, 0:height] = (keep[...] + got[...].astype(f32)).astype(bf16)
    for i, src in enumerate((source[0], owners[1 + xl] // 4)):
        part = bases[src, i * per : (i + 1) * per]
        for k in range(nz):
            sent[k, height + i * per : height + (i + 1) * per] = part
    chosen = bases[source[0], 2 * per :].astype(f32)
    place = lax.broadcasted_iota(jnp.int32, chosen.shape, 0)
    for i in (1, 2):
        chosen = jnp.where(place == i, bases[source[i], 2 * per :].astype(f32), chosen)
    vals[...] = chosen.astype(bf16)


def reduce_z(got, a_keep, a_got, sent, factor_g, bases):
    nz, _, slab = got.shape
    group = a_keep.shape[1]
    half = bases.shape[0] // 2
    per = half // nz
    height = per + 2 * group
    total = got[0, 0:height].astype(f32)
    for k in range(1, nz):
        total = total + got[k, 0:height].astype(f32)
    grad = total[0:per].astype(bf16)
    for k in range(nz):
        sent[k, 0:per] = grad
    sent[:, per:] = (a_keep[...] + a_got[...].astype(f32)).astype(bf16)
    for j in range(2):
        factor_g[j] = total[per + j * group : per + (j + 1) * group]
    bases[0:half] = got[:, height : height + per].reshape(half, slab)
    bases[half:] = got[:, height + per :].reshape(half, slab)


def pair_bases(own, got, qa, qg):
    half = own.shape[0] // 2
    side = lax.axis_index("t") % 2
    for slot, ref in ((side, own), (1 - side, got)):
        qa[slot] = ref[0:half]
        qg[slot] = ref[half:]


def stack_pairs(own, one, two, three, after, whole):
    first = lax.axis_index("t") // 2
    for k, pair in enumerate((own, one, two, three)):
        for side in range(2):
            whole[2 * (first ^ k) + side] = pair[side]


def pack_t(got, vals, pair, sent, factor_a, same):
    nz, height, slab = got.shape
    group = factor_a.shape[0]
    per = height - group
    nt, width, _ = sent.shape[1:]
    piece = width - VALS
    grad = got[:, 0:per].reshape(nz * per, slab).reshape(nt, piece, slab)
    for c in range(2):
        sent[c, :, 0:piece] = grad
        for k in range(nt):
            sent[c, k, piece:] = vals[...]
    total = got[0, per:].astype(f32)
    for k in range(1, nz):
        total = total + got[k, per:].astype(f32)
    factor_a[...] = total
    same[...] = pair[...]


def rotate(got, own, other, sent, grad):
    nt, half, slab = own.shape
    piece = half // nt
    core = lax.axis_index("c")
    for c in range(2):
        for k in range(nt):
            grad[c * piece : (c + 1) * piece, k * slab : (k + 1) * slab] = got[c, k, 0:piece]
    near = grad[:, pl.ds(pl.multiple_of(core * half, half), half)]
    far = grad[:, pl.ds(pl.multiple_of((1 - core) * half, half), half)]
    for i in range(nt // 2):
        k = core * (nt // 2) + i
        turned = dot(near, own[k]) + dot(far, other[k])
        turned = turned.T.astype(bf16)
        sent[2 * i] = turned[0:piece]
        sent[2 * i + 1] = turned[piece:]


def scale_rows(rows, own, other, got, sent, rot, scaled, column):
    nt, piece, slab = rows.shape
    half = own.shape[1]
    core, xl, t = lax.axis_index("c"), lax.axis_index("xl"), lax.axis_index("t")
    row = got[0, core * (nt // 2) + t // 2, piece:].astype(f32)[0:1]
    column[...] = jnp.broadcast_to(row, (slab, slab)).T
    la = column[pl.ds(pl.multiple_of((t % 2) * piece, piece), piece)]
    for k in range(nt):
        rot[:, k * slab : (k + 1) * slab] = rows[k]
    near = rot[:, pl.ds(pl.multiple_of(core * half, half), half)]
    far = rot[:, pl.ds(pl.multiple_of((1 - core) * half, half), half)]
    for k in range(nt):
        spectral = dot(near, own[k]) + dot(far, other[k])
        values = got[0, k, piece:].astype(f32)
        lg = jnp.where(xl == 0, values[1:2], values[2:3])
        scaled[k] = (spectral / (la * lg + damping)).astype(bf16)
    for side, ref in ((core, own), (1 - core, other)):
        mixed = dot(scaled[0], ref[0], ((1,), (1,)))
        for k in range(1, nt):
            mixed = mixed + dot(scaled[k], ref[k], ((1,), (1,)))
        mixed = mixed.astype(bf16)
        for i in range(nt // 2):
            for copy in range(2):
                sent[copy, side * (nt // 2) + i] = mixed[:, i * slab : (i + 1) * slab]


def finish(groups, own, other, own_mixed, other_mixed, pre, worker):
    blocks, nt, piece, slab = own_mixed.shape
    half = own.shape[1]
    core = lax.axis_index("c")
    replica = (lax.axis_index("z") * 2 + lax.axis_index("xl")) * 2 + core
    group = groups[replica]
    for side, ref in ((core, own), (1 - core, other)):
        total = jnp.zeros((half, blocks * slab), f32)
        for part, mixed in ((core, own_mixed), (1 - core, other_mixed)):
            for i in range(nt // 2):
                right = jnp.concatenate(
                    [mixed[j, 2 * i : 2 * i + 2].reshape(2 * piece, slab) for j in range(blocks)], 1
                )
                total = total + dot(ref[part * (nt // 2) + i], right)
        total = total.astype(bf16)
        place = pl.ds(pl.multiple_of(side * half, half), half)
        pre[place] = total.reshape(half, blocks, slab)
        choose(
            group == 0,
            worker,
            (0, place),
            lambda: total[:, :slab],
            lambda: total[:, slab:],
        )


def input_grad(cot, weight, grad):
    tok, blocks, full = cot.shape
    left = cot[...].reshape(tok, blocks * full)
    right = weight[...].reshape(weight.shape[0], blocks * full)
    grad[...] = dot(left, right, ((1,), (1,))).astype(bf16)


def input_factor(whole, act, sent, keep, packed):
    nz, _, _, group, slab = packed.shape
    scale = 1.0 / (act.shape[0] * nz * 4)
    packed[...] = (dot(whole[...], act[...], ((0,), (0,))) * scale).reshape(packed.shape)
    core = lax.axis_index("c")
    sent[...] = packed[:, :, 1 - core].astype(bf16)
    keep[...] = packed[:, :, core]


def input_factor_core(keep, got, sent, rest):
    xl = lax.axis_index("xl")
    sent[...] = (keep[:, 1 - xl] + got[:, 1 - xl].astype(f32)).astype(bf16)
    rest[...] = keep[:, xl] + got[:, xl].astype(f32)


def local(act, cot, weight, owners, worker_group, basis_a, values_a, basis_g, values_g):
    tok, slab = act.shape
    blocks, full = cot.shape[1:]
    nz, nt = lax.axis_size("z"), lax.axis_size("t")
    group = full // (nz * 4)
    half, piece = full // 2, slab // 2
    per = half // nz
    height = per + blocks * group

    shape = (3 * half + VALS, slab)
    sent, keep = call(
        pack_bases,
        [out(shape), out(shape)],
        [],
        [basis_a, basis_g, values_a, values_g],
        [pltpu.HBM, pltpu.HBM, pltpu.VMEM, pltpu.VMEM],
        scratch=[pltpu.SemaphoreType.DMA((2, 3))],
    )
    got = swap(sent, "c")
    shape = (2 * half + VALS, slab)
    sent, keep = call(select_core, [out(shape), out(shape)], [owners], [keep, got])
    got = swap(sent, "xl")
    (sent,) = call(select_x, [out((nz, 2 * per + VALS, slab))], [owners], [keep, got])
    got_bases = exchange(sent, "z")

    whole_act = lax.all_gather(act, "t", axis=1, tiled=True)

    block = (2, nz, height, slab)
    sent, keep = call(
        terms,
        [out(block), out(block, f32)],
        [],
        [cot, act],
        scratch=[pltpu.VMEM((2,) + block, f32), pltpu.VMEM((tok, blocks * full), bf16)],
        flops=8 * tok * full * slab,
    )
    got = swap(sent, "c")
    sent, keep = call(add_core, [out(block[1:]), out(block[1:], f32)], [], [keep, got])
    got = swap(sent, "xl")

    sent, vals = call(
        pack_z,
        [out((nz, height + 2 * per, slab)), out((VALS, slab))],
        [owners],
        [keep, got, got_bases],
    )
    got = exchange(sent, "z")

    block = (nz, 2, group, slab)
    sent, keep = call(
        input_factor,
        [out(block), out(block, f32)],
        [],
        [whole_act, act],
        scratch=[pltpu.VMEM((nz, 2, 2, group, slab), f32)],
        flops=2 * tok * full * slab,
    )
    a_got = swap(sent, "c")
    block = (nz, group, slab)
    sent, keep = call(input_factor_core, [out(block), out(block, f32)], [], [keep, a_got])
    a_got = swap(sent, "xl")

    sent, factor_g, bases = call(
        reduce_z,
        [out((nz, per + group, slab)), out((blocks, group, slab), f32), out((2 * half, slab))],
        [],
        [got, keep, a_got],
    )
    pair = out((2, half, slab))
    whole = out((nt, half, slab))
    orders = [pltpu.VMEM] * 4 + [pl.ANY]
    got = exchange(sent, "z")
    near = across(bases, "t", 1)
    qa, qg = call(pair_bases, [pair, pair], [], [bases, near])
    pairs = [qa] + [across(qa, "t", 2 * k) for k in range(1, nt // 2)]
    (qa_own,) = call(stack_pairs, [whole], [], pairs + [got], orders)
    qa_other = swap(qa_own, "c")

    sent, factor_a, qg = call(
        pack_t,
        [out((2, nt, piece + VALS, slab)), out((group, slab), f32), pair],
        [],
        [got, vals, qg],
    )
    columns = exchange(sent.reshape(2 * nt, piece + VALS, slab), ("c", "t"))
    columns = columns.reshape(2, nt, piece + VALS, slab)
    pairs = [qg] + [across(qg, "t", 2 * k) for k in range(1, nt // 2)]
    (qg_own,) = call(stack_pairs, [whole], [], pairs + [columns], orders)
    qg_other = swap(qg_own, "c")
    (sent,) = call(
        rotate,
        [out((nt, piece, slab))],
        [],
        [columns, qa_own, qa_other],
        scratch=[pltpu.VMEM((slab, full), bf16)],
        flops=2 * slab * full * half,
    )
    rows = exchange(sent, "t")
    (sent,) = call(
        scale_rows,
        [out((blocks, nt, piece, slab))],
        [],
        [rows, qg_own, qg_other, columns],
        scratch=[
            pltpu.VMEM((piece, full), bf16),
            pltpu.VMEM((nt, piece, slab), bf16),
            pltpu.VMEM((slab, slab), f32),
        ],
        flops=4 * piece * full * full,
    )
    own_mixed = exchange(sent.reshape(blocks * nt, piece, slab), ("xl", "t"))
    own_mixed = own_mixed.reshape(blocks, nt, piece, slab)
    other_mixed = swap(own_mixed, "c")
    pre, worker = call(
        finish,
        [out((full, blocks, slab)), out((1, full, slab))],
        [worker_group],
        [qa_own, qa_other, own_mixed, other_mixed],
        flops=4 * full * full * slab,
    )

    (grad_input,) = call(
        input_grad, [out((tok, slab))], [], [cot, weight], flops=4 * tok * full * slab
    )
    return grad_input, factor_a, factor_g.transpose(1, 0, 2), pre, worker


def solution(mesh):
    dp, tensor = mesh.devices.shape
    fine = Mesh(mesh.devices.reshape(dp // 4, 2, 2, tensor), ("z", "xl", "c", "t"))
    dp = ("z", "xl", "c")
    return jax.shard_map(
        local,
        mesh=fine,
        in_specs=(
            P(dp, "t"),
            P(dp, None, None),
            P("t", None, None),
            P(),
            P(),
            P(dp, None, "t"),
            P(dp, "t"),
            P(dp, None, None, "t"),
            P(dp, None, "t"),
        ),
        out_specs=(
            P(dp, "t"),
            P(dp, "t"),
            P(dp, None, "t"),
            P(None, None, "t"),
            P(dp, None, "t"),
        ),
        check_vma=False,
    )
```

```python
import functools

import jax
import jax.numpy as jnp
from jax import lax
from jax.experimental import pallas as pl
from jax.experimental.pallas import tpu as pltpu
from jax.sharding import Mesh, PartitionSpec as P

damping = 0.001
f32 = jnp.float32
bf16 = jnp.bfloat16
VALS = 16


def exchange(array, axis):
    return lax.all_to_all(array, axis, 0, 0, tiled=True)


def swap(array, axis):
    return lax.ppermute(array, axis, [(0, 1), (1, 0)])


def call(body, outs, scalars, args, places=None, scratch=(), flops=0, limit=40):
    places = places or [pltpu.VMEM] * len(args)
    specs, arrays = [], []
    for arg, place in zip(args, places):
        if isinstance(arg, tuple):
            array, rows, block = arg
            shape = (array.shape[0], rows, array.shape[2])
            specs.append(pl.BlockSpec(shape, functools.partial(lambda k, i: (0, k, 0), block)))
        else:
            array = arg
            specs.append(pl.BlockSpec(memory_space=place))
        arrays.append(array)
    bytes_all = sum(a.size * a.dtype.itemsize for a in arrays + list(outs))
    return pl.pallas_call(
        body,
        grid=(1,),
        out_shape=outs,
        in_specs=[pl.BlockSpec(memory_space=pltpu.SMEM)] * len(scalars) + specs,
        out_specs=[pl.BlockSpec(memory_space=pltpu.VMEM)] * len(outs),
        scratch_shapes=list(scratch),
        compiler_params=pltpu.CompilerParams(vmem_limit_bytes=limit * 1024 * 1024),
        cost_estimate=pl.CostEstimate(flops=flops, bytes_accessed=bytes_all, transcendentals=0),
    )(*scalars, *arrays)


def out(shape, dtype=bf16):
    return jax.ShapeDtypeStruct(shape, dtype)


def dot(left, right, dims=((1,), (0,))):
    return lax.dot_general(left, right, (dims, ((), ())), preferred_element_type=f32)


def value_rows(flags, own, other):
    place = lax.broadcasted_iota(jnp.int32, own.shape, 0)
    take = jnp.zeros(own.shape, jnp.int32)
    for row, flag in enumerate(flags):
        take = jnp.where(place == row, flag.astype(jnp.int32), take)
    return jnp.where(take > 0, own.astype(f32), other.astype(f32)).astype(bf16)


def choose(flag, ref, place, own, other):
    @pl.when(flag)
    def _():
        ref[place] = own()

    @pl.when(jnp.logical_not(flag))
    def _():
        ref[place] = other()


def pack_bases(ba, bg, va, vg, sent, keep, sem):
    half = ba.shape[1] // 2
    core = lax.axis_index("c")
    place = lax.broadcasted_iota(jnp.int32, (VALS, ba.shape[2]), 0)
    vals = jnp.where(place == 0, va[...].astype(f32), 0.0)
    for j in range(2):
        row = vg[0].astype(f32)[j : j + 1]
        vals = jnp.where(place == 1 + j, row, vals)
    copies = []
    for side, (ref, who) in enumerate(((sent, 1 - core), (keep, core))):
        rows = pl.ds(pl.multiple_of(who * half, half), half)
        for i in range(3):
            source = ba.at[0, rows] if i == 0 else bg.at[0, i - 1, rows]
            copies.append(
                pltpu.make_async_copy(source, ref.at[i * half : (i + 1) * half], sem.at[side, i])
            )
            copies[-1].start()
    sent[3 * half :] = vals.astype(bf16)
    keep[3 * half :] = vals.astype(bf16)
    for copy in copies:
        copy.wait()


def select_core(owners, own, got, sent, keep):
    half = (own.shape[0] - VALS) // 3
    core, xl = lax.axis_index("c"), lax.axis_index("xl")
    flags = [owners[i] % 2 == core for i in range(3)]

    def fill(ref, slot, i):
        start = pl.multiple_of(i * half, half)
        choose(
            owners[i] % 2 == core,
            ref,
            slice(slot * half, (slot + 1) * half),
            lambda: own[pl.ds(start, half)],
            lambda: got[pl.ds(start, half)],
        )

    vals = value_rows(flags, own[3 * half :], got[3 * half :])
    for ref, block in ((sent, 2 - xl), (keep, 1 + xl)):
        fill(ref, 0, 0)
        fill(ref, 1, block)
        ref[2 * half :] = vals


def select_x(owners, own, got, sent):
    nz, _, slab = sent.shape
    half = (own.shape[0] - VALS) // 2
    per = half // nz
    xl = lax.axis_index("xl")
    here = [(owners[i] // 2) % 2 == xl for i in range(3)]
    flags = (here[0], (owners[1 + xl] // 2) % 2 == xl)
    for i, flag in enumerate(flags):
        rows = slice(i * half, (i + 1) * half)
        choose(
            flag,
            sent,
            (slice(None), slice(i * per, (i + 1) * per)),
            lambda: own[rows].reshape(nz, per, slab),
            lambda: got[rows].reshape(nz, per, slab),
        )
    vals = value_rows(here, own[2 * half :], got[2 * half :])
    for k in range(nz):
        sent[k, 2 * per :] = vals


def terms(cot, act, whole, sent, keep, packed, flat, cov):
    _, _, nz, height, slab = packed.shape
    tok, blocks, full = cot.shape
    nt = full // slab
    per = full // 2 // nz
    group = (height - per) // 3
    scale = 1.0 / (tok * nz * 4)
    flat[...] = cot[...].reshape(tok, blocks * full)
    t = lax.axis_index("t")
    for k in range(nt):
        cov[k * slab : (k + 1) * slab] = dot(whole[k], act[...], ((0,), (0,))) * scale
    place = slice(per + 2 * group, height)
    for c in range(2):
        for xl in range(2):
            packed[c, xl, :, place] = cov[...].reshape(nz, 2, 2, group, slab)[:, xl, c]
    for j in range(2):
        own = flat[:, pl.ds(pl.multiple_of(j * full + t * slab, slab), slab)]
        right = jnp.concatenate([act[...], own], 1)
        both = dot(flat[:, j * full : (j + 1) * full], right, ((0,), (0,))) * scale
        grad = both[:, :slab].reshape(nt, 2, slab // 2, slab)
        out_cov = both[:, slab:].reshape(nz, 2, 2, group, slab)
        for c in range(2):
            packed[c, j, :, 0:per] = grad[:, c].reshape(nz, per, slab)
            for xl in range(2):
                packed[c, xl, :, per + j * group : per + (j + 1) * group] = out_cov[:, xl, c]
    core = lax.axis_index("c")
    sent[...] = packed[1 - core].astype(bf16)
    keep[...] = packed[core]


def add_core(keep, got, sent, rest):
    xl = lax.axis_index("xl")
    sent[...] = (keep[1 - xl] + got[1 - xl].astype(f32)).astype(bf16)
    rest[...] = keep[xl] + got[xl].astype(f32)


def pack_z(owners, keep, got, bases, sent, vals):
    nz, height, slab = keep.shape
    per = (bases.shape[1] - VALS) // 2
    xl = lax.axis_index("xl")
    source = [owners[i] // 4 for i in range(3)]
    sent[:, 0:height] = (keep[...] + got[...].astype(f32)).astype(bf16)
    for i, src in enumerate((source[0], owners[1 + xl] // 4)):
        part = bases[src, i * per : (i + 1) * per]
        for k in range(nz):
            sent[k, height + i * per : height + (i + 1) * per] = part
    chosen = bases[source[0], 2 * per :].astype(f32)
    place = lax.broadcasted_iota(jnp.int32, chosen.shape, 0)
    for i in (1, 2):
        chosen = jnp.where(place == i, bases[source[i], 2 * per :].astype(f32), chosen)
    vals[...] = chosen.astype(bf16)


def reduce_z(got, vals, grad, factor_a, factor_g, sent):
    nz, _, slab = got.shape
    group = factor_a.shape[0]
    per = grad.shape[0]
    half = nz * per
    height = per + 3 * group
    total = got[0, 0:height].astype(f32)
    for k in range(1, nz):
        total = total + got[k, 0:height].astype(f32)
    grad[...] = total[0:per].astype(bf16)
    for j in range(2):
        factor_g[j] = total[per + j * group : per + (j + 1) * group]
    factor_a[...] = total[per + 2 * group :]
    for k in range(sent.shape[0]):
        sent[k, 0:half] = got[:, height : height + per].reshape(half, slab)
        sent[k, half : 2 * half] = got[:, height + per :].reshape(half, slab)
        sent[k, 2 * half :] = vals[...]


def pack_t(grad, sent):
    nt, piece, slab = sent.shape[1:]
    for c in range(2):
        sent[c] = grad[...].reshape(nt, piece, slab)


def rotate(got, own, other, sent, grad):
    nt, half, slab = own.shape
    piece = half // nt
    core = lax.axis_index("c")
    for c in range(2):
        for k in range(nt):
            grad[c * piece : (c + 1) * piece, k * slab : (k + 1) * slab] = got[c, k, 0:piece]
    near = grad[:, pl.ds(pl.multiple_of(core * half, half), half)]
    far = grad[:, pl.ds(pl.multiple_of((1 - core) * half, half), half)]
    for i in range(nt // 2):
        k = core * (nt // 2) + i
        turned = dot(near, own[k]) + dot(far, other[k])
        turned = turned.T.astype(bf16)
        sent[2 * i] = turned[0:piece]
        sent[2 * i + 1] = turned[piece:]


def scale_rows(rows, own, other, vals, sent, rot, scaled, column):
    nt, piece, slab = rows.shape
    half = own.shape[1]
    core, xl, t = lax.axis_index("c"), lax.axis_index("xl"), lax.axis_index("t")
    row = vals[core * (nt // 2) + t // 2].astype(f32)[0:1]
    column[...] = jnp.broadcast_to(row, (slab, slab)).T
    la = column[pl.ds(pl.multiple_of((t % 2) * piece, piece), piece)]
    for k in range(nt):
        rot[:, k * slab : (k + 1) * slab] = rows[k]
    near = rot[:, pl.ds(pl.multiple_of(core * half, half), half)]
    far = rot[:, pl.ds(pl.multiple_of((1 - core) * half, half), half)]
    for k in range(nt):
        spectral = dot(near, own[k]) + dot(far, other[k])
        values = vals[k].astype(f32)
        lg = jnp.where(xl == 0, values[1:2], values[2:3])
        scaled[k] = (spectral / (la * lg + damping)).astype(bf16)
    for side, ref in ((core, own), (1 - core, other)):
        mixed = dot(scaled[0], ref[0], ((1,), (1,)))
        for k in range(1, nt):
            mixed = mixed + dot(scaled[k], ref[k], ((1,), (1,)))
        mixed = mixed.astype(bf16)
        for i in range(nt // 2):
            for copy in range(2):
                sent[copy, side * (nt // 2) + i] = mixed[:, i * slab : (i + 1) * slab]


def finish(groups, own, other, own_mixed, other_mixed, pre, worker):
    blocks, nt, piece, slab = own_mixed.shape
    half = own.shape[1]
    core = lax.axis_index("c")
    replica = (lax.axis_index("z") * 2 + lax.axis_index("xl")) * 2 + core
    group = groups[replica]
    for side, ref in ((core, own), (1 - core, other)):
        total = jnp.zeros((half, blocks * slab), f32)
        for part, mixed in ((core, own_mixed), (1 - core, other_mixed)):
            for i in range(nt // 2):
                right = jnp.concatenate(
                    [mixed[j, 2 * i : 2 * i + 2].reshape(2 * piece, slab) for j in range(blocks)], 1
                )
                total = total + dot(ref[part * (nt // 2) + i], right)
        total = total.astype(bf16)
        place = pl.ds(pl.multiple_of(side * half, half), half)
        pre[place] = total.reshape(half, blocks, slab)
        choose(
            group == 0,
            worker,
            (0, place),
            lambda: total[:, :slab],
            lambda: total[:, slab:],
        )


def input_grad(cot, weight, grad):
    tok, blocks, full = cot.shape
    left = cot[...].reshape(tok, blocks * full)
    right = weight[...].reshape(weight.shape[0], blocks * full)
    grad[...] = dot(left, right, ((1,), (1,))).astype(bf16)


def local(act, cot, weight, owners, worker_group, basis_a, values_a, basis_g, values_g):
    tok, slab = act.shape
    blocks, full = cot.shape[1:]
    nz, nt = lax.axis_size("z"), lax.axis_size("t")
    group = full // (nz * 4)
    half, piece = full // 2, slab // 2
    per = half // nz
    height = per + (blocks + 1) * group

    whole_act = exchange(jnp.broadcast_to(act[None], (nt, tok, slab)), "t")

    shape = (3 * half + VALS, slab)
    sent, keep = call(
        pack_bases,
        [out(shape), out(shape)],
        [],
        [basis_a, basis_g, values_a, values_g],
        [pl.ANY, pl.ANY, pltpu.VMEM, pltpu.VMEM],
        scratch=[pltpu.SemaphoreType.DMA((2, 3))],
        limit=56,
    )
    got = swap(sent, "c")
    shape = (2 * half + VALS, slab)
    sent, keep = call(select_core, [out(shape), out(shape)], [owners], [keep, got])
    got = swap(sent, "xl")
    (sent,) = call(select_x, [out((nz, 2 * per + VALS, slab))], [owners], [keep, got])
    got_bases = exchange(sent, "z")

    block = (2, nz, height, slab)
    sent, keep = call(
        terms,
        [out(block), out(block, f32)],
        [],
        [cot, act, whole_act],
        scratch=[
            pltpu.VMEM((2,) + block, f32),
            pltpu.VMEM((tok, blocks * full), bf16),
            pltpu.VMEM((full, slab), f32),
        ],
        flops=10 * tok * full * slab,
    )
    got = swap(sent, "c")
    sent, keep = call(add_core, [out(block[1:]), out(block[1:], f32)], [], [keep, got])
    got = swap(sent, "xl")

    sent, vals = call(
        pack_z,
        [out((nz, height + 2 * per, slab)), out((VALS, slab))],
        [owners],
        [keep, got, got_bases],
    )
    got = exchange(sent, "z")

    width = 2 * half + VALS
    grad, factor_a, factor_g, sent = call(
        reduce_z,
        [
            out((per, slab)),
            out((group, slab), f32),
            out((blocks, group, slab), f32),
            out((nt, width, slab)),
        ],
        [],
        [got, vals],
    )
    own = exchange(sent, "t")
    grad = lax.all_gather(grad, "z", axis=0, tiled=True)
    other = swap(own, "c")

    (sent,) = call(pack_t, [out((2, nt, piece, slab))], [], [grad])
    columns = exchange(sent.reshape(2 * nt, piece, slab), ("c", "t"))
    columns = columns.reshape(2, nt, piece, slab)
    (sent,) = call(
        rotate,
        [out((nt, piece, slab))],
        [],
        [columns, (own, half, 0), (other, half, 0)],
        scratch=[pltpu.VMEM((slab, full), bf16)],
        flops=2 * slab * full * half,
    )
    rows = exchange(sent, "t")
    (sent,) = call(
        scale_rows,
        [out((blocks, nt, piece, slab))],
        [],
        [rows, (own, half, 1), (other, half, 1), (own, VALS, 2 * half // VALS)],
        scratch=[
            pltpu.VMEM((piece, full), bf16),
            pltpu.VMEM((nt, piece, slab), bf16),
            pltpu.VMEM((slab, slab), f32),
        ],
        flops=4 * piece * full * full,
    )
    own_mixed = exchange(sent.reshape(blocks * nt, piece, slab), ("xl", "t"))
    own_mixed = own_mixed.reshape(blocks, nt, piece, slab)
    other_mixed = swap(own_mixed, "c")
    pre, worker = call(
        finish,
        [out((full, blocks, slab)), out((1, full, slab))],
        [worker_group],
        [(own, half, 0), (other, half, 0), own_mixed, other_mixed],
        flops=4 * full * full * slab,
    )

    (grad_input,) = call(
        input_grad, [out((tok, slab))], [], [cot, weight], flops=4 * tok * full * slab
    )
    return grad_input, factor_a, factor_g.transpose(1, 0, 2), pre, worker


def solution(mesh):
    dp, tensor = mesh.devices.shape
    fine = Mesh(mesh.devices.reshape(dp // 4, 2, 2, tensor), ("z", "xl", "c", "t"))
    dp = ("z", "xl", "c")
    return jax.shard_map(
        local,
        mesh=fine,
        in_specs=(
            P(dp, "t"),
            P(dp, None, None),
            P("t", None, None),
            P(),
            P(),
            P(dp, None, "t"),
            P(dp, "t"),
            P(dp, None, None, "t"),
            P(dp, None, "t"),
        ),
        out_specs=(
            P(dp, "t"),
            P(dp, "t"),
            P(dp, None, "t"),
            P(None, None, "t"),
            P(dp, None, "t"),
        ),
        check_vma=False,
    )
```

```python
import functools

import jax
import jax.numpy as jnp
from jax import lax
from jax.experimental import pallas as pl
from jax.experimental.pallas import tpu as pltpu
from jax.sharding import Mesh, PartitionSpec as P

damping = 0.001
f32 = jnp.float32
bf16 = jnp.bfloat16
VALS = 16


def exchange(array, axis):
    return lax.all_to_all(array, axis, 0, 0, tiled=True)


def swap(array, axis):
    return lax.ppermute(array, axis, [(0, 1), (1, 0)])


def call(body, outs, scalars, args, places=None, scratch=(), flops=0, limit=40):
    places = places or [pltpu.VMEM] * len(args)
    specs, arrays = [], []
    for arg, place in zip(args, places):
        if isinstance(arg, tuple):
            array, rows, block = arg
            shape = (array.shape[0], rows, array.shape[2])
            specs.append(pl.BlockSpec(shape, functools.partial(lambda k, i: (0, k, 0), block)))
        else:
            array = arg
            specs.append(pl.BlockSpec(memory_space=place))
        arrays.append(array)
    bytes_all = sum(a.size * a.dtype.itemsize for a in arrays + list(outs))
    return pl.pallas_call(
        body,
        grid=(1,),
        out_shape=outs,
        in_specs=[pl.BlockSpec(memory_space=pltpu.SMEM)] * len(scalars) + specs,
        out_specs=[pl.BlockSpec(memory_space=pltpu.VMEM)] * len(outs),
        scratch_shapes=list(scratch),
        compiler_params=pltpu.CompilerParams(vmem_limit_bytes=limit * 1024 * 1024),
        cost_estimate=pl.CostEstimate(flops=flops, bytes_accessed=bytes_all, transcendentals=0),
    )(*scalars, *arrays)


def out(shape, dtype=bf16):
    return jax.ShapeDtypeStruct(shape, dtype)


def dot(left, right, dims=((1,), (0,))):
    return lax.dot_general(left, right, (dims, ((), ())), preferred_element_type=f32)


def value_rows(flags, own, other):
    place = lax.broadcasted_iota(jnp.int32, own.shape, 0)
    take = jnp.zeros(own.shape, jnp.int32)
    for row, flag in enumerate(flags):
        take = jnp.where(place == row, flag.astype(jnp.int32), take)
    return jnp.where(take > 0, own.astype(f32), other.astype(f32)).astype(bf16)


def choose(flag, ref, place, own, other):
    @pl.when(flag)
    def _():
        ref[place] = own()

    @pl.when(jnp.logical_not(flag))
    def _():
        ref[place] = other()


def pack_bases(ba, bg, va, vg, sent, keep, sem):
    half = ba.shape[1] // 2
    core = lax.axis_index("c")
    place = lax.broadcasted_iota(jnp.int32, (VALS, ba.shape[2]), 0)
    vals = jnp.where(place == 0, va[...].astype(f32), 0.0)
    for j in range(2):
        row = vg[0].astype(f32)[j : j + 1]
        vals = jnp.where(place == 1 + j, row, vals)
    copies = []
    for side, (ref, who) in enumerate(((sent, 1 - core), (keep, core))):
        rows = pl.ds(pl.multiple_of(who * half, half), half)
        for i in range(3):
            source = ba.at[0, rows] if i == 0 else bg.at[0, i - 1, rows]
            copies.append(
                pltpu.make_async_copy(source, ref.at[i * half : (i + 1) * half], sem.at[side, i])
            )
            copies[-1].start()
    sent[3 * half :] = vals.astype(bf16)
    keep[3 * half :] = vals.astype(bf16)
    for copy in copies:
        copy.wait()


def select_core(owners, own, got, sent, keep):
    half = (own.shape[0] - VALS) // 3
    core, xl = lax.axis_index("c"), lax.axis_index("xl")
    flags = [owners[i] % 2 == core for i in range(3)]

    def fill(ref, slot, i):
        start = pl.multiple_of(i * half, half)
        choose(
            owners[i] % 2 == core,
            ref,
            slice(slot * half, (slot + 1) * half),
            lambda: own[pl.ds(start, half)],
            lambda: got[pl.ds(start, half)],
        )

    vals = value_rows(flags, own[3 * half :], got[3 * half :])
    for ref, block in ((sent, 2 - xl), (keep, 1 + xl)):
        fill(ref, 0, 0)
        fill(ref, 1, block)
        ref[2 * half :] = vals


def select_x(owners, own, got, sent):
    nz, _, slab = sent.shape
    half = (own.shape[0] - VALS) // 2
    per = half // nz
    xl = lax.axis_index("xl")
    here = [(owners[i] // 2) % 2 == xl for i in range(3)]
    flags = (here[0], (owners[1 + xl] // 2) % 2 == xl)
    for i, flag in enumerate(flags):
        rows = slice(i * half, (i + 1) * half)
        choose(
            flag,
            sent,
            (slice(None), slice(i * per, (i + 1) * per)),
            lambda: own[rows].reshape(nz, per, slab),
            lambda: got[rows].reshape(nz, per, slab),
        )
    vals = value_rows(here, own[2 * half :], got[2 * half :])
    for k in range(nz):
        sent[k, 2 * per :] = vals


def terms(cot, act, whole, sent, keep, packed, flat, cov):
    _, _, nz, height, slab = packed.shape
    tok, blocks, full = cot.shape
    nt = full // slab
    per = full // 2 // nz
    group = (height - per) // 3
    scale = 1.0 / (tok * nz * 4)
    flat[...] = cot[...].reshape(tok, blocks * full)
    t = lax.axis_index("t")
    for k in range(nt):
        cov[k * slab : (k + 1) * slab] = dot(whole[k], act[...], ((0,), (0,))) * scale
    place = slice(per + 2 * group, height)
    for c in range(2):
        for xl in range(2):
            packed[c, xl, :, place] = cov[...].reshape(nz, 2, 2, group, slab)[:, xl, c]
    for j in range(2):
        own = flat[:, pl.ds(pl.multiple_of(j * full + t * slab, slab), slab)]
        right = jnp.concatenate([act[...], own], 1)
        both = dot(flat[:, j * full : (j + 1) * full], right, ((0,), (0,))) * scale
        grad = both[:, :slab].reshape(nt, 2, slab // 2, slab)
        out_cov = both[:, slab:].reshape(nz, 2, 2, group, slab)
        for c in range(2):
            packed[c, j, :, 0:per] = grad[:, c].reshape(nz, per, slab)
            for xl in range(2):
                packed[c, xl, :, per + j * group : per + (j + 1) * group] = out_cov[:, xl, c]
    core = lax.axis_index("c")
    sent[...] = packed[1 - core].astype(bf16)
    keep[...] = packed[core]


def add_core(keep, got, sent, rest):
    xl = lax.axis_index("xl")
    sent[...] = (keep[1 - xl] + got[1 - xl].astype(f32)).astype(bf16)
    rest[...] = keep[xl] + got[xl].astype(f32)


def pack_z(owners, keep, got, bases, sent, part, vals):
    per = (bases.shape[1] - VALS) // 2
    xl = lax.axis_index("xl")
    source = [owners[i] // 4 for i in range(3)]
    sent[...] = (keep[...] + got[...].astype(f32)).astype(bf16)
    for i, src in enumerate((source[0], owners[1 + xl] // 4)):
        part[i * per : (i + 1) * per] = bases[src, i * per : (i + 1) * per]
    chosen = bases[source[0], 2 * per :].astype(f32)
    place = lax.broadcasted_iota(jnp.int32, chosen.shape, 0)
    for i in (1, 2):
        chosen = jnp.where(place == i, bases[source[i], 2 * per :].astype(f32), chosen)
    vals[...] = chosen.astype(bf16)


def reduce_z(got, bases, vals, grad, factor_a, factor_g, sent):
    nz, height, slab = got.shape
    group = factor_a.shape[0]
    per = grad.shape[0]
    half = nz * per
    total = got[0].astype(f32)
    for k in range(1, nz):
        total = total + got[k].astype(f32)
    grad[...] = total[0:per].astype(bf16)
    for j in range(2):
        factor_g[j] = total[per + j * group : per + (j + 1) * group]
    factor_a[...] = total[per + 2 * group :]
    for k in range(sent.shape[0]):
        sent[k, 0:half] = bases[:, 0:per].reshape(half, slab)
        sent[k, half : 2 * half] = bases[:, per:].reshape(half, slab)
        sent[k, 2 * half :] = vals[...]


def pack_t(grad, own, sent, qa, qg, vals):
    nt, piece, slab = sent.shape[1:]
    half = qa.shape[1]
    for c in range(2):
        sent[c] = grad[...].reshape(nt, piece, slab)
    qa[...] = own[:, 0:half]
    qg[...] = own[:, half : 2 * half]
    vals[...] = own[:, 2 * half :]


def rotate(got, own, other, sent, grad):
    nt, half, slab = own.shape
    piece = half // nt
    core = lax.axis_index("c")
    for c in range(2):
        for k in range(nt):
            grad[c * piece : (c + 1) * piece, k * slab : (k + 1) * slab] = got[c, k, 0:piece]
    near = grad[:, pl.ds(pl.multiple_of(core * half, half), half)]
    far = grad[:, pl.ds(pl.multiple_of((1 - core) * half, half), half)]
    for i in range(nt // 2):
        k = core * (nt // 2) + i
        turned = dot(near, own[k]) + dot(far, other[k])
        turned = turned.T.astype(bf16)
        sent[2 * i] = turned[0:piece]
        sent[2 * i + 1] = turned[piece:]


def scale_rows(rows, own, other, vals, sent, rot, scaled, column):
    nt, piece, slab = rows.shape
    half = own.shape[1]
    core, xl, t = lax.axis_index("c"), lax.axis_index("xl"), lax.axis_index("t")
    row = vals[core * (nt // 2) + t // 2].astype(f32)[0:1]
    column[...] = jnp.broadcast_to(row, (slab, slab)).T
    la = column[pl.ds(pl.multiple_of((t % 2) * piece, piece), piece)]
    for k in range(nt):
        rot[:, k * slab : (k + 1) * slab] = rows[k]
    near = rot[:, pl.ds(pl.multiple_of(core * half, half), half)]
    far = rot[:, pl.ds(pl.multiple_of((1 - core) * half, half), half)]
    for k in range(nt):
        spectral = dot(near, own[k]) + dot(far, other[k])
        values = vals[k].astype(f32)
        lg = jnp.where(xl == 0, values[1:2], values[2:3])
        scaled[k] = (spectral / (la * lg + damping)).astype(bf16)
    for side, ref in ((core, own), (1 - core, other)):
        mixed = dot(scaled[0], ref[0], ((1,), (1,)))
        for k in range(1, nt):
            mixed = mixed + dot(scaled[k], ref[k], ((1,), (1,)))
        mixed = mixed.astype(bf16)
        for i in range(nt // 2):
            for copy in range(2):
                sent[copy, side * (nt // 2) + i] = mixed[:, i * slab : (i + 1) * slab]


def finish(groups, own, other, own_mixed, other_mixed, pre, worker):
    blocks, nt, piece, slab = own_mixed.shape
    half = own.shape[1]
    core = lax.axis_index("c")
    replica = (lax.axis_index("z") * 2 + lax.axis_index("xl")) * 2 + core
    group = groups[replica]
    for side, ref in ((core, own), (1 - core, other)):
        total = jnp.zeros((half, blocks * slab), f32)
        for part, mixed in ((core, own_mixed), (1 - core, other_mixed)):
            for i in range(nt // 2):
                right = jnp.concatenate(
                    [mixed[j, 2 * i : 2 * i + 2].reshape(2 * piece, slab) for j in range(blocks)], 1
                )
                total = total + dot(ref[part * (nt // 2) + i], right)
        total = total.astype(bf16)
        place = pl.ds(pl.multiple_of(side * half, half), half)
        pre[place] = total.reshape(half, blocks, slab)
        choose(
            group == 0,
            worker,
            (0, place),
            lambda: total[:, :slab],
            lambda: total[:, slab:],
        )


def input_grad(cot, weight, grad):
    tok, blocks, full = cot.shape
    left = cot[...].reshape(tok, blocks * full)
    right = weight[...].reshape(weight.shape[0], blocks * full)
    grad[...] = dot(left, right, ((1,), (1,))).astype(bf16)


def local(act, cot, weight, owners, worker_group, basis_a, values_a, basis_g, values_g):
    tok, slab = act.shape
    blocks, full = cot.shape[1:]
    nz, nt = lax.axis_size("z"), lax.axis_size("t")
    group = full // (nz * 4)
    half, piece = full // 2, slab // 2
    per = half // nz
    height = per + (blocks + 1) * group

    whole_act = exchange(jnp.broadcast_to(act[None], (nt, tok, slab)), "t")

    shape = (3 * half + VALS, slab)
    sent, keep = call(
        pack_bases,
        [out(shape), out(shape)],
        [],
        [basis_a, basis_g, values_a, values_g],
        [pl.ANY, pl.ANY, pltpu.VMEM, pltpu.VMEM],
        scratch=[pltpu.SemaphoreType.DMA((2, 3))],
        limit=56,
    )
    got = swap(sent, "c")
    shape = (2 * half + VALS, slab)
    sent, keep = call(select_core, [out(shape), out(shape)], [owners], [keep, got])
    got = swap(sent, "xl")
    (sent,) = call(select_x, [out((nz, 2 * per + VALS, slab))], [owners], [keep, got])
    got_bases = exchange(sent, "z")

    block = (2, nz, height, slab)
    sent, keep = call(
        terms,
        [out(block), out(block, f32)],
        [],
        [cot, act, whole_act],
        scratch=[
            pltpu.VMEM((2,) + block, f32),
            pltpu.VMEM((tok, blocks * full), bf16),
            pltpu.VMEM((full, slab), f32),
        ],
        flops=10 * tok * full * slab,
    )
    got = swap(sent, "c")
    sent, keep = call(add_core, [out(block[1:]), out(block[1:], f32)], [], [keep, got])
    got = swap(sent, "xl")

    sent, part, vals = call(
        pack_z,
        [out((nz, height, slab)), out((2 * per, slab)), out((VALS, slab))],
        [owners],
        [keep, got, got_bases],
    )
    got = exchange(sent, "z")
    bases = lax.all_gather(part, "z", axis=0)

    width = 2 * half + VALS
    grad, factor_a, factor_g, sent = call(
        reduce_z,
        [
            out((per, slab)),
            out((group, slab), f32),
            out((blocks, group, slab), f32),
            out((nt, width, slab)),
        ],
        [],
        [got, bases, vals],
    )
    own = exchange(sent, "t")
    grad = lax.all_gather(grad, "z", axis=0, tiled=True)
    sent, qa, qg, vals = call(
        pack_t,
        [
            out((2, nt, piece, slab)),
            out((nt, half, slab)),
            out((nt, half, slab)),
            out((nt, VALS, slab)),
        ],
        [],
        [grad, own],
    )
    qa_other, qg_other = swap(qa, "c"), swap(qg, "c")
    columns = exchange(sent.reshape(2 * nt, piece, slab), ("c", "t"))
    columns = columns.reshape(2, nt, piece, slab)
    (sent,) = call(
        rotate,
        [out((nt, piece, slab))],
        [],
        [columns, qa, qa_other],
        scratch=[pltpu.VMEM((slab, full), bf16)],
        flops=2 * slab * full * half,
    )
    rows = exchange(sent, "t")
    (sent,) = call(
        scale_rows,
        [out((blocks, nt, piece, slab))],
        [],
        [rows, qg, qg_other, vals],
        scratch=[
            pltpu.VMEM((piece, full), bf16),
            pltpu.VMEM((nt, piece, slab), bf16),
            pltpu.VMEM((slab, slab), f32),
        ],
        flops=4 * piece * full * full,
    )
    own_mixed = exchange(sent.reshape(blocks * nt, piece, slab), ("xl", "t"))
    own_mixed = own_mixed.reshape(blocks, nt, piece, slab)
    other_mixed = swap(own_mixed, "c")
    pre, worker = call(
        finish,
        [out((full, blocks, slab)), out((1, full, slab))],
        [worker_group],
        [qa, qa_other, own_mixed, other_mixed],
        flops=4 * full * full * slab,
    )

    (grad_input,) = call(
        input_grad, [out((tok, slab))], [], [cot, weight], flops=4 * tok * full * slab
    )
    return grad_input, factor_a, factor_g.transpose(1, 0, 2), pre, worker


def solution(mesh):
    dp, tensor = mesh.devices.shape
    fine = Mesh(mesh.devices.reshape(dp // 4, 2, 2, tensor), ("z", "xl", "c", "t"))
    dp = ("z", "xl", "c")
    return jax.shard_map(
        local,
        mesh=fine,
        in_specs=(
            P(dp, "t"),
            P(dp, None, None),
            P("t", None, None),
            P(),
            P(),
            P(dp, None, "t"),
            P(dp, "t"),
            P(dp, None, None, "t"),
            P(dp, None, "t"),
        ),
        out_specs=(
            P(dp, "t"),
            P(dp, "t"),
            P(dp, None, "t"),
            P(None, None, "t"),
            P(dp, None, "t"),
        ),
        check_vma=False,
    )
```

```python
import functools

import jax
import jax.numpy as jnp
from jax import lax
from jax.experimental import pallas as pl
from jax.experimental.pallas import tpu as pltpu
from jax.sharding import Mesh, PartitionSpec as P

damping = 0.001
f32 = jnp.float32
bf16 = jnp.bfloat16
VALS = 16


def exchange(array, axis):
    return lax.all_to_all(array, axis, 0, 0, tiled=True)


def swap(array, axis):
    return lax.ppermute(array, axis, [(0, 1), (1, 0)])


def across(array, axis, step):
    pairs = [(i, i ^ step) for i in range(lax.axis_size(axis))]
    return lax.ppermute(array, axis, pairs)


def call(body, outs, scalars, args, places=None, scratch=(), flops=0, limit=40):
    places = places or [pltpu.VMEM] * len(args)
    specs, arrays = [], []
    for arg, place in zip(args, places):
        if isinstance(arg, tuple):
            array, rows, block = arg
            shape = (array.shape[0], rows, array.shape[2])
            specs.append(pl.BlockSpec(shape, functools.partial(lambda k, i: (0, k, 0), block)))
        else:
            array = arg
            specs.append(pl.BlockSpec(memory_space=place))
        arrays.append(array)
    bytes_all = sum(a.size * a.dtype.itemsize for a in arrays + list(outs))
    return pl.pallas_call(
        body,
        grid=(1,),
        out_shape=outs,
        in_specs=[pl.BlockSpec(memory_space=pltpu.SMEM)] * len(scalars) + specs,
        out_specs=[pl.BlockSpec(memory_space=pltpu.VMEM)] * len(outs),
        scratch_shapes=list(scratch),
        compiler_params=pltpu.CompilerParams(vmem_limit_bytes=limit * 1024 * 1024),
        cost_estimate=pl.CostEstimate(flops=flops, bytes_accessed=bytes_all, transcendentals=0),
    )(*scalars, *arrays)


def out(shape, dtype=bf16):
    return jax.ShapeDtypeStruct(shape, dtype)


def dot(left, right, dims=((1,), (0,))):
    return lax.dot_general(left, right, (dims, ((), ())), preferred_element_type=f32)


def value_rows(flags, own, other):
    place = lax.broadcasted_iota(jnp.int32, own.shape, 0)
    take = jnp.zeros(own.shape, jnp.int32)
    for row, flag in enumerate(flags):
        take = jnp.where(place == row, flag.astype(jnp.int32), take)
    return jnp.where(take > 0, own.astype(f32), other.astype(f32)).astype(bf16)


def choose(flag, ref, place, own, other):
    @pl.when(flag)
    def _():
        ref[place] = own()

    @pl.when(jnp.logical_not(flag))
    def _():
        ref[place] = other()


def pack_bases(ba, bg, va, vg, act, sent, keep, every, sem):
    half = ba.shape[1] // 2
    core = lax.axis_index("c")
    place = lax.broadcasted_iota(jnp.int32, (VALS, ba.shape[2]), 0)
    vals = jnp.where(place == 0, va[...].astype(f32), 0.0)
    for j in range(2):
        row = vg[0].astype(f32)[j : j + 1]
        vals = jnp.where(place == 1 + j, row, vals)
    copies = []
    for side, (ref, who) in enumerate(((sent, 1 - core), (keep, core))):
        rows = pl.ds(pl.multiple_of(who * half, half), half)
        for i in range(3):
            source = ba.at[0, rows] if i == 0 else bg.at[0, i - 1, rows]
            copies.append(
                pltpu.make_async_copy(source, ref.at[i * half : (i + 1) * half], sem.at[side, i])
            )
            copies[-1].start()
    sent[3 * half :] = vals.astype(bf16)
    keep[3 * half :] = vals.astype(bf16)
    for k in range(every.shape[0]):
        every[k] = act[...]
    for copy in copies:
        copy.wait()


def select_core(owners, own, got, sent, keep):
    half = (own.shape[0] - VALS) // 3
    core, xl = lax.axis_index("c"), lax.axis_index("xl")
    flags = [owners[i] % 2 == core for i in range(3)]

    def fill(ref, slot, i):
        start = pl.multiple_of(i * half, half)
        choose(
            owners[i] % 2 == core,
            ref,
            slice(slot * half, (slot + 1) * half),
            lambda: own[pl.ds(start, half)],
            lambda: got[pl.ds(start, half)],
        )

    vals = value_rows(flags, own[3 * half :], got[3 * half :])
    for ref, block in ((sent, 2 - xl), (keep, 1 + xl)):
        fill(ref, 0, 0)
        fill(ref, 1, block)
        ref[2 * half :] = vals


def grad_terms(cot, act, sent, keep, flat):
    blocks, half, slab = keep.shape
    tok, _, full = cot.shape
    nt = full // slab
    scale = 1.0 / (tok * lax.axis_size("z") * 4)
    core = lax.axis_index("c")
    flat[...] = cot[...].reshape(tok, blocks * full)
    for j in range(blocks):
        term = dot(flat[:, j * full : (j + 1) * full], act[...], ((0,), (0,))) * scale
        term = term.reshape(nt, 2, slab // 2, slab)
        for c in range(2):
            part = term[:, c].reshape(half, slab)

            @pl.when(core == c)
            def _():
                keep[j] = part

            @pl.when(core != c)
            def _():
                sent[j] = part.astype(bf16)


def add_core(keep, got, sent, rest):
    xl = lax.axis_index("xl")
    sent[...] = (keep[1 - xl] + got[1 - xl].astype(f32)).astype(bf16)
    rest[...] = keep[xl] + got[xl].astype(f32)


def pack_z(owners, keep, got, own, other, after, sent):
    nz, _, slab = sent.shape
    half = (own.shape[0] - VALS) // 2
    per = half // nz
    xl = lax.axis_index("xl")
    total = (keep[...] + got[...].astype(f32)).astype(bf16)
    sent[:, 0:per] = total.reshape(nz, per, slab)
    here = [(owners[i] // 2) % 2 == xl for i in range(3)]
    flags = (here[0], (owners[1 + xl] // 2) % 2 == xl)
    for i, flag in enumerate(flags):
        rows = slice(i * half, (i + 1) * half)
        choose(
            flag,
            sent,
            (slice(None), slice((1 + i) * per, (2 + i) * per)),
            lambda: own[rows].reshape(nz, per, slab),
            lambda: other[rows].reshape(nz, per, slab),
        )
    vals = value_rows(here, own[2 * half :], other[2 * half :])
    for k in range(nz):
        sent[k, 3 * per :] = vals


def reduce_z(owners, got, sent, vals):
    nz, height, _ = sent.shape
    per = height // 3
    xl = lax.axis_index("xl")
    source = [owners[i] // 4 for i in range(3)]
    total = got[0, 0:per].astype(f32)
    for k in range(1, nz):
        total = total + got[k, 0:per].astype(f32)
    parts = [total.astype(bf16)]
    for i, src in enumerate((source[0], owners[1 + xl] // 4)):
        parts.append(got[src, (1 + i) * per : (2 + i) * per])
    for i, part in enumerate(parts):
        for k in range(nz):
            sent[k, i * per : (i + 1) * per] = part
    chosen = got[source[0], 3 * per :].astype(f32)
    place = lax.broadcasted_iota(jnp.int32, chosen.shape, 0)
    for i in (1, 2):
        chosen = jnp.where(place == i, got[source[i], 3 * per :].astype(f32), chosen)
    vals[...] = chosen.astype(bf16)


def factor_terms(cot, act, whole, sent, keep, flat, both):
    nz, _, height, slab = keep.shape
    group = height // 3
    tok, blocks, full = cot.shape
    nt = full // slab
    scale = 1.0 / (tok * nz * 4)
    core, t = lax.axis_index("c"), lax.axis_index("t")
    flat[...] = cot[...].reshape(tok, blocks * full)
    for j in range(blocks):
        own = flat[:, pl.ds(pl.multiple_of(j * full + t * slab, slab), slab)]
        both[j] = dot(flat[:, j * full : (j + 1) * full], own, ((0,), (0,))) * scale
    for k in range(nt):
        both[blocks, k * slab : (k + 1) * slab] = dot(whole[k], act[...], ((0,), (0,))) * scale
    for i in range(blocks + 1):
        term = both[i].reshape(nz, 2, 2, group, slab)
        rows = slice(i * group, (i + 1) * group)
        for c in range(2):

            @pl.when(core == c)
            def _():
                keep[:, :, rows] = term[:, :, c]

            @pl.when(core != c)
            def _():
                sent[:, :, rows] = term[:, :, c].astype(bf16)


def factor_core(keep, got, sent, rest):
    xl = lax.axis_index("xl")
    sent[...] = (keep[:, 1 - xl] + got[:, 1 - xl].astype(f32)).astype(bf16)
    rest[...] = keep[:, xl] + got[:, xl].astype(f32)


def factor_z(bit, keep, got, sent, rest):
    count, height, slab = keep.shape
    total = keep[...] + got[...].astype(f32)
    if count == 1:
        rest[...] = total
    else:
        mine = (lax.axis_index("z") // bit) % 2
        total = total.reshape(count // 2, 2, height, slab)
        for side in range(2):

            @pl.when(mine == side)
            def _():
                rest[...] = total[:, side]
                sent[...] = total[:, 1 - side].astype(bf16)


def pack_t(got, vals, keep, f_got, sent, f_sent, f_rest):
    nz, height, slab = got.shape
    nt = sent.shape[0]
    per = height // 3
    half = nz * per
    piece = half // nt
    sent[:, 0:piece] = got[:, 0:per].reshape(nt, piece, slab)
    for k in range(nt):
        for i in range(2):
            rows = got[:, (1 + i) * per : (2 + i) * per].reshape(half, slab)
            sent[k, piece + i * half : piece + (i + 1) * half] = rows
        sent[k, piece + 2 * half :] = vals[...]
    factor_z(1, keep, f_got, f_sent, f_rest)


def split(own, keep, f_got, near, qg, vals, factor_a, factor_g):
    nt, height, slab = near.shape
    half = qg.shape[1]
    near[...] = own[:, 0:height]
    qg[...] = own[:, height : height + half]
    vals[...] = own[:, height + half :]
    group = factor_a.shape[0]
    total = keep[0] + f_got[0].astype(f32)
    for j in range(2):
        factor_g[j] = total[j * group : (j + 1) * group]
    factor_a[...] = total[2 * group :]


def rotate(own, other, sent, grad):
    nt, height, slab = own.shape
    piece = slab // 2
    half = height - piece
    core = lax.axis_index("c")
    mine = pl.multiple_of(core * piece, piece)
    theirs = pl.multiple_of((1 - core) * piece, piece)
    for k in range(nt):
        grad[pl.ds(mine, piece), k * slab : (k + 1) * slab] = own[k, 0:piece]
        grad[pl.ds(theirs, piece), k * slab : (k + 1) * slab] = other[k, 0:piece]
    near = grad[:, pl.ds(pl.multiple_of(core * half, half), half)]
    far = grad[:, pl.ds(pl.multiple_of((1 - core) * half, half), half)]
    for i in range(nt // 2):
        k = core * (nt // 2) + i
        turned = dot(near, own[k, piece:]) + dot(far, other[k, piece:])
        turned = turned.T.astype(bf16)
        sent[2 * i] = turned[0:piece]
        sent[2 * i + 1] = turned[piece:]


def scale_rows(rows, own, other, vals, sent, rot, scaled, column):
    nt, piece, slab = rows.shape
    half = own.shape[1]
    core, xl, t = lax.axis_index("c"), lax.axis_index("xl"), lax.axis_index("t")
    row = vals[core * (nt // 2) + t // 2].astype(f32)[0:1]
    column[...] = jnp.broadcast_to(row, (slab, slab)).T
    la = column[pl.ds(pl.multiple_of((t % 2) * piece, piece), piece)]
    for k in range(nt):
        rot[:, k * slab : (k + 1) * slab] = rows[k]
    near = rot[:, pl.ds(pl.multiple_of(core * half, half), half)]
    far = rot[:, pl.ds(pl.multiple_of((1 - core) * half, half), half)]
    for k in range(nt):
        spectral = dot(near, own[k]) + dot(far, other[k])
        values = vals[k].astype(f32)
        lg = jnp.where(xl == 0, values[1:2], values[2:3])
        scaled[k] = (spectral / (la * lg + damping)).astype(bf16)
    for side, ref in ((core, own), (1 - core, other)):
        mixed = dot(scaled[0], ref[0], ((1,), (1,)))
        for k in range(1, nt):
            mixed = mixed + dot(scaled[k], ref[k], ((1,), (1,)))
        mixed = mixed.astype(bf16)
        for i in range(nt // 2):
            for copy in range(2):
                sent[copy, side * (nt // 2) + i] = mixed[:, i * slab : (i + 1) * slab]


def finish(groups, own, other, own_mixed, other_mixed, pre, worker):
    blocks, nt, piece, slab = own_mixed.shape
    half = own.shape[1] - piece
    core = lax.axis_index("c")
    replica = (lax.axis_index("z") * 2 + lax.axis_index("xl")) * 2 + core
    group = groups[replica]
    for side, ref in ((core, own), (1 - core, other)):
        total = jnp.zeros((half, blocks * slab), f32)
        for part, mixed in ((core, own_mixed), (1 - core, other_mixed)):
            for i in range(nt // 2):
                right = jnp.concatenate(
                    [mixed[j, 2 * i : 2 * i + 2].reshape(2 * piece, slab) for j in range(blocks)], 1
                )
                total = total + dot(ref[part * (nt // 2) + i, piece:], right)
        total = total.astype(bf16)
        place = pl.ds(pl.multiple_of(side * half, half), half)
        pre[place] = total.reshape(half, blocks, slab)
        choose(
            group == 0,
            worker,
            (0, place),
            lambda: total[:, :slab],
            lambda: total[:, slab:],
        )


def input_grad(cot, weight, grad):
    tok, blocks, full = cot.shape
    left = cot[...].reshape(tok, blocks * full)
    right = weight[...].reshape(weight.shape[0], blocks * full)
    grad[...] = dot(left, right, ((1,), (1,))).astype(bf16)


def local(act, cot, weight, owners, worker_group, basis_a, values_a, basis_g, values_g):
    tok, slab = act.shape
    blocks, full = cot.shape[1:]
    nz, nt = lax.axis_size("z"), lax.axis_size("t")
    group = full // (nz * 4)
    half, piece = full // 2, slab // 2
    per = half // nz

    shape = (3 * half + VALS, slab)
    sent, keep, every = call(
        pack_bases,
        [out(shape), out(shape), out((nt, tok, slab))],
        [],
        [basis_a, basis_g, values_a, values_g, act],
        [pl.ANY, pl.ANY, pltpu.VMEM, pltpu.VMEM, pltpu.VMEM],
        scratch=[pltpu.SemaphoreType.DMA((2, 3))],
        limit=56,
    )
    got = swap(sent, "c")
    whole_act = exchange(every, "t")
    shape = (2 * half + VALS, slab)
    sent, base = call(select_core, [out(shape), out(shape)], [owners], [keep, got])
    base_got = swap(sent, "xl")

    flat = pltpu.VMEM((tok, blocks * full), bf16)
    shape = (blocks, half, slab)
    sent, keep = call(
        grad_terms,
        [out(shape), out(shape, f32)],
        [],
        [cot, act],
        scratch=[flat],
        flops=4 * tok * full * slab,
    )
    got = swap(sent, "c")
    sent, keep = call(add_core, [out(shape[1:]), out(shape[1:], f32)], [], [keep, got])
    got = swap(sent, "xl")

    (sent,) = call(
        pack_z,
        [out((nz, 3 * per + VALS, slab))],
        [owners],
        [keep, got, base, base_got, whole_act],
        [pltpu.VMEM] * 4 + [pl.ANY],
    )
    got = exchange(sent, "z")
    sent, vals = call(
        reduce_z, [out((nz, 3 * per, slab)), out((VALS, slab))], [owners], [got]
    )
    got = exchange(sent, "z")

    height = (blocks + 1) * group
    shape = (nz, 2, height, slab)
    sent, keep = call(
        factor_terms,
        [out(shape), out(shape, f32)],
        [],
        [cot, act, whole_act],
        scratch=[flat, pltpu.VMEM((blocks + 1, full, slab), f32)],
        flops=6 * tok * full * slab,
    )
    f_got = swap(sent, "c")
    shape = (nz, height, slab)
    sent, keep = call(factor_core, [out(shape), out(shape, f32)], [], [keep, f_got])
    f_got = swap(sent, "xl")

    width = piece + 2 * half + VALS
    shape = (nz // 2, height, slab)
    sent, f_sent, f_keep = call(
        pack_t,
        [out((nt, width, slab)), out(shape), out(shape, f32)],
        [],
        [got, vals, keep, f_got],
    )
    own = exchange(sent, "t")
    f_got = across(f_sent, "z", 1)
    bit = 2
    while bit < nz:
        shape = (nz // 2 // bit, height, slab)
        f_sent, f_keep = call(
            functools.partial(factor_z, bit), [out(shape), out(shape, f32)], [], [f_keep, f_got]
        )
        f_got = across(f_sent, "z", bit)
        bit *= 2
    near, qg, vals, factor_a, factor_g = call(
        split,
        [
            out((nt, piece + half, slab)),
            out((nt, half, slab)),
            out((nt, VALS, slab)),
            out((group, slab), f32),
            out((blocks, group, slab), f32),
        ],
        [],
        [own, f_keep, f_got],
    )
    near_other, qg_other = swap(near, "c"), swap(qg, "c")
    (sent,) = call(
        rotate,
        [out((nt, piece, slab))],
        [],
        [near, near_other],
        scratch=[pltpu.VMEM((slab, full), bf16)],
        flops=2 * slab * full * half,
    )
    rows = exchange(sent, "t")
    (sent,) = call(
        scale_rows,
        [out((blocks, nt, piece, slab))],
        [],
        [rows, qg, qg_other, vals],
        scratch=[
            pltpu.VMEM((piece, full), bf16),
            pltpu.VMEM((nt, piece, slab), bf16),
            pltpu.VMEM((slab, slab), f32),
        ],
        flops=4 * piece * full * full,
    )
    own_mixed = exchange(sent.reshape(blocks * nt, piece, slab), ("xl", "t"))
    own_mixed = own_mixed.reshape(blocks, nt, piece, slab)
    other_mixed = swap(own_mixed, "c")
    pre, worker = call(
        finish,
        [out((full, blocks, slab)), out((1, full, slab))],
        [worker_group],
        [near, near_other, own_mixed, other_mixed],
        flops=4 * full * full * slab,
    )

    (grad_input,) = call(
        input_grad, [out((tok, slab))], [], [cot, weight], flops=4 * tok * full * slab
    )
    return grad_input, factor_a, factor_g.transpose(1, 0, 2), pre, worker


def solution(mesh):
    dp, tensor = mesh.devices.shape
    fine = Mesh(mesh.devices.reshape(dp // 4, 2, 2, tensor), ("z", "xl", "c", "t"))
    dp = ("z", "xl", "c")
    return jax.shard_map(
        local,
        mesh=fine,
        in_specs=(
            P(dp, "t"),
            P(dp, None, None),
            P("t", None, None),
            P(),
            P(),
            P(dp, None, "t"),
            P(dp, "t"),
            P(dp, None, None, "t"),
            P(dp, None, "t"),
        ),
        out_specs=(
            P(dp, "t"),
            P(dp, "t"),
            P(dp, None, "t"),
            P(None, None, "t"),
            P(dp, None, "t"),
        ),
        check_vma=False,
    )
```

```python
import functools

import jax
import jax.numpy as jnp
from jax import lax
from jax.experimental import pallas as pl
from jax.experimental.pallas import tpu as pltpu
from jax.sharding import Mesh, PartitionSpec as P

damping = 0.001
f32 = jnp.float32
bf16 = jnp.bfloat16
VALS = 16


def exchange(array, axis):
    return lax.all_to_all(array, axis, 0, 0, tiled=True)


def swap(array, axis):
    return lax.ppermute(array, axis, [(0, 1), (1, 0)])


def across(array, axis, step):
    pairs = [(i, i ^ step) for i in range(lax.axis_size(axis))]
    return lax.ppermute(array, axis, pairs)


def call(body, outs, scalars, args, places=None, scratch=(), flops=0, limit=20):
    places = places or [pltpu.VMEM] * len(args)
    specs, arrays = [], []
    for arg, place in zip(args, places):
        if isinstance(arg, tuple):
            array, rows, block = arg
            shape = (array.shape[0], rows, array.shape[2])
            specs.append(pl.BlockSpec(shape, functools.partial(lambda k, i: (0, k, 0), block)))
        else:
            array = arg
            specs.append(pl.BlockSpec(memory_space=place))
        arrays.append(array)
    bytes_all = sum(a.size * a.dtype.itemsize for a in arrays + list(outs))
    return pl.pallas_call(
        body,
        grid=(1,),
        out_shape=outs,
        in_specs=[pl.BlockSpec(memory_space=pltpu.SMEM)] * len(scalars) + specs,
        out_specs=[pl.BlockSpec(memory_space=pltpu.VMEM)] * len(outs),
        scratch_shapes=list(scratch),
        compiler_params=pltpu.CompilerParams(vmem_limit_bytes=limit * 1024 * 1024),
        cost_estimate=pl.CostEstimate(flops=flops, bytes_accessed=bytes_all, transcendentals=0),
    )(*scalars, *arrays)


def follow(array, after):
    return pl.pallas_call(
        lambda *refs: None,
        out_shape=jax.ShapeDtypeStruct(array.shape, array.dtype),
        in_specs=[pl.BlockSpec(memory_space=pl.ANY)] * 2,
        out_specs=pl.BlockSpec(memory_space=pl.ANY),
        input_output_aliases={0: 0},
    )(array, after)


def out(shape, dtype=bf16):
    return jax.ShapeDtypeStruct(shape, dtype)


def dot(left, right, dims=((1,), (0,))):
    return lax.dot_general(left, right, (dims, ((), ())), preferred_element_type=f32)


def value_rows(flags, own, other):
    place = lax.broadcasted_iota(jnp.int32, own.shape, 0)
    take = jnp.zeros(own.shape, jnp.int32)
    for row, flag in enumerate(flags):
        take = jnp.where(place == row, flag.astype(jnp.int32), take)
    return jnp.where(take > 0, own.astype(f32), other.astype(f32)).astype(bf16)


def choose(flag, ref, place, own, other):
    @pl.when(flag)
    def _():
        ref[place] = own()

    @pl.when(jnp.logical_not(flag))
    def _():
        ref[place] = other()


def pack_bases(ba, bg, va, vg, act, sent, keep, every, sem):
    half = ba.shape[1] // 2
    core = lax.axis_index("c")
    place = lax.broadcasted_iota(jnp.int32, (VALS, ba.shape[2]), 0)
    vals = jnp.where(place == 0, va[...].astype(f32), 0.0)
    for j in range(2):
        row = vg[0].astype(f32)[j : j + 1]
        vals = jnp.where(place == 1 + j, row, vals)
    copies = []
    for side, (ref, who) in enumerate(((sent, 1 - core), (keep, core))):
        rows = pl.ds(pl.multiple_of(who * half, half), half)
        for i in range(3):
            source = ba.at[0, rows] if i == 0 else bg.at[0, i - 1, rows]
            copies.append(
                pltpu.make_async_copy(source, ref.at[i * half : (i + 1) * half], sem.at[side, i])
            )
            copies[-1].start()
    sent[3 * half :] = vals.astype(bf16)
    keep[3 * half :] = vals.astype(bf16)
    for k in range(every.shape[0]):
        every[k] = act[...]
    for copy in copies:
        copy.wait()


def select_core(owners, own, got, sent, keep):
    half = (own.shape[0] - VALS) // 3
    core, xl = lax.axis_index("c"), lax.axis_index("xl")
    flags = [owners[i] % 2 == core for i in range(3)]

    def fill(ref, slot, i):
        start = pl.multiple_of(i * half, half)
        choose(
            owners[i] % 2 == core,
            ref,
            slice(slot * half, (slot + 1) * half),
            lambda: own[pl.ds(start, half)],
            lambda: got[pl.ds(start, half)],
        )

    vals = value_rows(flags, own[3 * half :], got[3 * half :])
    for ref, block in ((sent, 2 - xl), (keep, 1 + xl)):
        fill(ref, 0, 0)
        fill(ref, 1, block)
        ref[2 * half :] = vals


def grad_terms(cot, act, sent, keep, flat):
    blocks, half, slab = keep.shape
    tok, _, full = cot.shape
    nt = full // slab
    scale = 1.0 / (tok * lax.axis_size("z") * 4)
    core = lax.axis_index("c")
    flat[...] = cot[...].reshape(tok, blocks * full)
    for j in range(blocks):
        term = dot(flat[:, j * full : (j + 1) * full], act[...], ((0,), (0,))) * scale
        term = term.reshape(nt, 2, slab // 2, slab)
        for c in range(2):
            part = term[:, c].reshape(half, slab)

            @pl.when(core == c)
            def _():
                keep[j] = part

            @pl.when(core != c)
            def _():
                sent[j] = part.astype(bf16)


def add_core(keep, got, sent, rest):
    xl = lax.axis_index("xl")
    sent[...] = (keep[1 - xl] + got[1 - xl].astype(f32)).astype(bf16)
    rest[...] = keep[xl] + got[xl].astype(f32)


def pack_z(owners, keep, got, own, other, after, sent):
    nz, _, slab = sent.shape
    half = (own.shape[0] - VALS) // 2
    per = half // nz
    xl = lax.axis_index("xl")
    total = (keep[...] + got[...].astype(f32)).astype(bf16)
    sent[:, 0:per] = total.reshape(nz, per, slab)
    here = [(owners[i] // 2) % 2 == xl for i in range(3)]
    flags = (here[0], (owners[1 + xl] // 2) % 2 == xl)
    for i, flag in enumerate(flags):
        rows = slice(i * half, (i + 1) * half)
        choose(
            flag,
            sent,
            (slice(None), slice((1 + i) * per, (2 + i) * per)),
            lambda: own[rows].reshape(nz, per, slab),
            lambda: other[rows].reshape(nz, per, slab),
        )
    vals = value_rows(here, own[2 * half :], other[2 * half :])
    for k in range(nz):
        sent[k, 3 * per :] = vals


def reduce_z(owners, got, sent, vals):
    nz, height, _ = sent.shape
    per = height // 3
    xl = lax.axis_index("xl")
    source = [owners[i] // 4 for i in range(3)]
    total = got[0, 0:per].astype(f32)
    for k in range(1, nz):
        total = total + got[k, 0:per].astype(f32)
    parts = [total.astype(bf16)]
    for i, src in enumerate((source[0], owners[1 + xl] // 4)):
        parts.append(got[src, (1 + i) * per : (2 + i) * per])
    for i, part in enumerate(parts):
        for k in range(nz):
            sent[k, i * per : (i + 1) * per] = part
    chosen = got[source[0], 3 * per :].astype(f32)
    place = lax.broadcasted_iota(jnp.int32, chosen.shape, 0)
    for i in (1, 2):
        chosen = jnp.where(place == i, got[source[i], 3 * per :].astype(f32), chosen)
    vals[...] = chosen.astype(bf16)


def factor_terms(cot, act, whole, sent, keep, flat, both):
    nz, _, height, slab = keep.shape
    group = height // 3
    tok, blocks, full = cot.shape
    nt = full // slab
    scale = 1.0 / (tok * nz * 4)
    core, t = lax.axis_index("c"), lax.axis_index("t")
    flat[...] = cot[...].reshape(tok, blocks * full)
    for j in range(blocks):
        own = flat[:, pl.ds(pl.multiple_of(j * full + t * slab, slab), slab)]
        both[j] = dot(flat[:, j * full : (j + 1) * full], own, ((0,), (0,))) * scale
    for k in range(nt):
        both[blocks, k * slab : (k + 1) * slab] = dot(whole[k], act[...], ((0,), (0,))) * scale
    for i in range(blocks + 1):
        term = both[i].reshape(nz, 2, 2, group, slab)
        rows = slice(i * group, (i + 1) * group)
        for c in range(2):

            @pl.when(core == c)
            def _():
                keep[:, :, rows] = term[:, :, c]

            @pl.when(core != c)
            def _():
                sent[:, :, rows] = term[:, :, c].astype(bf16)


def factor_core(keep, got, sent, rest):
    xl = lax.axis_index("xl")
    sent[...] = (keep[:, 1 - xl] + got[:, 1 - xl].astype(f32)).astype(bf16)
    rest[...] = keep[:, xl] + got[:, xl].astype(f32)


def factor_z(bit, keep, got, sent, rest):
    count, height, slab = keep.shape
    total = keep[...] + got[...].astype(f32)
    if count == 1:
        rest[...] = total
    else:
        mine = (lax.axis_index("z") // bit) % 2
        total = total.reshape(count // 2, 2, height, slab)
        for side in range(2):

            @pl.when(mine == side)
            def _():
                rest[...] = total[:, side]
                sent[...] = total[:, 1 - side].astype(bf16)


def pack_t(got, vals, keep, f_got, sent, f_sent, f_rest):
    nz, height, slab = got.shape
    nt = sent.shape[0]
    per = height // 3
    half = nz * per
    piece = half // nt
    for k in range(nt):
        for i in range(2):
            rows = got[:, (1 + i) * per : (2 + i) * per].reshape(half, slab)
            sent[k, i * half : (i + 1) * half] = rows
        sent[k, 2 * half + piece :] = vals[...]
    sent[:, 2 * half : 2 * half + piece] = got[:, 0:per].reshape(nt, piece, slab)
    factor_z(1, keep, f_got, f_sent, f_rest)


def factor_out(keep, got, factor_a, factor_g):
    group = factor_a.shape[0]
    total = keep[0] + got[0].astype(f32)
    for j in range(2):
        factor_g[j] = total[j * group : (j + 1) * group]
    factor_a[...] = total[2 * group :]


def rotate(own, other, own_grad, other_grad, sent, grad):
    nt, half, slab = own.shape
    piece = slab // 2
    core = lax.axis_index("c")
    mine = pl.multiple_of(core * piece, piece)
    theirs = pl.multiple_of((1 - core) * piece, piece)
    for k in range(nt):
        grad[pl.ds(mine, piece), k * slab : (k + 1) * slab] = own_grad[k]
        grad[pl.ds(theirs, piece), k * slab : (k + 1) * slab] = other_grad[k]
    near = grad[:, pl.ds(pl.multiple_of(core * half, half), half)]
    far = grad[:, pl.ds(pl.multiple_of((1 - core) * half, half), half)]
    for i in range(nt // 2):
        k = core * (nt // 2) + i
        turned = dot(near, own[k]) + dot(far, other[k])
        turned = turned.T.astype(bf16)
        sent[2 * i] = turned[0:piece]
        sent[2 * i + 1] = turned[piece:]


def scale_rows(rows, own, other, vals, after, sent, rot, scaled, column):
    nt, piece, slab = rows.shape
    half = own.shape[1]
    core, xl, t = lax.axis_index("c"), lax.axis_index("xl"), lax.axis_index("t")
    row = vals[core * (nt // 2) + t // 2].astype(f32)[0:1]
    column[...] = jnp.broadcast_to(row, (slab, slab)).T
    la = column[pl.ds(pl.multiple_of((t % 2) * piece, piece), piece)]
    for k in range(nt):
        rot[:, k * slab : (k + 1) * slab] = rows[k]
    near = rot[:, pl.ds(pl.multiple_of(core * half, half), half)]
    far = rot[:, pl.ds(pl.multiple_of((1 - core) * half, half), half)]
    for k in range(nt):
        spectral = dot(near, own[k]) + dot(far, other[k])
        values = vals[k].astype(f32)
        lg = jnp.where(xl == 0, values[1:2], values[2:3])
        scaled[k] = (spectral / (la * lg + damping)).astype(bf16)
    for side, ref in ((core, own), (1 - core, other)):
        mixed = dot(scaled[0], ref[0], ((1,), (1,)))
        for k in range(1, nt):
            mixed = mixed + dot(scaled[k], ref[k], ((1,), (1,)))
        mixed = mixed.astype(bf16)
        for i in range(nt // 2):
            for copy in range(2):
                sent[copy, side * (nt // 2) + i] = mixed[:, i * slab : (i + 1) * slab]


def finish(groups, own, other, own_mixed, other_mixed, pre, worker):
    blocks, nt, piece, slab = own_mixed.shape
    half = own.shape[1]
    core = lax.axis_index("c")
    replica = (lax.axis_index("z") * 2 + lax.axis_index("xl")) * 2 + core
    group = groups[replica]
    for side, ref in ((core, own), (1 - core, other)):
        total = jnp.zeros((half, blocks * slab), f32)
        for part, mixed in ((core, own_mixed), (1 - core, other_mixed)):
            for i in range(nt // 2):
                right = jnp.concatenate(
                    [mixed[j, 2 * i : 2 * i + 2].reshape(2 * piece, slab) for j in range(blocks)], 1
                )
                total = total + dot(ref[part * (nt // 2) + i], right)
        total = total.astype(bf16)
        place = pl.ds(pl.multiple_of(side * half, half), half)
        pre[place] = total.reshape(half, blocks, slab)
        choose(
            group == 0,
            worker,
            (0, place),
            lambda: total[:, :slab],
            lambda: total[:, slab:],
        )


def input_grad(cot, weight, grad):
    tok, blocks, full = cot.shape
    left = cot[...].reshape(tok, blocks * full)
    right = weight[...].reshape(weight.shape[0], blocks * full)
    grad[...] = dot(left, right, ((1,), (1,))).astype(bf16)


def local(act, cot, weight, owners, worker_group, basis_a, values_a, basis_g, values_g):
    tok, slab = act.shape
    blocks, full = cot.shape[1:]
    nz, nt = lax.axis_size("z"), lax.axis_size("t")
    group = full // (nz * 4)
    half, piece = full // 2, slab // 2
    per = half // nz

    shape = (3 * half + VALS, slab)
    sent, keep, every = call(
        pack_bases,
        [out(shape), out(shape), out((nt, tok, slab))],
        [],
        [basis_a, basis_g, values_a, values_g, act],
        [pl.ANY, pl.ANY, pltpu.VMEM, pltpu.VMEM, pltpu.VMEM],
        scratch=[pltpu.SemaphoreType.DMA((2, 3))],
        limit=56,
    )
    got = swap(sent, "c")
    whole_act = exchange(every, "t")
    shape = (2 * half + VALS, slab)
    sent, base = call(select_core, [out(shape), out(shape)], [owners], [keep, got])
    base_got = swap(sent, "xl")

    flat = pltpu.VMEM((tok, blocks * full), bf16)
    shape = (blocks, half, slab)
    sent, keep = call(
        grad_terms,
        [out(shape), out(shape, f32)],
        [],
        [cot, act],
        scratch=[flat],
        flops=4 * tok * full * slab,
    )
    got = swap(sent, "c")
    sent, keep = call(add_core, [out(shape[1:]), out(shape[1:], f32)], [], [keep, got])
    got = swap(sent, "xl")

    (sent,) = call(
        pack_z,
        [out((nz, 3 * per + VALS, slab))],
        [owners],
        [keep, got, base, base_got, whole_act],
        [pltpu.VMEM] * 4 + [pl.ANY],
    )
    got = exchange(sent, "z")
    sent, vals = call(
        reduce_z, [out((nz, 3 * per, slab)), out((VALS, slab))], [owners], [got]
    )
    got = exchange(sent, "z")

    height = (blocks + 1) * group
    shape = (nz, 2, height, slab)
    sent, keep = call(
        factor_terms,
        [out(shape), out(shape, f32)],
        [],
        [cot, act, whole_act],
        scratch=[flat, pltpu.VMEM((blocks + 1, full, slab), f32)],
        flops=6 * tok * full * slab,
    )
    f_got = swap(sent, "c")
    shape = (nz, height, slab)
    sent, keep = call(factor_core, [out(shape), out(shape, f32)], [], [keep, f_got])
    f_got = swap(sent, "xl")

    width = piece + 2 * half + VALS
    shape = (nz // 2, height, slab)
    sent, f_sent, f_keep = call(
        pack_t,
        [out((nt, width, slab)), out(shape), out(shape, f32)],
        [],
        [got, vals, keep, f_got],
    )
    own = exchange(sent, "t")
    f_got = across(f_sent, "z", 1)
    bit = 2
    while bit < nz:
        shape = (nz // 2 // bit, height, slab)
        f_sent, f_keep = call(
            functools.partial(factor_z, bit), [out(shape), out(shape, f32)], [], [f_keep, f_got]
        )
        f_got = across(f_sent, "z", bit)
        bit *= 2
    factor_a, factor_g = call(
        factor_out,
        [out((group, slab), f32), out((blocks, group, slab), f32)],
        [],
        [f_keep, f_got],
    )
    own = follow(own, f_sent)
    other = swap(own, "c")
    qa, qa_other = (own, half, 0), (other, half, 0)
    qg, qg_other = (own, half, 1), (other, half, 1)
    columns, columns_other = (own, piece, 2 * half // piece), (other, piece, 2 * half // piece)
    vals = (own, VALS, (2 * half + piece) // VALS)
    (sent,) = call(
        rotate,
        [out((nt, piece, slab))],
        [],
        [qa, qa_other, columns, columns_other],
        scratch=[pltpu.VMEM((slab, full), bf16)],
        flops=2 * slab * full * half,
    )
    rows = exchange(sent, "t")
    (sent,) = call(
        scale_rows,
        [out((blocks, nt, piece, slab))],
        [],
        [rows, qg, qg_other, vals, factor_a],
        [pltpu.VMEM] * 4 + [pl.ANY],
        scratch=[
            pltpu.VMEM((piece, full), bf16),
            pltpu.VMEM((nt, piece, slab), bf16),
            pltpu.VMEM((slab, slab), f32),
        ],
        flops=4 * piece * full * full,
    )
    own_mixed = exchange(sent.reshape(blocks * nt, piece, slab), ("xl", "t"))
    own_mixed = own_mixed.reshape(blocks, nt, piece, slab)
    other_mixed = swap(own_mixed, "c")
    pre, worker = call(
        finish,
        [out((full, blocks, slab)), out((1, full, slab))],
        [worker_group],
        [qa, qa_other, own_mixed, other_mixed],
        flops=4 * full * full * slab,
    )

    (grad_input,) = call(
        input_grad, [out((tok, slab))], [], [cot, weight], flops=4 * tok * full * slab
    )
    return grad_input, factor_a, factor_g.transpose(1, 0, 2), pre, worker


def solution(mesh):
    dp, tensor = mesh.devices.shape
    fine = Mesh(mesh.devices.reshape(dp // 4, 2, 2, tensor), ("z", "xl", "c", "t"))
    dp = ("z", "xl", "c")
    return jax.shard_map(
        local,
        mesh=fine,
        in_specs=(
            P(dp, "t"),
            P(dp, None, None),
            P("t", None, None),
            P(),
            P(),
            P(dp, None, "t"),
            P(dp, "t"),
            P(dp, None, None, "t"),
            P(dp, None, "t"),
        ),
        out_specs=(
            P(dp, "t"),
            P(dp, "t"),
            P(dp, None, "t"),
            P(None, None, "t"),
            P(dp, None, "t"),
        ),
        check_vma=False,
    )
```

```python
import functools

import jax
import jax.numpy as jnp
from jax import lax
from jax.experimental import pallas as pl
from jax.experimental.pallas import tpu as pltpu
from jax.sharding import Mesh, PartitionSpec as P

damping = 0.001
f32 = jnp.float32
bf16 = jnp.bfloat16
VALS = 16


def exchange(array, axis):
    return lax.all_to_all(array, axis, 0, 0, tiled=True)


def swap(array, axis):
    return lax.ppermute(array, axis, [(0, 1), (1, 0)])


def across(array, axis, step):
    pairs = [(i, i ^ step) for i in range(lax.axis_size(axis))]
    return lax.ppermute(array, axis, pairs)


def full_block(array):
    return pl.BlockSpec(array.shape, lambda i: (0,) * array.ndim)


def call(body, outs, scalars, args, places=None, scratch=(), flops=0, limit=20):
    specs, arrays = [], []
    for arg, place in zip(args, places or [None] * len(args)):
        if isinstance(arg, tuple):
            array, rows, block = arg
            shape = (array.shape[0], rows, array.shape[2])
            specs.append(pl.BlockSpec(shape, functools.partial(lambda k, i: (0, k, 0), block)))
        else:
            array = arg
            specs.append(pl.BlockSpec(memory_space=place) if place else full_block(array))
        arrays.append(array)
    bytes_all = sum(a.size * a.dtype.itemsize for a in arrays + list(outs))
    return pl.pallas_call(
        body,
        grid=(1,),
        out_shape=outs,
        in_specs=[pl.BlockSpec(memory_space=pltpu.SMEM)] * len(scalars) + specs,
        out_specs=[full_block(o) for o in outs],
        scratch_shapes=list(scratch),
        compiler_params=pltpu.CompilerParams(vmem_limit_bytes=limit * 1024 * 1024),
        cost_estimate=pl.CostEstimate(flops=flops, bytes_accessed=bytes_all, transcendentals=0),
    )(*scalars, *arrays)


def follow(array, after):
    return pl.pallas_call(
        lambda *refs: None,
        out_shape=jax.ShapeDtypeStruct(array.shape, array.dtype),
        in_specs=[pl.BlockSpec(memory_space=pl.ANY)] * 2,
        out_specs=pl.BlockSpec(memory_space=pl.ANY),
        input_output_aliases={0: 0},
    )(array, after)


def out(shape, dtype=bf16):
    return jax.ShapeDtypeStruct(shape, dtype)


def dot(left, right, dims=((1,), (0,))):
    return lax.dot_general(left, right, (dims, ((), ())), preferred_element_type=f32)


def value_rows(flags, own, other):
    place = lax.broadcasted_iota(jnp.int32, own.shape, 0)
    take = jnp.zeros(own.shape, jnp.int32)
    for row, flag in enumerate(flags):
        take = jnp.where(place == row, flag.astype(jnp.int32), take)
    return jnp.where(take > 0, own.astype(f32), other.astype(f32)).astype(bf16)


def choose(flag, ref, place, own, other):
    @pl.when(flag)
    def _():
        ref[place] = own()

    @pl.when(jnp.logical_not(flag))
    def _():
        ref[place] = other()


def pack_bases(ba, bg, va, vg, act, sent, keep, every, sem):
    half = ba.shape[1] // 2
    core = lax.axis_index("c")
    place = lax.broadcasted_iota(jnp.int32, (VALS, ba.shape[2]), 0)
    vals = jnp.where(place == 0, va[...].astype(f32), 0.0)
    for j in range(2):
        row = vg[0].astype(f32)[j : j + 1]
        vals = jnp.where(place == 1 + j, row, vals)
    copies = []
    for side, (ref, who) in enumerate(((sent, 1 - core), (keep, core))):
        rows = pl.ds(pl.multiple_of(who * half, half), half)
        for i in range(3):
            source = ba.at[0, rows] if i == 0 else bg.at[0, i - 1, rows]
            copies.append(
                pltpu.make_async_copy(source, ref.at[i * half : (i + 1) * half], sem.at[side, i])
            )
            copies[-1].start()
    sent[3 * half :] = vals.astype(bf16)
    keep[3 * half :] = vals.astype(bf16)
    for k in range(every.shape[0]):
        every[k] = act[...]
    for copy in copies:
        copy.wait()


def select_core(owners, own, got, sent, keep):
    half = (own.shape[0] - VALS) // 3
    core, xl = lax.axis_index("c"), lax.axis_index("xl")
    flags = [owners[i] % 2 == core for i in range(3)]

    def fill(ref, slot, i):
        start = pl.multiple_of(i * half, half)
        choose(
            owners[i] % 2 == core,
            ref,
            slice(slot * half, (slot + 1) * half),
            lambda: own[pl.ds(start, half)],
            lambda: got[pl.ds(start, half)],
        )

    vals = value_rows(flags, own[3 * half :], got[3 * half :])
    for ref, block in ((sent, 2 - xl), (keep, 1 + xl)):
        fill(ref, 0, 0)
        fill(ref, 1, block)
        ref[2 * half :] = vals


def grad_terms(cot, act, sent, keep, flat):
    blocks, half, slab = keep.shape
    tok, _, full = cot.shape
    nt = full // slab
    scale = 1.0 / (tok * lax.axis_size("z") * 4)
    core = lax.axis_index("c")
    flat[...] = cot[...].reshape(tok, blocks * full)
    for j in range(blocks):
        term = dot(flat[:, j * full : (j + 1) * full], act[...], ((0,), (0,))) * scale
        term = term.reshape(nt, 2, slab // 2, slab)
        for c in range(2):
            part = term[:, c].reshape(half, slab)

            @pl.when(core == c)
            def _():
                keep[j] = part

            @pl.when(core != c)
            def _():
                sent[j] = part.astype(bf16)


def add_core(keep, got, sent, rest):
    xl = lax.axis_index("xl")
    sent[...] = (keep[1 - xl] + got[1 - xl].astype(f32)).astype(bf16)
    rest[...] = keep[xl] + got[xl].astype(f32)


def pack_z(owners, keep, got, own, other, after, sent):
    nz, _, slab = sent.shape
    half = (own.shape[0] - VALS) // 2
    per = half // nz
    xl = lax.axis_index("xl")
    total = (keep[...] + got[...].astype(f32)).astype(bf16)
    sent[:, 0:per] = total.reshape(nz, per, slab)
    here = [(owners[i] // 2) % 2 == xl for i in range(3)]
    flags = (here[0], (owners[1 + xl] // 2) % 2 == xl)
    for i, flag in enumerate(flags):
        rows = slice(i * half, (i + 1) * half)
        choose(
            flag,
            sent,
            (slice(None), slice((1 + i) * per, (2 + i) * per)),
            lambda: own[rows].reshape(nz, per, slab),
            lambda: other[rows].reshape(nz, per, slab),
        )
    vals = value_rows(here, own[2 * half :], other[2 * half :])
    for k in range(nz):
        sent[k, 3 * per :] = vals


def reduce_z(owners, got, keep, f_got, sent, vals, f_sent, f_rest):
    nz, height, _ = sent.shape
    per = height // 3
    xl = lax.axis_index("xl")
    source = [owners[i] // 4 for i in range(3)]
    total = got[0, 0:per].astype(f32)
    for k in range(1, nz):
        total = total + got[k, 0:per].astype(f32)
    parts = [total.astype(bf16)]
    for i, src in enumerate((source[0], owners[1 + xl] // 4)):
        parts.append(got[src, (1 + i) * per : (2 + i) * per])
    for i, part in enumerate(parts):
        for k in range(nz):
            sent[k, i * per : (i + 1) * per] = part
    chosen = got[source[0], 3 * per :].astype(f32)
    place = lax.broadcasted_iota(jnp.int32, chosen.shape, 0)
    for i in (1, 2):
        chosen = jnp.where(place == i, got[source[i], 3 * per :].astype(f32), chosen)
    vals[...] = chosen.astype(bf16)
    factor_z(1, keep, f_got, f_sent, f_rest)


def factor_terms(cot, act, whole, sent, keep, flat, both):
    nz, _, height, slab = keep.shape
    group = height // 3
    tok, blocks, full = cot.shape
    nt = full // slab
    scale = 1.0 / (tok * nz * 4)
    core, t = lax.axis_index("c"), lax.axis_index("t")
    flat[...] = cot[...].reshape(tok, blocks * full)
    for j in range(blocks):
        own = flat[:, pl.ds(pl.multiple_of(j * full + t * slab, slab), slab)]
        both[j] = dot(flat[:, j * full : (j + 1) * full], own, ((0,), (0,))) * scale
    for k in range(nt):
        both[blocks, k * slab : (k + 1) * slab] = dot(whole[k], act[...], ((0,), (0,))) * scale
    for i in range(blocks + 1):
        term = both[i].reshape(nz, 2, 2, group, slab)
        rows = slice(i * group, (i + 1) * group)
        for c in range(2):

            @pl.when(core == c)
            def _():
                keep[:, :, rows] = term[:, :, c]

            @pl.when(core != c)
            def _():
                sent[:, :, rows] = term[:, :, c].astype(bf16)


def factor_core(keep, got, sent, rest):
    xl = lax.axis_index("xl")
    sent[...] = (keep[:, 1 - xl] + got[:, 1 - xl].astype(f32)).astype(bf16)
    rest[...] = keep[:, xl] + got[:, xl].astype(f32)


def factor_z(bit, keep, got, sent, rest):
    count, height, slab = keep.shape
    total = keep[...] + got[...].astype(f32)
    if count == 1:
        rest[...] = total
    else:
        mine = (lax.axis_index("z") // bit) % 2
        total = total.reshape(count // 2, 2, height, slab)
        for side in range(2):

            @pl.when(mine == side)
            def _():
                rest[...] = total[:, side]
                sent[...] = total[:, 1 - side].astype(bf16)


def pack_t(got, vals, keep, f_got, sent, f_sent, f_rest):
    nz, height, slab = got.shape
    nt = sent.shape[0]
    per = height // 3
    half = nz * per
    piece = half // nt
    for k in range(nt):
        for i in range(2):
            rows = got[:, (1 + i) * per : (2 + i) * per].reshape(half, slab)
            sent[k, i * half : (i + 1) * half] = rows
        sent[k, 2 * half + piece :] = vals[...]
    sent[:, 2 * half : 2 * half + piece] = got[:, 0:per].reshape(nt, piece, slab)
    factor_z(4, keep, f_got, f_sent, f_rest)


def factor_out(keep, got, factor_a, factor_g):
    group = factor_a.shape[0]
    total = keep[0] + got[0].astype(f32)
    for j in range(2):
        factor_g[j] = total[j * group : (j + 1) * group]
    factor_a[...] = total[2 * group :]


def rotate(own, other, own_grad, other_grad, sent, grad):
    nt, half, slab = own.shape
    piece = slab // 2
    core = lax.axis_index("c")
    mine = pl.multiple_of(core * piece, piece)
    theirs = pl.multiple_of((1 - core) * piece, piece)
    for k in range(nt):
        grad[pl.ds(mine, piece), k * slab : (k + 1) * slab] = own_grad[k]
        grad[pl.ds(theirs, piece), k * slab : (k + 1) * slab] = other_grad[k]
    near = grad[:, pl.ds(pl.multiple_of(core * half, half), half)]
    far = grad[:, pl.ds(pl.multiple_of((1 - core) * half, half), half)]
    for i in range(nt // 2):
        k = core * (nt // 2) + i
        turned = dot(near, own[k]) + dot(far, other[k])
        turned = turned.T.astype(bf16)
        sent[2 * i] = turned[0:piece]
        sent[2 * i + 1] = turned[piece:]


def scale_rows(rows, own, other, vals, sent, rot, scaled, column):
    nt, piece, slab = rows.shape
    half = own.shape[1]
    core, xl, t = lax.axis_index("c"), lax.axis_index("xl"), lax.axis_index("t")
    row = vals[core * (nt // 2) + t // 2].astype(f32)[0:1]
    column[...] = jnp.broadcast_to(row, (slab, slab)).T
    la = column[pl.ds(pl.multiple_of((t % 2) * piece, piece), piece)]
    for k in range(nt):
        rot[:, k * slab : (k + 1) * slab] = rows[k]
    near = rot[:, pl.ds(pl.multiple_of(core * half, half), half)]
    far = rot[:, pl.ds(pl.multiple_of((1 - core) * half, half), half)]
    for k in range(nt):
        spectral = dot(near, own[k]) + dot(far, other[k])
        values = vals[k].astype(f32)
        lg = jnp.where(xl == 0, values[1:2], values[2:3])
        scaled[k] = (spectral / (la * lg + damping)).astype(bf16)
    for side, ref in ((core, own), (1 - core, other)):
        mixed = dot(scaled[0], ref[0], ((1,), (1,)))
        for k in range(1, nt):
            mixed = mixed + dot(scaled[k], ref[k], ((1,), (1,)))
        mixed = mixed.astype(bf16)
        for i in range(nt // 2):
            for copy in range(2):
                sent[copy, side * (nt // 2) + i] = mixed[:, i * slab : (i + 1) * slab]


def finish(groups, own, other, own_mixed, other_mixed, pre, worker):
    blocks, nt, piece, slab = own_mixed.shape
    half = own.shape[1]
    core = lax.axis_index("c")
    replica = (lax.axis_index("z") * 2 + lax.axis_index("xl")) * 2 + core
    group = groups[replica]
    for side, ref in ((core, own), (1 - core, other)):
        total = jnp.zeros((half, blocks * slab), f32)
        for part, mixed in ((core, own_mixed), (1 - core, other_mixed)):
            for i in range(nt // 2):
                right = jnp.concatenate(
                    [mixed[j, 2 * i : 2 * i + 2].reshape(2 * piece, slab) for j in range(blocks)], 1
                )
                total = total + dot(ref[part * (nt // 2) + i], right)
        total = total.astype(bf16)
        place = pl.ds(pl.multiple_of(side * half, half), half)
        pre[place] = total.reshape(half, blocks, slab)
        choose(
            group == 0,
            worker,
            (0, place),
            lambda: total[:, :slab],
            lambda: total[:, slab:],
        )


def input_grad(cot, weight, grad):
    tok, blocks, full = cot.shape
    left = cot[...].reshape(tok, blocks * full)
    right = weight[...].reshape(weight.shape[0], blocks * full)
    grad[...] = dot(left, right, ((1,), (1,))).astype(bf16)


def local(act, cot, weight, owners, worker_group, basis_a, values_a, basis_g, values_g):
    tok, slab = act.shape
    blocks, full = cot.shape[1:]
    nz, nt = lax.axis_size("z"), lax.axis_size("t")
    group = full // (nz * 4)
    half, piece = full // 2, slab // 2
    per = half // nz

    shape = (3 * half + VALS, slab)
    sent, keep, every = call(
        pack_bases,
        [out(shape), out(shape), out((nt, tok, slab))],
        [],
        [basis_a, basis_g, values_a, values_g, act],
        [pl.ANY, pl.ANY, None, None, None],
        scratch=[pltpu.SemaphoreType.DMA((2, 3))],
        limit=56,
    )
    got = swap(sent, "c")
    whole_act = exchange(every, "t")
    shape = (2 * half + VALS, slab)
    sent, base = call(select_core, [out(shape), out(shape)], [owners], [keep, got])
    base_got = swap(sent, "xl")

    flat = pltpu.VMEM((tok, blocks * full), bf16)
    shape = (blocks, half, slab)
    sent, keep = call(
        grad_terms,
        [out(shape), out(shape, f32)],
        [],
        [cot, act],
        scratch=[flat],
        flops=4 * tok * full * slab,
    )
    got = swap(sent, "c")
    sent, keep = call(add_core, [out(shape[1:]), out(shape[1:], f32)], [], [keep, got])
    got = swap(sent, "xl")

    (sent,) = call(
        pack_z,
        [out((nz, 3 * per + VALS, slab))],
        [owners],
        [keep, got, base, base_got, whole_act],
        [None] * 4 + [pl.ANY],
    )
    got = exchange(sent, "z")

    height = (blocks + 1) * group
    shape = (nz, 2, height, slab)
    sent, f_keep = call(
        factor_terms,
        [out(shape), out(shape, f32)],
        [],
        [cot, act, whole_act],
        scratch=[flat, pltpu.VMEM((blocks + 1, full, slab), f32)],
        flops=6 * tok * full * slab,
    )
    f_got = swap(sent, "c")
    shape = (nz, height, slab)
    sent, f_keep = call(factor_core, [out(shape), out(shape, f32)], [], [f_keep, f_got])
    f_got = swap(sent, "xl")

    shape = (nz // 2, height, slab)
    sent, vals, f_sent, f_keep = call(
        reduce_z,
        [out((nz, 3 * per, slab)), out((VALS, slab)), out(shape), out(shape, f32)],
        [owners],
        [got, f_keep, f_got],
    )
    got = exchange(sent, "z")
    f_got = across(f_sent, "z", 1)
    shape = (nz // 4, height, slab)
    f_sent, f_keep = call(
        functools.partial(factor_z, 2), [out(shape), out(shape, f32)], [], [f_keep, f_got]
    )
    f_got = across(f_sent, "z", 2)

    width = piece + 2 * half + VALS
    shape = (nz // 8, height, slab)
    sent, f_sent, f_keep = call(
        pack_t,
        [out((nt, width, slab)), out(shape), out(shape, f32)],
        [],
        [got, vals, f_keep, f_got],
    )
    own = exchange(sent, "t")
    f_got = across(f_sent, "z", 4)
    shape = (nz // 16, height, slab)
    f_sent, f_keep = call(
        functools.partial(factor_z, 8), [out(shape), out(shape, f32)], [], [f_keep, f_got]
    )
    f_got = across(f_sent, "z", 8)
    factor_a, factor_g = call(
        factor_out,
        [out((group, slab), f32), out((blocks, group, slab), f32)],
        [],
        [f_keep, f_got],
    )
    own = follow(own, factor_a)
    other = swap(own, "c")
    qa, qa_other = (own, half, 0), (other, half, 0)
    qg, qg_other = (own, half, 1), (other, half, 1)
    columns, columns_other = (own, piece, 2 * half // piece), (other, piece, 2 * half // piece)
    vals = (own, VALS, (2 * half + piece) // VALS)
    (sent,) = call(
        rotate,
        [out((nt, piece, slab))],
        [],
        [qa, qa_other, columns, columns_other],
        scratch=[pltpu.VMEM((slab, full), bf16)],
        flops=2 * slab * full * half,
    )
    rows = exchange(sent, "t")
    (sent,) = call(
        scale_rows,
        [out((blocks, nt, piece, slab))],
        [],
        [rows, qg, qg_other, vals],
        scratch=[
            pltpu.VMEM((piece, full), bf16),
            pltpu.VMEM((nt, piece, slab), bf16),
            pltpu.VMEM((slab, slab), f32),
        ],
        flops=4 * piece * full * full,
    )
    own_mixed = exchange(sent.reshape(blocks * nt, piece, slab), ("xl", "t"))
    own_mixed = own_mixed.reshape(blocks, nt, piece, slab)
    other_mixed = swap(own_mixed, "c")
    pre, worker = call(
        finish,
        [out((full, blocks, slab)), out((1, full, slab))],
        [worker_group],
        [qa, qa_other, own_mixed, other_mixed],
        flops=4 * full * full * slab,
    )

    (grad_input,) = call(
        input_grad, [out((tok, slab))], [], [cot, weight], flops=4 * tok * full * slab
    )
    return grad_input, factor_a, factor_g.transpose(1, 0, 2), pre, worker


def solution(mesh):
    dp, tensor = mesh.devices.shape
    fine = Mesh(mesh.devices.reshape(dp // 4, 2, 2, tensor), ("z", "xl", "c", "t"))
    dp = ("z", "xl", "c")
    return jax.shard_map(
        local,
        mesh=fine,
        in_specs=(
            P(dp, "t"),
            P(dp, None, None),
            P("t", None, None),
            P(),
            P(),
            P(dp, None, "t"),
            P(dp, "t"),
            P(dp, None, None, "t"),
            P(dp, None, "t"),
        ),
        out_specs=(
            P(dp, "t"),
            P(dp, "t"),
            P(dp, None, "t"),
            P(None, None, "t"),
            P(dp, None, "t"),
        ),
        check_vma=False,
    )
```

```python
import functools

import jax
import jax.numpy as jnp
from jax import lax
from jax.experimental import pallas as pl
from jax.experimental.pallas import tpu as pltpu
from jax.sharding import Mesh, PartitionSpec as P

damping = 0.001
f32 = jnp.float32
bf16 = jnp.bfloat16
VALS = 16


def exchange(array, axis):
    return lax.all_to_all(array, axis, 0, 0, tiled=True)


def swap(array, axis):
    return lax.ppermute(array, axis, [(0, 1), (1, 0)])


def across(array, axis, step):
    pairs = [(i, i ^ step) for i in range(lax.axis_size(axis))]
    return lax.ppermute(array, axis, pairs)


def full_block(array):
    return pl.BlockSpec(array.shape, lambda i: (0,) * array.ndim)


def call(body, outs, scalars, args, places=None, scratch=(), flops=0, limit=20):
    specs, arrays = [], []
    for arg, place in zip(args, places or [None] * len(args)):
        if isinstance(arg, tuple):
            array, rows, block = arg
            shape = (array.shape[0], rows, array.shape[2])
            specs.append(pl.BlockSpec(shape, functools.partial(lambda k, i: (0, k, 0), block)))
        else:
            array = arg
            specs.append(pl.BlockSpec(memory_space=place) if place else full_block(array))
        arrays.append(array)
    bytes_all = sum(a.size * a.dtype.itemsize for a in arrays + list(outs))
    return pl.pallas_call(
        body,
        grid=(1,),
        out_shape=outs,
        in_specs=[pl.BlockSpec(memory_space=pltpu.SMEM)] * len(scalars) + specs,
        out_specs=[full_block(o) for o in outs],
        scratch_shapes=list(scratch),
        compiler_params=pltpu.CompilerParams(vmem_limit_bytes=limit * 1024 * 1024),
        cost_estimate=pl.CostEstimate(flops=flops, bytes_accessed=bytes_all, transcendentals=0),
    )(*scalars, *arrays)


def follow(array, after):
    return pl.pallas_call(
        lambda *refs: None,
        out_shape=jax.ShapeDtypeStruct(array.shape, array.dtype),
        in_specs=[pl.BlockSpec(memory_space=pl.ANY)] * 2,
        out_specs=pl.BlockSpec(memory_space=pl.ANY),
        input_output_aliases={0: 0},
        compiler_params=pltpu.CompilerParams(vmem_limit_bytes=56 * 1024 * 1024),
    )(array, after)


def out(shape, dtype=bf16):
    return jax.ShapeDtypeStruct(shape, dtype)


def dot(left, right, dims=((1,), (0,))):
    return lax.dot_general(left, right, (dims, ((), ())), preferred_element_type=f32)


def value_rows(flags, own, other):
    place = lax.broadcasted_iota(jnp.int32, own.shape, 0)
    take = jnp.zeros(own.shape, jnp.int32)
    for row, flag in enumerate(flags):
        take = jnp.where(place == row, flag.astype(jnp.int32), take)
    return jnp.where(take > 0, own.astype(f32), other.astype(f32)).astype(bf16)


def choose(flag, ref, place, own, other):
    @pl.when(flag)
    def _():
        ref[place] = own()

    @pl.when(jnp.logical_not(flag))
    def _():
        ref[place] = other()


def pack_bases(ba, bg, va, vg, act, sent, keep, every, sem):
    half = ba.shape[1] // 2
    core = lax.axis_index("c")
    place = lax.broadcasted_iota(jnp.int32, (VALS, ba.shape[2]), 0)
    vals = jnp.where(place == 0, va[...].astype(f32), 0.0)
    for j in range(2):
        row = vg[0].astype(f32)[j : j + 1]
        vals = jnp.where(place == 1 + j, row, vals)
    copies = []
    for side, (ref, who) in enumerate(((sent, 1 - core), (keep, core))):
        rows = pl.ds(pl.multiple_of(who * half, half), half)
        for i in range(3):
            source = ba.at[0, rows] if i == 0 else bg.at[0, i - 1, rows]
            copies.append(
                pltpu.make_async_copy(source, ref.at[i * half : (i + 1) * half], sem.at[side, i])
            )
            copies[-1].start()
    sent[3 * half :] = vals.astype(bf16)
    keep[3 * half :] = vals.astype(bf16)
    for k in range(every.shape[0]):
        every[k] = act[...]
    for copy in copies:
        copy.wait()


def select_core(owners, own, got, sent, keep):
    half = (own.shape[0] - VALS) // 3
    core, xl = lax.axis_index("c"), lax.axis_index("xl")
    flags = [owners[i] % 2 == core for i in range(3)]

    def fill(ref, slot, i):
        start = pl.multiple_of(i * half, half)
        choose(
            owners[i] % 2 == core,
            ref,
            slice(slot * half, (slot + 1) * half),
            lambda: own[pl.ds(start, half)],
            lambda: got[pl.ds(start, half)],
        )

    vals = value_rows(flags, own[3 * half :], got[3 * half :])
    for ref, block in ((sent, 2 - xl), (keep, 1 + xl)):
        fill(ref, 0, 0)
        fill(ref, 1, block)
        ref[2 * half :] = vals


def grad_terms(cot, act, sent, keep, flat):
    blocks, half, slab = keep.shape
    tok, _, full = cot.shape
    nt = full // slab
    scale = 1.0 / (tok * lax.axis_size("z") * 4)
    core = lax.axis_index("c")
    flat[...] = cot[...].reshape(tok, blocks * full)
    for j in range(blocks):
        term = dot(flat[:, j * full : (j + 1) * full], act[...], ((0,), (0,))) * scale
        term = term.reshape(nt, 2, slab // 2, slab)
        for c in range(2):
            part = term[:, c].reshape(half, slab)

            @pl.when(core == c)
            def _():
                keep[j] = part

            @pl.when(core != c)
            def _():
                sent[j] = part.astype(bf16)


def add_core(keep, got, sent, rest):
    xl = lax.axis_index("xl")
    sent[...] = (keep[1 - xl] + got[1 - xl].astype(f32)).astype(bf16)
    rest[...] = keep[xl] + got[xl].astype(f32)


def pack_z(owners, keep, got, own, other, sent):
    nz, _, slab = sent.shape
    half = (own.shape[0] - VALS) // 2
    per = half // nz
    xl = lax.axis_index("xl")
    total = (keep[...] + got[...].astype(f32)).astype(bf16)
    sent[:, 0:per] = total.reshape(nz, per, slab)
    here = [(owners[i] // 2) % 2 == xl for i in range(3)]
    flags = (here[0], (owners[1 + xl] // 2) % 2 == xl)
    for i, flag in enumerate(flags):
        rows = slice(i * half, (i + 1) * half)
        choose(
            flag,
            sent,
            (slice(None), slice((1 + i) * per, (2 + i) * per)),
            lambda: own[rows].reshape(nz, per, slab),
            lambda: other[rows].reshape(nz, per, slab),
        )
    vals = value_rows(here, own[2 * half :], other[2 * half :])
    for k in range(nz):
        sent[k, 3 * per :] = vals


def reduce_z(owners, got, keep, f_got, sent, vals, f_sent, f_rest):
    nz, height, _ = sent.shape
    per = height // 3
    xl = lax.axis_index("xl")
    source = [owners[i] // 4 for i in range(3)]
    total = got[0, 0:per].astype(f32)
    for k in range(1, nz):
        total = total + got[k, 0:per].astype(f32)
    parts = [total.astype(bf16)]
    for i, src in enumerate((source[0], owners[1 + xl] // 4)):
        parts.append(got[src, (1 + i) * per : (2 + i) * per])
    for i, part in enumerate(parts):
        for k in range(nz):
            sent[k, i * per : (i + 1) * per] = part
    chosen = got[source[0], 3 * per :].astype(f32)
    place = lax.broadcasted_iota(jnp.int32, chosen.shape, 0)
    for i in (1, 2):
        chosen = jnp.where(place == i, got[source[i], 3 * per :].astype(f32), chosen)
    vals[...] = chosen.astype(bf16)
    factor_z(1, keep, f_got, f_sent, f_rest)


def factor_terms(cot, act, whole, sent, keep, flat, both):
    nz, _, height, slab = keep.shape
    group = height // 3
    tok, blocks, full = cot.shape
    nt = full // slab
    scale = 1.0 / (tok * nz * 4)
    core, t = lax.axis_index("c"), lax.axis_index("t")
    flat[...] = cot[...].reshape(tok, blocks * full)
    for j in range(blocks):
        own = flat[:, pl.ds(pl.multiple_of(j * full + t * slab, slab), slab)]
        both[j] = dot(flat[:, j * full : (j + 1) * full], own, ((0,), (0,))) * scale
    for k in range(nt):
        both[blocks, k * slab : (k + 1) * slab] = dot(whole[k], act[...], ((0,), (0,))) * scale
    for i in range(blocks + 1):
        term = both[i].reshape(nz, 2, 2, group, slab)
        rows = slice(i * group, (i + 1) * group)
        for c in range(2):

            @pl.when(core == c)
            def _():
                keep[:, :, rows] = term[:, :, c]

            @pl.when(core != c)
            def _():
                sent[:, :, rows] = term[:, :, c].astype(bf16)


def factor_core(keep, got, sent, rest):
    xl = lax.axis_index("xl")
    sent[...] = (keep[:, 1 - xl] + got[:, 1 - xl].astype(f32)).astype(bf16)
    rest[...] = keep[:, xl] + got[:, xl].astype(f32)


def factor_z(bit, keep, got, sent, rest):
    count, height, slab = keep.shape
    total = keep[...] + got[...].astype(f32)
    if count == 1:
        rest[...] = total
    else:
        mine = (lax.axis_index("z") // bit) % 2
        total = total.reshape(count // 2, 2, height, slab)
        for side in range(2):

            @pl.when(mine == side)
            def _():
                rest[...] = total[:, side]
                sent[...] = total[:, 1 - side].astype(bf16)


def pack_t(got, vals, keep, f_got, sent, f_sent, f_rest):
    nz, height, slab = got.shape
    nt = sent.shape[0]
    per = height // 3
    half = nz * per
    piece = half // nt
    for k in range(nt):
        for i in range(2):
            rows = got[:, (1 + i) * per : (2 + i) * per].reshape(half, slab)
            sent[k, i * half : (i + 1) * half] = rows
        sent[k, 2 * half + piece :] = vals[...]
    sent[:, 2 * half : 2 * half + piece] = got[:, 0:per].reshape(nt, piece, slab)
    factor_z(2, keep, f_got, f_sent, f_rest)


def factor_out(keep, got, factor_a, factor_g):
    group = factor_a.shape[0]
    total = keep[0] + got[0].astype(f32)
    for j in range(2):
        factor_g[j] = total[j * group : (j + 1) * group]
    factor_a[...] = total[2 * group :]


def rotate(own, other, own_grad, other_grad, sent, grad):
    nt, half, slab = own.shape
    piece = slab // 2
    core = lax.axis_index("c")
    mine = pl.multiple_of(core * piece, piece)
    theirs = pl.multiple_of((1 - core) * piece, piece)
    for k in range(nt):
        grad[pl.ds(mine, piece), k * slab : (k + 1) * slab] = own_grad[k]
        grad[pl.ds(theirs, piece), k * slab : (k + 1) * slab] = other_grad[k]
    near = grad[:, pl.ds(pl.multiple_of(core * half, half), half)]
    far = grad[:, pl.ds(pl.multiple_of((1 - core) * half, half), half)]
    for i in range(nt // 2):
        k = core * (nt // 2) + i
        turned = dot(near, own[k]) + dot(far, other[k])
        turned = turned.T.astype(bf16)
        sent[2 * i] = turned[0:piece]
        sent[2 * i + 1] = turned[piece:]


def scale_rows(rows, own, other, vals, sent, rot, scaled, column):
    nt, piece, slab = rows.shape
    half = own.shape[1]
    core, xl, t = lax.axis_index("c"), lax.axis_index("xl"), lax.axis_index("t")
    row = vals[core * (nt // 2) + t // 2].astype(f32)[0:1]
    column[...] = jnp.broadcast_to(row, (slab, slab)).T
    la = column[pl.ds(pl.multiple_of((t % 2) * piece, piece), piece)]
    for k in range(nt):
        rot[:, k * slab : (k + 1) * slab] = rows[k]
    near = rot[:, pl.ds(pl.multiple_of(core * half, half), half)]
    far = rot[:, pl.ds(pl.multiple_of((1 - core) * half, half), half)]
    for k in range(nt):
        spectral = dot(near, own[k]) + dot(far, other[k])
        values = vals[k].astype(f32)
        lg = jnp.where(xl == 0, values[1:2], values[2:3])
        scaled[k] = (spectral / (la * lg + damping)).astype(bf16)
    for side, ref in ((core, own), (1 - core, other)):
        mixed = dot(scaled[0], ref[0], ((1,), (1,)))
        for k in range(1, nt):
            mixed = mixed + dot(scaled[k], ref[k], ((1,), (1,)))
        mixed = mixed.astype(bf16)
        for i in range(nt // 2):
            for copy in range(2):
                sent[copy, side * (nt // 2) + i] = mixed[:, i * slab : (i + 1) * slab]


def finish(groups, own, other, own_mixed, other_mixed, pre, worker):
    blocks, nt, piece, slab = own_mixed.shape
    half = own.shape[1]
    core = lax.axis_index("c")
    replica = (lax.axis_index("z") * 2 + lax.axis_index("xl")) * 2 + core
    group = groups[replica]
    for side, ref in ((core, own), (1 - core, other)):
        total = jnp.zeros((half, blocks * slab), f32)
        for part, mixed in ((core, own_mixed), (1 - core, other_mixed)):
            for i in range(nt // 4):
                k = part * (nt // 2) + 2 * i
                left = jnp.concatenate([ref[k], ref[k + 1]], 1)
                right = jnp.concatenate(
                    [mixed[j, 4 * i : 4 * i + 4].reshape(4 * piece, slab) for j in range(blocks)], 1
                )
                total = total + dot(left, right)
        total = total.astype(bf16)
        place = pl.ds(pl.multiple_of(side * half, half), half)
        pre[place] = total.reshape(half, blocks, slab)
        choose(
            group == 0,
            worker,
            (0, place),
            lambda: total[:, :slab],
            lambda: total[:, slab:],
        )


def input_grad(cot, weight, grad):
    tok, blocks, full = cot.shape
    left = cot[...].reshape(tok, blocks * full)
    right = weight[...].reshape(weight.shape[0], blocks * full)
    grad[...] = dot(left, right, ((1,), (1,))).astype(bf16)


def local(act, cot, weight, owners, worker_group, basis_a, values_a, basis_g, values_g):
    tok, slab = act.shape
    blocks, full = cot.shape[1:]
    nz, nt = lax.axis_size("z"), lax.axis_size("t")
    group = full // (nz * 4)
    half, piece = full // 2, slab // 2
    per = half // nz

    shape = (3 * half + VALS, slab)
    sent, keep, every = call(
        pack_bases,
        [out(shape), out(shape), out((nt, tok, slab))],
        [],
        [basis_a, basis_g, values_a, values_g, act],
        [pl.ANY, pl.ANY, None, None, None],
        scratch=[pltpu.SemaphoreType.DMA((2, 3))],
        limit=56,
    )
    got = swap(sent, "c")
    whole_act = exchange(every, "t")
    shape = (2 * half + VALS, slab)
    sent, base = call(select_core, [out(shape), out(shape)], [owners], [keep, got])
    base_got = swap(sent, "xl")

    flat = pltpu.VMEM((tok, blocks * full), bf16)
    shape = (blocks, half, slab)
    sent, keep = call(
        grad_terms,
        [out(shape), out(shape, f32)],
        [],
        [cot, act],
        scratch=[flat],
        flops=4 * tok * full * slab,
    )
    got = swap(sent, "c")
    sent, keep = call(add_core, [out(shape[1:]), out(shape[1:], f32)], [], [keep, got])
    got = swap(sent, "xl")

    (sent,) = call(
        pack_z,
        [out((nz, 3 * per + VALS, slab))],
        [owners],
        [keep, got, base, base_got],
    )
    got = exchange(follow(sent, whole_act), "z")

    height = (blocks + 1) * group
    shape = (nz, 2, height, slab)
    sent, f_keep = call(
        factor_terms,
        [out(shape), out(shape, f32)],
        [],
        [cot, act, whole_act],
        scratch=[flat, pltpu.VMEM((blocks + 1, full, slab), f32)],
        flops=6 * tok * full * slab,
    )
    f_got = swap(sent, "c")
    shape = (nz, height, slab)
    sent, f_keep = call(factor_core, [out(shape), out(shape, f32)], [], [f_keep, f_got])
    f_got = swap(sent, "xl")

    shape = (nz // 2, height, slab)
    sent, vals, f_sent, f_keep = call(
        reduce_z,
        [out((nz, 3 * per, slab)), out((VALS, slab)), out(shape), out(shape, f32)],
        [owners],
        [got, f_keep, f_got],
    )
    got = exchange(sent, "z")
    f_got = across(f_sent, "z", 1)

    width = piece + 2 * half + VALS
    shape = (nz // 4, height, slab)
    sent, f_sent, f_keep = call(
        pack_t,
        [out((nt, width, slab)), out(shape), out(shape, f32)],
        [],
        [got, vals, f_keep, f_got],
        limit=56,
    )
    own = exchange(sent, "t")
    f_got = across(f_sent, "z", 2)
    for bit in (4, 8):
        shape = (nz // 2 // bit, height, slab)
        f_sent, f_keep = call(
            functools.partial(factor_z, bit), [out(shape), out(shape, f32)], [], [f_keep, f_got]
        )
        f_got = across(f_sent, "z", bit)
    factor_a, factor_g = call(
        factor_out,
        [out((group, slab), f32), out((blocks, group, slab), f32)],
        [],
        [f_keep, f_got],
    )
    own = follow(own, factor_a)
    other = swap(own, "c")
    qa, qa_other = (own, half, 0), (other, half, 0)
    qg, qg_other = (own, half, 1), (other, half, 1)
    columns, columns_other = (own, piece, 2 * half // piece), (other, piece, 2 * half // piece)
    vals = (own, VALS, (2 * half + piece) // VALS)
    (sent,) = call(
        rotate,
        [out((nt, piece, slab))],
        [],
        [qa, qa_other, columns, columns_other],
        scratch=[pltpu.VMEM((slab, full), bf16)],
        flops=2 * slab * full * half,
        limit=56,
    )
    rows = exchange(sent, "t")
    (sent,) = call(
        scale_rows,
        [out((blocks, nt, piece, slab))],
        [],
        [rows, qg, qg_other, vals],
        scratch=[
            pltpu.VMEM((piece, full), bf16),
            pltpu.VMEM((nt, piece, slab), bf16),
            pltpu.VMEM((slab, slab), f32),
        ],
        flops=4 * piece * full * full,
        limit=56,
    )
    own_mixed = exchange(sent.reshape(blocks * nt, piece, slab), ("xl", "t"))
    own_mixed = own_mixed.reshape(blocks, nt, piece, slab)
    other_mixed = swap(own_mixed, "c")
    pre, worker = call(
        finish,
        [out((full, blocks, slab)), out((1, full, slab))],
        [worker_group],
        [qa, qa_other, own_mixed, other_mixed],
        flops=4 * full * full * slab,
        limit=56,
    )

    (grad_input,) = call(
        input_grad, [out((tok, slab))], [], [cot, weight], flops=4 * tok * full * slab
    )
    return grad_input, factor_a, factor_g.transpose(1, 0, 2), pre, worker


def solution(mesh):
    dp, tensor = mesh.devices.shape
    fine = Mesh(mesh.devices.reshape(dp // 4, 2, 2, tensor), ("z", "xl", "c", "t"))
    dp = ("z", "xl", "c")
    return jax.shard_map(
        local,
        mesh=fine,
        in_specs=(
            P(dp, "t"),
            P(dp, None, None),
            P("t", None, None),
            P(),
            P(),
            P(dp, None, "t"),
            P(dp, "t"),
            P(dp, None, None, "t"),
            P(dp, None, "t"),
        ),
        out_specs=(
            P(dp, "t"),
            P(dp, "t"),
            P(dp, None, "t"),
            P(None, None, "t"),
            P(dp, None, "t"),
        ),
        check_vma=False,
    )
```

```python
import functools

import jax
import jax.numpy as jnp
from jax import lax
from jax.experimental import pallas as pl
from jax.experimental.pallas import tpu as pltpu
from jax.sharding import Mesh, PartitionSpec as P

damping = 0.001
f32 = jnp.float32
bf16 = jnp.bfloat16
VALS = 16


def exchange(array, axis):
    return lax.all_to_all(array, axis, 0, 0, tiled=True)


def swap(array, axis):
    return lax.ppermute(array, axis, [(0, 1), (1, 0)])


def across(array, axis, step):
    pairs = [(i, i ^ step) for i in range(lax.axis_size(axis))]
    return lax.ppermute(array, axis, pairs)


def full_block(array):
    return pl.BlockSpec(array.shape, lambda i: (0,) * array.ndim)


def call(body, outs, scalars, args, places=None, scratch=(), flops=0, limit=20):
    specs, arrays = [], []
    for arg, place in zip(args, places or [None] * len(args)):
        if isinstance(arg, tuple):
            array, rows, block = arg
            shape = (array.shape[0], rows, array.shape[2])
            specs.append(pl.BlockSpec(shape, functools.partial(lambda k, i: (0, k, 0), block)))
        else:
            array = arg
            specs.append(pl.BlockSpec(memory_space=place) if place else full_block(array))
        arrays.append(array)
    bytes_all = sum(a.size * a.dtype.itemsize for a in arrays + list(outs))
    return pl.pallas_call(
        body,
        grid=(1,),
        out_shape=outs,
        in_specs=[pl.BlockSpec(memory_space=pltpu.SMEM)] * len(scalars) + specs,
        out_specs=[full_block(o) for o in outs],
        scratch_shapes=list(scratch),
        compiler_params=pltpu.CompilerParams(vmem_limit_bytes=limit * 1024 * 1024),
        cost_estimate=pl.CostEstimate(flops=flops, bytes_accessed=bytes_all, transcendentals=0),
    )(*scalars, *arrays)


def follow(array, after, limit):
    return pl.pallas_call(
        lambda *refs: None,
        out_shape=jax.ShapeDtypeStruct(array.shape, array.dtype),
        in_specs=[pl.BlockSpec(memory_space=pl.ANY)] * 2,
        out_specs=pl.BlockSpec(memory_space=pl.ANY),
        input_output_aliases={0: 0},
        compiler_params=pltpu.CompilerParams(vmem_limit_bytes=limit * 1024 * 1024),
    )(array, after)


def out(shape, dtype=bf16):
    return jax.ShapeDtypeStruct(shape, dtype)


def dot(left, right, dims=((1,), (0,))):
    return lax.dot_general(left, right, (dims, ((), ())), preferred_element_type=f32)


def value_rows(flags, own, other):
    place = lax.broadcasted_iota(jnp.int32, own.shape, 0)
    take = jnp.zeros(own.shape, jnp.int32)
    for row, flag in enumerate(flags):
        take = jnp.where(place == row, flag.astype(jnp.int32), take)
    return jnp.where(take > 0, own.astype(f32), other.astype(f32)).astype(bf16)


def choose(flag, ref, place, own, other):
    @pl.when(flag)
    def _():
        ref[place] = own()

    @pl.when(jnp.logical_not(flag))
    def _():
        ref[place] = other()


def pack_bases(ba, bg, va, vg, act, sent, keep, every, sem):
    half = ba.shape[1] // 2
    core = lax.axis_index("c")
    place = lax.broadcasted_iota(jnp.int32, (VALS, ba.shape[2]), 0)
    vals = jnp.where(place == 0, va[...].astype(f32), 0.0)
    for j in range(2):
        row = vg[0].astype(f32)[j : j + 1]
        vals = jnp.where(place == 1 + j, row, vals)
    copies = []
    for side, (ref, who) in enumerate(((sent, 1 - core), (keep, core))):
        rows = pl.ds(pl.multiple_of(who * half, half), half)
        for i in range(3):
            source = ba.at[0, rows] if i == 0 else bg.at[0, i - 1, rows]
            copies.append(
                pltpu.make_async_copy(source, ref.at[i * half : (i + 1) * half], sem.at[side, i])
            )
            copies[-1].start()
    sent[3 * half :] = vals.astype(bf16)
    keep[3 * half :] = vals.astype(bf16)
    for k in range(every.shape[0]):
        every[k] = act[...]
    for copy in copies:
        copy.wait()


def select_core(owners, own, got, sent, keep):
    half = (own.shape[0] - VALS) // 3
    core, xl = lax.axis_index("c"), lax.axis_index("xl")
    flags = [owners[i] % 2 == core for i in range(3)]

    def fill(ref, slot, i):
        start = pl.multiple_of(i * half, half)
        choose(
            owners[i] % 2 == core,
            ref,
            slice(slot * half, (slot + 1) * half),
            lambda: own[pl.ds(start, half)],
            lambda: got[pl.ds(start, half)],
        )

    vals = value_rows(flags, own[3 * half :], got[3 * half :])
    for ref, block in ((sent, 2 - xl), (keep, 1 + xl)):
        fill(ref, 0, 0)
        fill(ref, 1, block)
        ref[2 * half :] = vals


def grad_terms(cot, act, sent, keep, flat):
    blocks, half, slab = keep.shape
    tok, _, full = cot.shape
    nt = full // slab
    scale = 1.0 / (tok * lax.axis_size("z") * 4)
    core = lax.axis_index("c")
    flat[...] = cot[...].reshape(tok, blocks * full)
    for j in range(blocks):
        term = dot(flat[:, j * full : (j + 1) * full], act[...], ((0,), (0,))) * scale
        term = term.reshape(nt, 2, slab // 2, slab)
        for c in range(2):
            part = term[:, c].reshape(half, slab)

            @pl.when(core == c)
            def _():
                keep[j] = part

            @pl.when(core != c)
            def _():
                sent[j] = part.astype(bf16)


def add_core(keep, got, sent, rest):
    xl = lax.axis_index("xl")
    sent[...] = (keep[1 - xl] + got[1 - xl].astype(f32)).astype(bf16)
    rest[...] = keep[xl] + got[xl].astype(f32)


def pack_z(owners, keep, got, own, other, sent, vals):
    nz, _, slab = sent.shape
    half = (own.shape[0] - VALS) // 2
    per = half // nz
    xl = lax.axis_index("xl")
    total = (keep[...] + got[...].astype(f32)).astype(bf16)
    sent[:, 0:per] = total.reshape(nz, per, slab)
    here = [(owners[i] // 2) % 2 == xl for i in range(3)]
    flags = (here[0], (owners[1 + xl] // 2) % 2 == xl)
    for i, flag in enumerate(flags):
        rows = slice(i * half, (i + 1) * half)
        choose(
            flag,
            sent,
            (slice(None), slice((1 + i) * per, (2 + i) * per)),
            lambda: own[rows].reshape(nz, per, slab),
            lambda: other[rows].reshape(nz, per, slab),
        )
    vals[...] = value_rows(here, own[2 * half :], other[2 * half :])


def halve(bit, total, vals, sent, rest):
    count, height, slab = total.shape
    total = total.reshape(count // 2, 2, height, slab)
    rows = count // 2 * height
    mine = (lax.axis_index("z") // bit) % 2
    for side in range(2):

        @pl.when(mine == side)
        def _():
            rest[...] = total[:, side]
            sent[0:rows] = total[:, 1 - side].astype(bf16).reshape(rows, slab)

    sent[rows:] = vals


def join(bit, owners, keep, got, vals):
    count, height, slab = keep.shape
    rows = count * height
    z = lax.axis_index("z")
    flags = [(owners[i] // 4 // bit) % 2 == (z // bit) % 2 for i in range(3)]
    total = keep[...] + got[0:rows].astype(f32).reshape(count, height, slab)
    return total, value_rows(flags, vals[...], got[rows:])


def factor_z(bit, owners, keep, got, vals, sent, rest, chosen):
    total, chosen[...] = join(bit // 2, owners, keep, got, vals)
    halve(bit, total, chosen[...], sent, rest)


def reduce_z(owners, got, keep, f_got, vals, sent, f_sent, f_rest):
    nz, height, _ = sent.shape
    per = height // 3
    xl = lax.axis_index("xl")
    total = got[0, 0:per].astype(f32)
    for k in range(1, nz):
        total = total + got[k, 0:per].astype(f32)
    parts = [total.astype(bf16)]
    for i, owner in enumerate((owners[0], owners[1 + xl])):
        parts.append(got[owner // 4, (1 + i) * per : (2 + i) * per])
    for i, part in enumerate(parts):
        for k in range(nz):
            sent[k, i * per : (i + 1) * per] = part
    halve(1, keep[...] + f_got[...].astype(f32), vals[...], f_sent, f_rest)


def factor_terms(cot, act, whole, sent, keep, flat, both):
    nz, _, height, slab = keep.shape
    group = height // 3
    tok, blocks, full = cot.shape
    nt = full // slab
    scale = 1.0 / (tok * nz * 4)
    core, t = lax.axis_index("c"), lax.axis_index("t")
    flat[...] = cot[...].reshape(tok, blocks * full)
    for j in range(blocks):
        own = flat[:, pl.ds(pl.multiple_of(j * full + t * slab, slab), slab)]
        both[j] = dot(flat[:, j * full : (j + 1) * full], own, ((0,), (0,))) * scale
    for k in range(nt):
        both[blocks, k * slab : (k + 1) * slab] = dot(whole[k], act[...], ((0,), (0,))) * scale
    for i in range(blocks + 1):
        term = both[i].reshape(nz, 2, 2, group, slab)
        rows = slice(i * group, (i + 1) * group)
        for c in range(2):

            @pl.when(core == c)
            def _():
                keep[:, :, rows] = term[:, :, c]

            @pl.when(core != c)
            def _():
                sent[:, :, rows] = term[:, :, c].astype(bf16)


def factor_core(keep, got, sent, rest):
    xl = lax.axis_index("xl")
    sent[...] = (keep[:, 1 - xl] + got[:, 1 - xl].astype(f32)).astype(bf16)
    rest[...] = keep[:, xl] + got[:, xl].astype(f32)


def pack_t(owners, got, keep, f_got, vals, sent, f_sent, f_rest, chosen):
    nz, height, slab = got.shape
    nt = sent.shape[0]
    per = height // 3
    half = nz * per
    piece = half // nt
    for k in range(nt):
        for i in range(2):
            rows = got[:, (1 + i) * per : (2 + i) * per].reshape(half, slab)
            sent[k, i * half : (i + 1) * half] = rows
    sent[:, 2 * half :] = got[:, 0:per].reshape(nt, piece, slab)
    factor_z(2, owners, keep, f_got, vals, f_sent, f_rest, chosen)


def factor_out(bit, owners, keep, got, vals, factor_a, factor_g, chosen):
    group = factor_a.shape[0]
    total, chosen[...] = join(bit, owners, keep, got, vals)
    for j in range(2):
        factor_g[j] = total[0, j * group : (j + 1) * group]
    factor_a[...] = total[0, 2 * group :]


def rotate(own, other, own_grad, other_grad, vals, sent, grad):
    nt, half, slab = own.shape
    piece = slab // 2
    core = lax.axis_index("c")
    mine = pl.multiple_of(core * piece, piece)
    theirs = pl.multiple_of((1 - core) * piece, piece)
    for k in range(nt):
        grad[pl.ds(mine, piece), k * slab : (k + 1) * slab] = own_grad[k]
        grad[pl.ds(theirs, piece), k * slab : (k + 1) * slab] = other_grad[k]
    near = grad[:, pl.ds(pl.multiple_of(core * half, half), half)]
    far = grad[:, pl.ds(pl.multiple_of((1 - core) * half, half), half)]
    for i in range(nt // 2):
        k = core * (nt // 2) + i
        turned = dot(near, own[k]) + dot(far, other[k])
        turned = turned.T.astype(bf16)
        sent[2 * i, 0:piece] = turned[0:piece]
        sent[2 * i + 1, 0:piece] = turned[piece:]
    for k in range(nt):
        sent[k, piece:] = vals[...]


def scale_rows(rows, own, other, sent, rot, scaled, column):
    nt, height, slab = rows.shape
    piece = height - VALS
    half = own.shape[1]
    core, xl, t = lax.axis_index("c"), lax.axis_index("xl"), lax.axis_index("t")
    row = rows[core * (nt // 2) + t // 2, piece:].astype(f32)[0:1]
    column[...] = jnp.broadcast_to(row, (slab, slab)).T
    la = column[pl.ds(pl.multiple_of((t % 2) * piece, piece), piece)]
    for k in range(nt):
        rot[:, k * slab : (k + 1) * slab] = rows[k, 0:piece]
    near = rot[:, pl.ds(pl.multiple_of(core * half, half), half)]
    far = rot[:, pl.ds(pl.multiple_of((1 - core) * half, half), half)]
    for k in range(nt):
        spectral = dot(near, own[k]) + dot(far, other[k])
        values = rows[k, piece:].astype(f32)
        lg = jnp.where(xl == 0, values[1:2], values[2:3])
        scaled[k] = (spectral / (la * lg + damping)).astype(bf16)
    for side, ref in ((core, own), (1 - core, other)):
        mixed = dot(scaled[0], ref[0], ((1,), (1,)))
        for k in range(1, nt):
            mixed = mixed + dot(scaled[k], ref[k], ((1,), (1,)))
        mixed = mixed.astype(bf16)
        for i in range(nt // 2):
            for copy in range(2):
                sent[copy, side * (nt // 2) + i] = mixed[:, i * slab : (i + 1) * slab]


def finish(groups, own, other, own_mixed, other_mixed, pre, worker):
    blocks, nt, piece, slab = own_mixed.shape
    half = own.shape[1]
    core = lax.axis_index("c")
    replica = (lax.axis_index("z") * 2 + lax.axis_index("xl")) * 2 + core
    group = groups[replica]
    for side, ref in ((core, own), (1 - core, other)):
        total = jnp.zeros((half, blocks * slab), f32)
        for part, mixed in ((core, own_mixed), (1 - core, other_mixed)):
            for i in range(nt // 4):
                k = part * (nt // 2) + 2 * i
                left = jnp.concatenate([ref[k], ref[k + 1]], 1)
                right = jnp.concatenate(
                    [mixed[j, 4 * i : 4 * i + 4].reshape(4 * piece, slab) for j in range(blocks)], 1
                )
                total = total + dot(left, right)
        total = total.astype(bf16)
        place = pl.ds(pl.multiple_of(side * half, half), half)
        pre[place] = total.reshape(half, blocks, slab)
        choose(
            group == 0,
            worker,
            (0, place),
            lambda: total[:, :slab],
            lambda: total[:, slab:],
        )


def input_grad(cot, weight, grad):
    tok, blocks, full = cot.shape
    left = cot[...].reshape(tok, blocks * full)
    right = weight[...].reshape(weight.shape[0], blocks * full)
    grad[...] = dot(left, right, ((1,), (1,))).astype(bf16)


def local(act, cot, weight, owners, worker_group, basis_a, values_a, basis_g, values_g):
    tok, slab = act.shape
    blocks, full = cot.shape[1:]
    nz, nt = lax.axis_size("z"), lax.axis_size("t")
    group = full // (nz * 4)
    half, piece = full // 2, slab // 2
    per = half // nz

    shape = (3 * half + VALS, slab)
    sent, keep, every = call(
        pack_bases,
        [out(shape), out(shape), out((nt, tok, slab))],
        [],
        [basis_a, basis_g, values_a, values_g, act],
        [pl.ANY, pl.ANY, None, None, None],
        scratch=[pltpu.SemaphoreType.DMA((2, 3))],
        limit=56,
    )
    got = swap(sent, "c")
    whole_act = exchange(every, "t")
    shape = (2 * half + VALS, slab)
    sent, base = call(select_core, [out(shape), out(shape)], [owners], [keep, got])
    base_got = swap(sent, "xl")

    flat = pltpu.VMEM((tok, blocks * full), bf16)
    shape = (blocks, half, slab)
    sent, keep = call(
        grad_terms,
        [out(shape), out(shape, f32)],
        [],
        [cot, act],
        scratch=[flat],
        flops=4 * tok * full * slab,
    )
    got = swap(sent, "c")
    sent, keep = call(add_core, [out(shape[1:]), out(shape[1:], f32)], [], [keep, got])
    got = swap(sent, "xl")

    sent, vals = call(
        pack_z,
        [out((nz, 3 * per, slab)), out((VALS, slab))],
        [owners],
        [keep, got, base, base_got],
    )
    got = exchange(follow(sent, whole_act, 56), "z")

    height = (blocks + 1) * group
    shape = (nz, 2, height, slab)
    sent, f_keep = call(
        factor_terms,
        [out(shape), out(shape, f32)],
        [],
        [cot, act, whole_act],
        scratch=[flat, pltpu.VMEM((blocks + 1, full, slab), f32)],
        flops=6 * tok * full * slab,
    )
    f_got = swap(sent, "c")
    shape = (nz, height, slab)
    sent, f_keep = call(factor_core, [out(shape), out(shape, f32)], [], [f_keep, f_got])
    f_got = swap(sent, "xl")

    def step_outs(count):
        return [out((count * height + VALS, slab)), out((count, height, slab), f32)]

    sent, f_sent, f_keep = call(
        reduce_z,
        [out((nz, 3 * per, slab))] + step_outs(nz // 2),
        [owners],
        [got, f_keep, f_got, vals],
    )
    got = exchange(sent, "z")
    f_got = across(f_sent, "z", 1)

    chosen = out((VALS, slab))
    sent, f_sent, f_keep, vals = call(
        pack_t,
        [out((nt, 2 * half + piece, slab))] + step_outs(nz // 4) + [chosen],
        [owners],
        [got, f_keep, f_got, vals],
    )
    own = exchange(sent, "t")
    f_got = across(f_sent, "z", 2)
    bit = 4
    while bit < nz:
        f_sent, f_keep, vals = call(
            functools.partial(factor_z, bit),
            step_outs(nz // 2 // bit) + [chosen],
            [owners],
            [f_keep, f_got, vals],
        )
        f_got = across(f_sent, "z", bit)
        bit *= 2
    factor_a, factor_g, vals = call(
        functools.partial(factor_out, nz // 2),
        [out((group, slab), f32), out((blocks, group, slab), f32), chosen],
        [owners],
        [f_keep, f_got, vals],
    )
    own = follow(own, factor_a, 20)
    other = swap(own, "c")
    qa, qa_other = (own, half, 0), (other, half, 0)
    qg, qg_other = (own, half, 1), (other, half, 1)
    columns, columns_other = (own, piece, 2 * half // piece), (other, piece, 2 * half // piece)
    (sent,) = call(
        rotate,
        [out((nt, piece + VALS, slab))],
        [],
        [qa, qa_other, columns, columns_other, vals],
        scratch=[pltpu.VMEM((slab, full), bf16)],
        flops=2 * slab * full * half,
    )
    rows = exchange(sent, "t")
    (sent,) = call(
        scale_rows,
        [out((blocks, nt, piece, slab))],
        [],
        [rows, qg, qg_other],
        scratch=[
            pltpu.VMEM((piece, full), bf16),
            pltpu.VMEM((nt, piece, slab), bf16),
            pltpu.VMEM((slab, slab), f32),
        ],
        flops=4 * piece * full * full,
    )
    own_mixed = exchange(sent.reshape(blocks * nt, piece, slab), ("xl", "t"))
    own_mixed = own_mixed.reshape(blocks, nt, piece, slab)
    other_mixed = swap(own_mixed, "c")
    pre, worker = call(
        finish,
        [out((full, blocks, slab)), out((1, full, slab))],
        [worker_group],
        [qa, qa_other, own_mixed, other_mixed],
        flops=4 * full * full * slab,
    )

    (grad_input,) = call(
        input_grad, [out((tok, slab))], [], [cot, weight], flops=4 * tok * full * slab
    )
    return grad_input, factor_a, factor_g.transpose(1, 0, 2), pre, worker


def solution(mesh):
    dp, tensor = mesh.devices.shape
    fine = Mesh(mesh.devices.reshape(dp // 4, 2, 2, tensor), ("z", "xl", "c", "t"))
    dp = ("z", "xl", "c")
    return jax.shard_map(
        local,
        mesh=fine,
        in_specs=(
            P(dp, "t"),
            P(dp, None, None),
            P("t", None, None),
            P(),
            P(),
            P(dp, None, "t"),
            P(dp, "t"),
            P(dp, None, None, "t"),
            P(dp, None, "t"),
        ),
        out_specs=(
            P(dp, "t"),
            P(dp, "t"),
            P(dp, None, "t"),
            P(None, None, "t"),
            P(dp, None, "t"),
        ),
        check_vma=False,
    )
```

```python
import functools

import jax
import jax.numpy as jnp
from jax import lax
from jax.experimental import pallas as pl
from jax.experimental.pallas import tpu as pltpu
from jax.sharding import Mesh, PartitionSpec as P

damping = 0.001
f32 = jnp.float32
bf16 = jnp.bfloat16
VALS = 16


def exchange(array, axis):
    return lax.all_to_all(array, axis, 0, 0, tiled=True)


def swap(array, axis):
    return lax.ppermute(array, axis, [(0, 1), (1, 0)])


def across(array, axis, step):
    pairs = [(i, i ^ step) for i in range(lax.axis_size(axis))]
    return lax.ppermute(array, axis, pairs)


def full_block(array):
    return pl.BlockSpec(array.shape, lambda i: (0,) * array.ndim)


def call(body, outs, scalars, args, places=None, scratch=(), flops=0, limit=20):
    specs, arrays = [], []
    for arg, place in zip(args, places or [None] * len(args)):
        if isinstance(arg, tuple):
            array, rows, block = arg
            shape = (array.shape[0], rows, array.shape[2])
            specs.append(pl.BlockSpec(shape, functools.partial(lambda k, i: (0, k, 0), block)))
        else:
            array = arg
            specs.append(pl.BlockSpec(memory_space=place) if place else full_block(array))
        arrays.append(array)
    bytes_all = sum(a.size * a.dtype.itemsize for a in arrays + list(outs))
    return pl.pallas_call(
        body,
        grid=(1,),
        out_shape=outs,
        in_specs=[pl.BlockSpec(memory_space=pltpu.SMEM)] * len(scalars) + specs,
        out_specs=[full_block(o) for o in outs],
        scratch_shapes=list(scratch),
        compiler_params=pltpu.CompilerParams(vmem_limit_bytes=limit * 1024 * 1024),
        cost_estimate=pl.CostEstimate(flops=flops, bytes_accessed=bytes_all, transcendentals=0),
    )(*scalars, *arrays)


def follow(array, after, limit):
    return pl.pallas_call(
        lambda *refs: None,
        out_shape=jax.ShapeDtypeStruct(array.shape, array.dtype),
        in_specs=[pl.BlockSpec(memory_space=pl.ANY)] * 2,
        out_specs=pl.BlockSpec(memory_space=pl.ANY),
        input_output_aliases={0: 0},
        compiler_params=pltpu.CompilerParams(vmem_limit_bytes=limit * 1024 * 1024),
    )(array, after)


def out(shape, dtype=bf16):
    return jax.ShapeDtypeStruct(shape, dtype)


def dot(left, right, dims=((1,), (0,))):
    return lax.dot_general(left, right, (dims, ((), ())), preferred_element_type=f32)


def value_rows(flags, own, other):
    place = lax.broadcasted_iota(jnp.int32, own.shape, 0)
    take = jnp.zeros(own.shape, jnp.int32)
    for row, flag in enumerate(flags):
        take = jnp.where(place == row, flag.astype(jnp.int32), take)
    return jnp.where(take > 0, own.astype(f32), other.astype(f32)).astype(bf16)


def choose(flag, ref, place, own, other):
    @pl.when(flag)
    def _():
        ref[place] = own()

    @pl.when(jnp.logical_not(flag))
    def _():
        ref[place] = other()


def pack_bases(ba, bg, va, vg, sent, keep, sem):
    half = ba.shape[1] // 2
    core = lax.axis_index("c")
    place = lax.broadcasted_iota(jnp.int32, (VALS, ba.shape[2]), 0)
    vals = jnp.where(place == 0, va[...].astype(f32), 0.0)
    for j in range(2):
        row = vg[0].astype(f32)[j : j + 1]
        vals = jnp.where(place == 1 + j, row, vals)
    copies = []
    for side, (ref, who) in enumerate(((sent, 1 - core), (keep, core))):
        rows = pl.ds(pl.multiple_of(who * half, half), half)
        for i in range(3):
            source = ba.at[0, rows] if i == 0 else bg.at[0, i - 1, rows]
            copies.append(
                pltpu.make_async_copy(source, ref.at[i * half : (i + 1) * half], sem.at[side, i])
            )
            copies[-1].start()
    sent[3 * half :] = vals.astype(bf16)
    keep[3 * half :] = vals.astype(bf16)
    for copy in copies:
        copy.wait()


def select_core(owners, own, got, sent, keep):
    half = (own.shape[0] - VALS) // 3
    core, xl = lax.axis_index("c"), lax.axis_index("xl")
    flags = [owners[i] % 2 == core for i in range(3)]

    def fill(ref, slot, i):
        start = pl.multiple_of(i * half, half)
        choose(
            owners[i] % 2 == core,
            ref,
            slice(slot * half, (slot + 1) * half),
            lambda: own[pl.ds(start, half)],
            lambda: got[pl.ds(start, half)],
        )

    vals = value_rows(flags, own[3 * half :], got[3 * half :])
    for ref, block in ((sent, 2 - xl), (keep, 1 + xl)):
        fill(ref, 0, 0)
        fill(ref, 1, block)
        ref[2 * half :] = vals


def grad_terms(cot, act, sent, keep, flat):
    blocks, half, slab = keep.shape
    tok, _, full = cot.shape
    nt = full // slab
    scale = 1.0 / (tok * lax.axis_size("z") * 4)
    core = lax.axis_index("c")
    flat[...] = cot[...].reshape(tok, blocks * full)
    for j in range(blocks):
        term = dot(flat[:, j * full : (j + 1) * full], act[...], ((0,), (0,))) * scale
        term = term.reshape(nt, 2, slab // 2, slab)
        for c in range(2):
            part = term[:, c].reshape(half, slab)

            @pl.when(core == c)
            def _():
                keep[j] = part

            @pl.when(core != c)
            def _():
                sent[j] = part.astype(bf16)


def add_core(keep, got, sent, rest):
    xl = lax.axis_index("xl")
    sent[...] = (keep[1 - xl] + got[1 - xl].astype(f32)).astype(bf16)
    rest[...] = keep[xl] + got[xl].astype(f32)


def pack_z(owners, keep, got, own, other, sent, vals):
    nz, _, slab = sent.shape
    half = (own.shape[0] - VALS) // 2
    per = half // nz
    xl = lax.axis_index("xl")
    total = (keep[...] + got[...].astype(f32)).astype(bf16)
    sent[:, 0:per] = total.reshape(nz, per, slab)
    here = [(owners[i] // 2) % 2 == xl for i in range(3)]
    flags = (here[0], (owners[1 + xl] // 2) % 2 == xl)
    for i, flag in enumerate(flags):
        rows = slice(i * half, (i + 1) * half)
        choose(
            flag,
            sent,
            (slice(None), slice((1 + i) * per, (2 + i) * per)),
            lambda: own[rows].reshape(nz, per, slab),
            lambda: other[rows].reshape(nz, per, slab),
        )
    vals[...] = value_rows(here, own[2 * half :], other[2 * half :])


def halve(bit, total, vals, sent, rest):
    count, height, slab = total.shape
    total = total.reshape(count // 2, 2, height, slab)
    rows = count // 2 * height
    mine = (lax.axis_index("z") // bit) % 2
    for side in range(2):

        @pl.when(mine == side)
        def _():
            rest[...] = total[:, side]
            sent[0:rows] = total[:, 1 - side].astype(bf16).reshape(rows, slab)

    sent[rows:] = vals


def join(bit, owners, keep, got, vals):
    count, height, slab = keep.shape
    rows = count * height
    z = lax.axis_index("z")
    flags = [(owners[i] // 4 // bit) % 2 == (z // bit) % 2 for i in range(3)]
    total = keep[...] + got[0:rows].astype(f32).reshape(count, height, slab)
    return total, value_rows(flags, vals[...], got[rows:])


def factor_z(bit, owners, keep, got, vals, sent, rest, chosen):
    total, chosen[...] = join(bit // 2, owners, keep, got, vals)
    halve(bit, total, chosen[...], sent, rest)


def reduce_z(owners, got, after, sent):
    nz, height, _ = sent.shape
    per = height // 3
    xl = lax.axis_index("xl")
    total = got[0, 0:per].astype(f32)
    for k in range(1, nz):
        total = total + got[k, 0:per].astype(f32)
    parts = [total.astype(bf16)]
    for i, owner in enumerate((owners[0], owners[1 + xl])):
        parts.append(got[owner // 4, (1 + i) * per : (2 + i) * per])
    for i, part in enumerate(parts):
        for k in range(nz):
            sent[k, i * per : (i + 1) * per] = part


def factor_first(keep, got, vals, sent, rest):
    halve(1, keep[...] + got[...].astype(f32), vals[...], sent, rest)


def factor_terms(cot, *refs):
    pieces, (sent, keep, flat, both) = refs[:-4], refs[-4:]
    act = pieces[0]
    nz, _, height, slab = keep.shape
    group = height // 3
    tok, blocks, full = cot.shape
    nt = full // slab
    scale = 1.0 / (tok * nz * 4)
    core, t = lax.axis_index("c"), lax.axis_index("t")
    flat[...] = cot[...].reshape(tok, blocks * full)
    for j in range(blocks):
        own = flat[:, pl.ds(pl.multiple_of(j * full + t * slab, slab), slab)]
        both[j] = dot(flat[:, j * full : (j + 1) * full], own, ((0,), (0,))) * scale
    for k, piece in enumerate(pieces):
        rows = pl.ds(pl.multiple_of((t ^ k) * slab, slab), slab)
        both[blocks, rows] = dot(piece[...], act[...], ((0,), (0,))) * scale
    for i in range(blocks + 1):
        term = both[i].reshape(nz, 2, 2, group, slab)
        rows = slice(i * group, (i + 1) * group)
        for c in range(2):

            @pl.when(core == c)
            def _():
                keep[:, :, rows] = term[:, :, c]

            @pl.when(core != c)
            def _():
                sent[:, :, rows] = term[:, :, c].astype(bf16)


def factor_core(keep, got, sent, rest):
    xl = lax.axis_index("xl")
    sent[...] = (keep[:, 1 - xl] + got[:, 1 - xl].astype(f32)).astype(bf16)
    rest[...] = keep[:, xl] + got[:, xl].astype(f32)


def pack_t(owners, got, keep, f_got, vals, sent, f_sent, f_rest, chosen):
    nz, height, slab = got.shape
    nt = sent.shape[0]
    per = height // 3
    half = nz * per
    piece = half // nt
    for k in range(nt):
        for i in range(2):
            rows = got[:, (1 + i) * per : (2 + i) * per].reshape(half, slab)
            sent[k, i * half : (i + 1) * half] = rows
    sent[:, 2 * half :] = got[:, 0:per].reshape(nt, piece, slab)
    factor_z(2, owners, keep, f_got, vals, f_sent, f_rest, chosen)


def factor_out(bit, owners, keep, got, vals, factor_a, factor_g, chosen):
    group = factor_a.shape[0]
    total, chosen[...] = join(bit, owners, keep, got, vals)
    for j in range(2):
        factor_g[j] = total[0, j * group : (j + 1) * group]
    factor_a[...] = total[0, 2 * group :]


def rotate(own, other, own_grad, other_grad, vals, sent, grad):
    nt, half, slab = own.shape
    piece = slab // 2
    core = lax.axis_index("c")
    mine = pl.multiple_of(core * piece, piece)
    theirs = pl.multiple_of((1 - core) * piece, piece)
    for k in range(nt):
        grad[pl.ds(mine, piece), k * slab : (k + 1) * slab] = own_grad[k]
        grad[pl.ds(theirs, piece), k * slab : (k + 1) * slab] = other_grad[k]
    near = grad[:, pl.ds(pl.multiple_of(core * half, half), half)]
    far = grad[:, pl.ds(pl.multiple_of((1 - core) * half, half), half)]
    for i in range(nt // 2):
        k = core * (nt // 2) + i
        turned = dot(near, own[k]) + dot(far, other[k])
        turned = turned.T.astype(bf16)
        sent[2 * i, 0:piece] = turned[0:piece]
        sent[2 * i + 1, 0:piece] = turned[piece:]
    for k in range(nt):
        sent[k, piece:] = vals[...]


def scale_rows(rows, own, other, sent, rot, scaled, column):
    nt, height, slab = rows.shape
    piece = height - VALS
    half = own.shape[1]
    core, xl, t = lax.axis_index("c"), lax.axis_index("xl"), lax.axis_index("t")
    row = rows[core * (nt // 2) + t // 2, piece:].astype(f32)[0:1]
    column[...] = jnp.broadcast_to(row, (slab, slab)).T
    la = column[pl.ds(pl.multiple_of((t % 2) * piece, piece), piece)]
    for k in range(nt):
        rot[:, k * slab : (k + 1) * slab] = rows[k, 0:piece]
    near = rot[:, pl.ds(pl.multiple_of(core * half, half), half)]
    far = rot[:, pl.ds(pl.multiple_of((1 - core) * half, half), half)]
    for k in range(nt):
        spectral = dot(near, own[k]) + dot(far, other[k])
        values = rows[k, piece:].astype(f32)
        lg = jnp.where(xl == 0, values[1:2], values[2:3])
        scaled[k] = (spectral / (la * lg + damping)).astype(bf16)
    for side, ref in ((core, own), (1 - core, other)):
        mixed = dot(scaled[0], ref[0], ((1,), (1,)))
        for k in range(1, nt):
            mixed = mixed + dot(scaled[k], ref[k], ((1,), (1,)))
        mixed = mixed.astype(bf16)
        for i in range(nt // 2):
            for copy in range(2):
                sent[copy, side * (nt // 2) + i] = mixed[:, i * slab : (i + 1) * slab]


def finish(groups, own, other, own_mixed, other_mixed, pre, worker):
    blocks, nt, piece, slab = own_mixed.shape
    half = own.shape[1]
    core = lax.axis_index("c")
    replica = (lax.axis_index("z") * 2 + lax.axis_index("xl")) * 2 + core
    group = groups[replica]
    for side, ref in ((core, own), (1 - core, other)):
        total = jnp.zeros((half, blocks * slab), f32)
        for part, mixed in ((core, own_mixed), (1 - core, other_mixed)):
            for i in range(nt // 4):
                k = part * (nt // 2) + 2 * i
                left = jnp.concatenate([ref[k], ref[k + 1]], 1)
                right = jnp.concatenate(
                    [mixed[j, 4 * i : 4 * i + 4].reshape(4 * piece, slab) for j in range(blocks)], 1
                )
                total = total + dot(left, right)
        total = total.astype(bf16)
        place = pl.ds(pl.multiple_of(side * half, half), half)
        pre[place] = total.reshape(half, blocks, slab)
        choose(
            group == 0,
            worker,
            (0, place),
            lambda: total[:, :slab],
            lambda: total[:, slab:],
        )


def input_grad(cot, weight, grad):
    tok, blocks, full = cot.shape
    left = cot[...].reshape(tok, blocks * full)
    right = weight[...].reshape(weight.shape[0], blocks * full)
    grad[...] = dot(left, right, ((1,), (1,))).astype(bf16)


def local(act, cot, weight, owners, worker_group, basis_a, values_a, basis_g, values_g):
    tok, slab = act.shape
    blocks, full = cot.shape[1:]
    nz, nt = lax.axis_size("z"), lax.axis_size("t")
    group = full // (nz * 4)
    half, piece = full // 2, slab // 2
    per = half // nz

    shape = (3 * half + VALS, slab)
    sent, keep = call(
        pack_bases,
        [out(shape), out(shape)],
        [],
        [basis_a, basis_g, values_a, values_g],
        [pl.ANY, pl.ANY, None, None],
        scratch=[pltpu.SemaphoreType.DMA((2, 3))],
        limit=56,
    )
    got = swap(sent, "c")
    shape = (2 * half + VALS, slab)
    sent, base = call(select_core, [out(shape), out(shape)], [owners], [keep, got])
    base_got = swap(sent, "xl")

    flat = pltpu.VMEM((tok, blocks * full), bf16)
    shape = (blocks, half, slab)
    sent, keep = call(
        grad_terms,
        [out(shape), out(shape, f32)],
        [],
        [cot, act],
        scratch=[flat],
        flops=4 * tok * full * slab,
    )
    got = swap(sent, "c")
    sent, keep = call(add_core, [out(shape[1:]), out(shape[1:], f32)], [], [keep, got])
    got = swap(sent, "xl")

    sent, vals = call(
        pack_z,
        [out((nz, 3 * per, slab)), out((VALS, slab))],
        [owners],
        [keep, got, base, base_got],
    )
    got = exchange(sent, "z")

    height = (blocks + 1) * group
    shape = (nz, 2, height, slab)
    pieces = [act] + [across(act, "t", k) for k in range(1, nt)]
    sent_f, f_keep = call(
        factor_terms,
        [out(shape), out(shape, f32)],
        [],
        [cot] + pieces,
        scratch=[flat, pltpu.VMEM((blocks + 1, full, slab), f32)],
        flops=6 * tok * full * slab,
    )

    def step_outs(count):
        return [out((count * height + VALS, slab)), out((count, height, slab), f32)]

    (sent,) = call(
        reduce_z,
        [out((nz, 3 * per, slab))],
        [owners],
        [got, sent_f],
        [None, pl.ANY],
    )
    got = exchange(sent, "z")
    f_got = swap(sent_f, "c")
    shape = (nz, height, slab)
    f_sent, f_keep = call(factor_core, [out(shape), out(shape, f32)], [], [f_keep, f_got])
    f_got = swap(f_sent, "xl")
    f_sent, f_keep = call(factor_first, step_outs(nz // 2), [], [f_keep, f_got, vals])
    f_got = across(f_sent, "z", 1)

    chosen = out((VALS, slab))
    sent, f_sent, f_keep, vals = call(
        pack_t,
        [out((nt, 2 * half + piece, slab))] + step_outs(nz // 4) + [chosen],
        [owners],
        [got, f_keep, f_got, vals],
    )
    own = exchange(sent, "t")
    f_got = across(f_sent, "z", 2)
    bit = 4
    while bit < nz:
        f_sent, f_keep, vals = call(
            functools.partial(factor_z, bit),
            step_outs(nz // 2 // bit) + [chosen],
            [owners],
            [f_keep, f_got, vals],
        )
        f_got = across(f_sent, "z", bit)
        bit *= 2
    factor_a, factor_g, vals = call(
        functools.partial(factor_out, nz // 2),
        [out((group, slab), f32), out((blocks, group, slab), f32), chosen],
        [owners],
        [f_keep, f_got, vals],
    )
    own = follow(own, factor_a, 20)
    other = swap(own, "c")
    qa, qa_other = (own, half, 0), (other, half, 0)
    qg, qg_other = (own, half, 1), (other, half, 1)
    columns, columns_other = (own, piece, 2 * half // piece), (other, piece, 2 * half // piece)
    (sent,) = call(
        rotate,
        [out((nt, piece + VALS, slab))],
        [],
        [qa, qa_other, columns, columns_other, vals],
        scratch=[pltpu.VMEM((slab, full), bf16)],
        flops=2 * slab * full * half,
    )
    rows = exchange(sent, "t")
    (sent,) = call(
        scale_rows,
        [out((blocks, nt, piece, slab))],
        [],
        [rows, qg, qg_other],
        scratch=[
            pltpu.VMEM((piece, full), bf16),
            pltpu.VMEM((nt, piece, slab), bf16),
            pltpu.VMEM((slab, slab), f32),
        ],
        flops=4 * piece * full * full,
    )
    own_mixed = exchange(sent.reshape(blocks * nt, piece, slab), ("xl", "t"))
    own_mixed = own_mixed.reshape(blocks, nt, piece, slab)
    other_mixed = swap(own_mixed, "c")
    pre, worker = call(
        finish,
        [out((full, blocks, slab)), out((1, full, slab))],
        [worker_group],
        [qa, qa_other, own_mixed, other_mixed],
        flops=4 * full * full * slab,
    )

    (grad_input,) = call(
        input_grad, [out((tok, slab))], [], [cot, weight], flops=4 * tok * full * slab
    )
    return grad_input, factor_a, factor_g.transpose(1, 0, 2), pre, worker


def solution(mesh):
    dp, tensor = mesh.devices.shape
    fine = Mesh(mesh.devices.reshape(dp // 4, 2, 2, tensor), ("z", "xl", "c", "t"))
    dp = ("z", "xl", "c")
    return jax.shard_map(
        local,
        mesh=fine,
        in_specs=(
            P(dp, "t"),
            P(dp, None, None),
            P("t", None, None),
            P(),
            P(),
            P(dp, None, "t"),
            P(dp, "t"),
            P(dp, None, None, "t"),
            P(dp, None, "t"),
        ),
        out_specs=(
            P(dp, "t"),
            P(dp, "t"),
            P(dp, None, "t"),
            P(None, None, "t"),
            P(dp, None, "t"),
        ),
        check_vma=False,
    )
```

```python
import functools

import jax
import jax.numpy as jnp
from jax import lax
from jax.experimental import pallas as pl
from jax.experimental.pallas import tpu as pltpu
from jax.sharding import Mesh, PartitionSpec as P

damping = 0.001
f32 = jnp.float32
bf16 = jnp.bfloat16
VALS = 16


def exchange(array, axis):
    return lax.all_to_all(array, axis, 0, 0, tiled=True)


def swap(array, axis):
    return lax.ppermute(array, axis, [(0, 1), (1, 0)])


def across(array, axis, step):
    pairs = [(i, i ^ step) for i in range(lax.axis_size(axis))]
    return lax.ppermute(array, axis, pairs)


def full_block(array):
    return pl.BlockSpec(array.shape, lambda i: (0,) * array.ndim)


def call(body, outs, scalars, args, places=None, scratch=(), flops=0, limit=20):
    specs, arrays = [], []
    for arg, place in zip(args, places or [None] * len(args)):
        if isinstance(arg, tuple):
            array, rows, block = arg
            shape = (array.shape[0], rows, array.shape[2])
            specs.append(pl.BlockSpec(shape, functools.partial(lambda k, i: (0, k, 0), block)))
        else:
            array = arg
            specs.append(pl.BlockSpec(memory_space=place) if place else full_block(array))
        arrays.append(array)
    bytes_all = sum(a.size * a.dtype.itemsize for a in arrays + list(outs))
    return pl.pallas_call(
        body,
        grid=(1,),
        out_shape=outs,
        in_specs=[pl.BlockSpec(memory_space=pltpu.SMEM)] * len(scalars) + specs,
        out_specs=[full_block(o) for o in outs],
        scratch_shapes=list(scratch),
        compiler_params=pltpu.CompilerParams(vmem_limit_bytes=limit * 1024 * 1024),
        cost_estimate=pl.CostEstimate(flops=flops, bytes_accessed=bytes_all, transcendentals=0),
    )(*scalars, *arrays)


def follow(array, after, limit):
    return pl.pallas_call(
        lambda *refs: None,
        out_shape=jax.ShapeDtypeStruct(array.shape, array.dtype),
        in_specs=[pl.BlockSpec(memory_space=pl.ANY)] * 2,
        out_specs=pl.BlockSpec(memory_space=pl.ANY),
        input_output_aliases={0: 0},
        compiler_params=pltpu.CompilerParams(vmem_limit_bytes=limit * 1024 * 1024),
    )(array, after)


def out(shape, dtype=bf16):
    return jax.ShapeDtypeStruct(shape, dtype)


def dot(left, right, dims=((1,), (0,))):
    return lax.dot_general(left, right, (dims, ((), ())), preferred_element_type=f32)


def value_rows(flags, own, other):
    place = lax.broadcasted_iota(jnp.int32, own.shape, 0)
    take = jnp.zeros(own.shape, jnp.int32)
    for row, flag in enumerate(flags):
        take = jnp.where(place == row, flag.astype(jnp.int32), take)
    return jnp.where(take > 0, own.astype(f32), other.astype(f32)).astype(bf16)


def choose(flag, ref, place, own, other):
    @pl.when(flag)
    def _():
        ref[place] = own()

    @pl.when(jnp.logical_not(flag))
    def _():
        ref[place] = other()


def pack_bases(ba, bg, va, vg, act, sent, keep, every, sem):
    half = ba.shape[1] // 2
    core = lax.axis_index("c")
    place = lax.broadcasted_iota(jnp.int32, (VALS, ba.shape[2]), 0)
    vals = jnp.where(place == 0, va[...].astype(f32), 0.0)
    for j in range(2):
        row = vg[0].astype(f32)[j : j + 1]
        vals = jnp.where(place == 1 + j, row, vals)
    copies = []
    for side, (ref, who) in enumerate(((sent, 1 - core), (keep, core))):
        rows = pl.ds(pl.multiple_of(who * half, half), half)
        for i in range(3):
            source = ba.at[0, rows] if i == 0 else bg.at[0, i - 1, rows]
            copies.append(
                pltpu.make_async_copy(source, ref.at[i * half : (i + 1) * half], sem.at[side, i])
            )
            copies[-1].start()
    sent[3 * half :] = vals.astype(bf16)
    keep[3 * half :] = vals.astype(bf16)
    for k in range(every.shape[0]):
        every[k] = act[...]
    for copy in copies:
        copy.wait()


def select_core(owners, own, got, sent, keep):
    half = (own.shape[0] - VALS) // 3
    core, xl = lax.axis_index("c"), lax.axis_index("xl")
    flags = [owners[i] % 2 == core for i in range(3)]

    def fill(ref, slot, i):
        start = pl.multiple_of(i * half, half)
        choose(
            owners[i] % 2 == core,
            ref,
            slice(slot * half, (slot + 1) * half),
            lambda: own[pl.ds(start, half)],
            lambda: got[pl.ds(start, half)],
        )

    vals = value_rows(flags, own[3 * half :], got[3 * half :])
    for ref, block in ((sent, 2 - xl), (keep, 1 + xl)):
        fill(ref, 0, 0)
        fill(ref, 1, block)
        ref[2 * half :] = vals


def grad_terms(cot, act, sent, keep, flat):
    blocks, half, slab = keep.shape
    tok, _, full = cot.shape
    nt = full // slab
    scale = 1.0 / (tok * lax.axis_size("z") * 4)
    core = lax.axis_index("c")
    flat[...] = cot[...].reshape(tok, blocks * full)
    for j in range(blocks):
        term = dot(flat[:, j * full : (j + 1) * full], act[...], ((0,), (0,))) * scale
        term = term.reshape(nt, 2, slab // 2, slab)
        for c in range(2):
            part = term[:, c].reshape(half, slab)

            @pl.when(core == c)
            def _():
                keep[j] = part

            @pl.when(core != c)
            def _():
                sent[j] = part.astype(bf16)


def add_core(keep, got, sent, rest):
    xl = lax.axis_index("xl")
    sent[...] = (keep[1 - xl] + got[1 - xl].astype(f32)).astype(bf16)
    rest[...] = keep[xl] + got[xl].astype(f32)


def pack_z(owners, keep, got, own, other, sent, vals):
    nz, _, slab = sent.shape
    half = (own.shape[0] - VALS) // 2
    per = half // nz
    xl = lax.axis_index("xl")
    total = (keep[...] + got[...].astype(f32)).astype(bf16)
    sent[:, 0:per] = total.reshape(nz, per, slab)
    here = [(owners[i] // 2) % 2 == xl for i in range(3)]
    flags = (here[0], (owners[1 + xl] // 2) % 2 == xl)
    for i, flag in enumerate(flags):
        rows = slice(i * half, (i + 1) * half)
        choose(
            flag,
            sent,
            (slice(None), slice((1 + i) * per, (2 + i) * per)),
            lambda: own[rows].reshape(nz, per, slab),
            lambda: other[rows].reshape(nz, per, slab),
        )
    vals[...] = value_rows(here, own[2 * half :], other[2 * half :])


def halve(bit, total, vals, sent, rest):
    count, height, slab = total.shape
    total = total.reshape(count // 2, 2, height, slab)
    rows = count // 2 * height
    mine = (lax.axis_index("z") // bit) % 2
    for side in range(2):

        @pl.when(mine == side)
        def _():
            rest[...] = total[:, side]
            sent[0:rows] = total[:, 1 - side].astype(bf16).reshape(rows, slab)

    sent[rows:] = vals


def join(bit, owners, keep, got, vals):
    count, height, slab = keep.shape
    rows = count * height
    z = lax.axis_index("z")
    flags = [(owners[i] // 4 // bit) % 2 == (z // bit) % 2 for i in range(3)]
    total = keep[...] + got[0:rows].astype(f32).reshape(count, height, slab)
    return total, value_rows(flags, vals[...], got[rows:])


def factor_z(bit, owners, keep, got, vals, sent, rest, chosen):
    total, chosen[...] = join(bit // 2, owners, keep, got, vals)
    halve(bit, total, chosen[...], sent, rest)


def factor_first(keep, got, vals, sent, rest):
    halve(1, keep[...] + got[...].astype(f32), vals[...], sent, rest)


def reduce_z(owners, got, keep, f_got, vals, sent, f_sent, f_rest, chosen):
    nz, height, _ = sent.shape
    per = height // 3
    xl = lax.axis_index("xl")
    total = got[0, 0:per].astype(f32)
    for k in range(1, nz):
        total = total + got[k, 0:per].astype(f32)
    parts = [total.astype(bf16)]
    for i, owner in enumerate((owners[0], owners[1 + xl])):
        parts.append(got[owner // 4, (1 + i) * per : (2 + i) * per])
    for i, part in enumerate(parts):
        for k in range(nz):
            sent[k, i * per : (i + 1) * per] = part
    factor_z(2, owners, keep, f_got, vals, f_sent, f_rest, chosen)


def factor_terms(cot, act, whole, sent, keep, flat, both):
    nz, _, height, slab = keep.shape
    group = height // 3
    tok, blocks, full = cot.shape
    nt = full // slab
    scale = 1.0 / (tok * nz * 4)
    core, t = lax.axis_index("c"), lax.axis_index("t")
    flat[...] = cot[...].reshape(tok, blocks * full)
    for j in range(blocks):
        own = flat[:, pl.ds(pl.multiple_of(j * full + t * slab, slab), slab)]
        both[j] = dot(flat[:, j * full : (j + 1) * full], own, ((0,), (0,))) * scale
    for k in range(nt):
        both[blocks, k * slab : (k + 1) * slab] = dot(whole[k], act[...], ((0,), (0,))) * scale
    for i in range(blocks + 1):
        term = both[i].reshape(nz, 2, 2, group, slab)
        rows = slice(i * group, (i + 1) * group)
        for c in range(2):

            @pl.when(core == c)
            def _():
                keep[:, :, rows] = term[:, :, c]

            @pl.when(core != c)
            def _():
                sent[:, :, rows] = term[:, :, c].astype(bf16)


def factor_core(keep, got, sent, rest):
    xl = lax.axis_index("xl")
    sent[...] = (keep[:, 1 - xl] + got[:, 1 - xl].astype(f32)).astype(bf16)
    rest[...] = keep[:, xl] + got[:, xl].astype(f32)


def pack_t(owners, got, keep, f_got, vals, sent, f_sent, f_rest, chosen):
    nz, height, slab = got.shape
    nt = sent.shape[0]
    per = height // 3
    half = nz * per
    piece = half // nt
    for k in range(nt):
        for i in range(2):
            rows = got[:, (1 + i) * per : (2 + i) * per].reshape(half, slab)
            sent[k, i * half : (i + 1) * half] = rows
    sent[:, 2 * half :] = got[:, 0:per].reshape(nt, piece, slab)
    factor_z(4, owners, keep, f_got, vals, f_sent, f_rest, chosen)


def factor_out(bit, owners, keep, got, vals, factor_a, factor_g, chosen):
    group = factor_a.shape[0]
    total, chosen[...] = join(bit, owners, keep, got, vals)
    for j in range(2):
        factor_g[j] = total[0, j * group : (j + 1) * group]
    factor_a[...] = total[0, 2 * group :]


def rotate(own, other, own_grad, other_grad, vals, sent, grad):
    nt, half, slab = own.shape
    piece = slab // 2
    core = lax.axis_index("c")
    mine = pl.multiple_of(core * piece, piece)
    theirs = pl.multiple_of((1 - core) * piece, piece)
    for k in range(nt):
        grad[pl.ds(mine, piece), k * slab : (k + 1) * slab] = own_grad[k]
        grad[pl.ds(theirs, piece), k * slab : (k + 1) * slab] = other_grad[k]
    near = grad[:, pl.ds(pl.multiple_of(core * half, half), half)]
    far = grad[:, pl.ds(pl.multiple_of((1 - core) * half, half), half)]
    for i in range(nt // 2):
        k = core * (nt // 2) + i
        turned = dot(near, own[k]) + dot(far, other[k])
        turned = turned.T.astype(bf16)
        sent[2 * i, 0:piece] = turned[0:piece]
        sent[2 * i + 1, 0:piece] = turned[piece:]
    for k in range(nt):
        sent[k, piece:] = vals[...]


def scale_rows(rows, own, other, sent, rot, scaled, column):
    nt, height, slab = rows.shape
    piece = height - VALS
    half = own.shape[1]
    core, xl, t = lax.axis_index("c"), lax.axis_index("xl"), lax.axis_index("t")
    row = rows[core * (nt // 2) + t // 2, piece:].astype(f32)[0:1]
    column[...] = jnp.broadcast_to(row, (slab, slab)).T
    la = column[pl.ds(pl.multiple_of((t % 2) * piece, piece), piece)]
    for k in range(nt):
        rot[:, k * slab : (k + 1) * slab] = rows[k, 0:piece]
    near = rot[:, pl.ds(pl.multiple_of(core * half, half), half)]
    far = rot[:, pl.ds(pl.multiple_of((1 - core) * half, half), half)]
    for k in range(nt):
        spectral = dot(near, own[k]) + dot(far, other[k])
        values = rows[k, piece:].astype(f32)
        lg = jnp.where(xl == 0, values[1:2], values[2:3])
        scaled[k] = (spectral / (la * lg + damping)).astype(bf16)
    for side, ref in ((core, own), (1 - core, other)):
        mixed = dot(scaled[0], ref[0], ((1,), (1,)))
        for k in range(1, nt):
            mixed = mixed + dot(scaled[k], ref[k], ((1,), (1,)))
        mixed = mixed.astype(bf16)
        for i in range(nt // 2):
            for copy in range(2):
                sent[copy, side * (nt // 2) + i] = mixed[:, i * slab : (i + 1) * slab]


def finish(groups, own, other, own_mixed, other_mixed, pre, worker):
    blocks, nt, piece, slab = own_mixed.shape
    half = own.shape[1]
    core = lax.axis_index("c")
    replica = (lax.axis_index("z") * 2 + lax.axis_index("xl")) * 2 + core
    group = groups[replica]
    for side, ref in ((core, own), (1 - core, other)):
        total = jnp.zeros((half, blocks * slab), f32)
        for part, mixed in ((core, own_mixed), (1 - core, other_mixed)):
            for i in range(nt // 4):
                k = part * (nt // 2) + 2 * i
                left = jnp.concatenate([ref[k], ref[k + 1]], 1)
                right = jnp.concatenate(
                    [mixed[j, 4 * i : 4 * i + 4].reshape(4 * piece, slab) for j in range(blocks)], 1
                )
                total = total + dot(left, right)
        total = total.astype(bf16)
        place = pl.ds(pl.multiple_of(side * half, half), half)
        pre[place] = total.reshape(half, blocks, slab)
        choose(
            group == 0,
            worker,
            (0, place),
            lambda: total[:, :slab],
            lambda: total[:, slab:],
        )


def input_grad(cot, weight, grad):
    tok, blocks, full = cot.shape
    left = cot[...].reshape(tok, blocks * full)
    right = weight[...].reshape(weight.shape[0], blocks * full)
    grad[...] = dot(left, right, ((1,), (1,))).astype(bf16)


def local(act, cot, weight, owners, worker_group, basis_a, values_a, basis_g, values_g):
    tok, slab = act.shape
    blocks, full = cot.shape[1:]
    nz, nt = lax.axis_size("z"), lax.axis_size("t")
    group = full // (nz * 4)
    half, piece = full // 2, slab // 2
    per = half // nz

    shape = (3 * half + VALS, slab)
    sent, keep, every = call(
        pack_bases,
        [out(shape), out(shape), out((nt, tok, slab))],
        [],
        [basis_a, basis_g, values_a, values_g, act],
        [pl.ANY, pl.ANY, None, None, None],
        scratch=[pltpu.SemaphoreType.DMA((2, 3))],
        limit=56,
    )
    got = swap(sent, "c")
    whole_act = exchange(every, "t")
    shape = (2 * half + VALS, slab)
    sent, base = call(select_core, [out(shape), out(shape)], [owners], [keep, got])
    base_got = swap(sent, "xl")

    flat = pltpu.VMEM((tok, blocks * full), bf16)
    shape = (blocks, half, slab)
    sent, keep = call(
        grad_terms,
        [out(shape), out(shape, f32)],
        [],
        [cot, act],
        scratch=[flat],
        flops=4 * tok * full * slab,
    )
    got = swap(sent, "c")
    sent, keep = call(add_core, [out(shape[1:]), out(shape[1:], f32)], [], [keep, got])
    got = swap(sent, "xl")

    sent, vals = call(
        pack_z,
        [out((nz, 3 * per, slab)), out((VALS, slab))],
        [owners],
        [keep, got, base, base_got],
    )
    got = exchange(follow(sent, whole_act, 56), "z")

    height = (blocks + 1) * group
    shape = (nz, 2, height, slab)
    sent, f_keep = call(
        factor_terms,
        [out(shape), out(shape, f32)],
        [],
        [cot, act, whole_act],
        scratch=[flat, pltpu.VMEM((blocks + 1, full, slab), f32)],
        flops=6 * tok * full * slab,
    )
    f_got = swap(sent, "c")
    shape = (nz, height, slab)
    sent, f_keep = call(factor_core, [out(shape), out(shape, f32)], [], [f_keep, f_got])
    f_got = swap(sent, "xl")

    def step_outs(count):
        return [out((count * height + VALS, slab)), out((count, height, slab), f32)]

    f_sent, f_keep = call(factor_first, step_outs(nz // 2), [], [f_keep, f_got, vals])
    f_got = across(f_sent, "z", 1)

    chosen = out((VALS, slab))
    sent, f_sent, f_keep, vals = call(
        reduce_z,
        [out((nz, 3 * per, slab))] + step_outs(nz // 4) + [chosen],
        [owners],
        [got, f_keep, f_got, vals],
    )
    got = exchange(sent, "z")
    f_got = across(f_sent, "z", 2)

    sent, f_sent, f_keep, vals = call(
        pack_t,
        [out((nt, 2 * half + piece, slab))] + step_outs(nz // 8) + [chosen],
        [owners],
        [got, f_keep, f_got, vals],
    )
    own = exchange(sent, "t")
    f_got = across(f_sent, "z", 4)
    f_sent, f_keep, vals = call(
        functools.partial(factor_z, 8),
        step_outs(nz // 16) + [chosen],
        [owners],
        [f_keep, f_got, vals],
    )
    f_got = across(f_sent, "z", 8)
    factor_a, factor_g, vals = call(
        functools.partial(factor_out, nz // 2),
        [out((group, slab), f32), out((blocks, group, slab), f32), chosen],
        [owners],
        [f_keep, f_got, vals],
    )
    own = follow(own, vals, 20)
    other = swap(own, "c")
    qa, qa_other = (own, half, 0), (other, half, 0)
    qg, qg_other = (own, half, 1), (other, half, 1)
    columns, columns_other = (own, piece, 2 * half // piece), (other, piece, 2 * half // piece)
    (sent,) = call(
        rotate,
        [out((nt, piece + VALS, slab))],
        [],
        [qa, qa_other, columns, columns_other, vals],
        scratch=[pltpu.VMEM((slab, full), bf16)],
        flops=2 * slab * full * half,
    )
    rows = exchange(sent, "t")
    (sent,) = call(
        scale_rows,
        [out((blocks, nt, piece, slab))],
        [],
        [rows, qg, qg_other],
        scratch=[
            pltpu.VMEM((piece, full), bf16),
            pltpu.VMEM((nt, piece, slab), bf16),
            pltpu.VMEM((slab, slab), f32),
        ],
        flops=4 * piece * full * full,
    )
    own_mixed = exchange(sent.reshape(blocks * nt, piece, slab), ("xl", "t"))
    own_mixed = own_mixed.reshape(blocks, nt, piece, slab)
    other_mixed = swap(own_mixed, "c")
    pre, worker = call(
        finish,
        [out((full, blocks, slab)), out((1, full, slab))],
        [worker_group],
        [qa, qa_other, own_mixed, other_mixed],
        flops=4 * full * full * slab,
    )

    (grad_input,) = call(
        input_grad, [out((tok, slab))], [], [cot, weight], flops=4 * tok * full * slab
    )
    return grad_input, factor_a, factor_g.transpose(1, 0, 2), pre, worker


def solution(mesh):
    dp, tensor = mesh.devices.shape
    fine = Mesh(mesh.devices.reshape(dp // 4, 2, 2, tensor), ("z", "xl", "c", "t"))
    dp = ("z", "xl", "c")
    return jax.shard_map(
        local,
        mesh=fine,
        in_specs=(
            P(dp, "t"),
            P(dp, None, None),
            P("t", None, None),
            P(),
            P(),
            P(dp, None, "t"),
            P(dp, "t"),
            P(dp, None, None, "t"),
            P(dp, None, "t"),
        ),
        out_specs=(
            P(dp, "t"),
            P(dp, "t"),
            P(dp, None, "t"),
            P(None, None, "t"),
            P(dp, None, "t"),
        ),
        check_vma=False,
    )
```

```python
import functools

import jax
import jax.numpy as jnp
from jax import lax
from jax.experimental import pallas as pl
from jax.experimental.pallas import tpu as pltpu
from jax.sharding import Mesh, PartitionSpec as P

damping = 0.001
f32 = jnp.float32
bf16 = jnp.bfloat16
VALS = 16


def exchange(array, axis):
    return lax.all_to_all(array, axis, 0, 0, tiled=True)


def swap(array, axis):
    return lax.ppermute(array, axis, [(0, 1), (1, 0)])


def across(array, axis, step):
    pairs = [(i, i ^ step) for i in range(lax.axis_size(axis))]
    return lax.ppermute(array, axis, pairs)


def full_block(array):
    return pl.BlockSpec(array.shape, lambda i: (0,) * array.ndim)


def call(body, outs, scalars, args, places=None, scratch=(), flops=0, limit=20):
    specs, arrays = [], []
    for arg, place in zip(args, places or [None] * len(args)):
        if isinstance(arg, tuple):
            array, rows, block = arg
            shape = (array.shape[0], rows, array.shape[2])
            specs.append(pl.BlockSpec(shape, functools.partial(lambda k, i: (0, k, 0), block)))
        else:
            array = arg
            specs.append(pl.BlockSpec(memory_space=place) if place else full_block(array))
        arrays.append(array)
    bytes_all = sum(a.size * a.dtype.itemsize for a in arrays + list(outs))
    return pl.pallas_call(
        body,
        grid=(1,),
        out_shape=outs,
        in_specs=[pl.BlockSpec(memory_space=pltpu.SMEM)] * len(scalars) + specs,
        out_specs=[full_block(o) for o in outs],
        scratch_shapes=list(scratch),
        compiler_params=pltpu.CompilerParams(vmem_limit_bytes=limit * 1024 * 1024),
        cost_estimate=pl.CostEstimate(flops=flops, bytes_accessed=bytes_all, transcendentals=0),
    )(*scalars, *arrays)


def follow(array, after, limit):
    block = (1,) * (after.ndim - 2) + (16, after.shape[-1])
    return pl.pallas_call(
        lambda *refs: None,
        grid=(1,),
        out_shape=jax.ShapeDtypeStruct(array.shape, array.dtype),
        in_specs=[
            pl.BlockSpec(memory_space=pl.ANY),
            pl.BlockSpec(block, lambda i: (0,) * after.ndim),
        ],
        out_specs=pl.BlockSpec(memory_space=pl.ANY),
        input_output_aliases={0: 0},
        compiler_params=pltpu.CompilerParams(vmem_limit_bytes=limit * 1024 * 1024),
    )(array, after)


def out(shape, dtype=bf16):
    return jax.ShapeDtypeStruct(shape, dtype)


def dot(left, right, dims=((1,), (0,))):
    return lax.dot_general(left, right, (dims, ((), ())), preferred_element_type=f32)


def value_rows(flags, own, other):
    place = lax.broadcasted_iota(jnp.int32, own.shape, 0)
    take = jnp.zeros(own.shape, jnp.int32)
    for row, flag in enumerate(flags):
        take = jnp.where(place == row, flag.astype(jnp.int32), take)
    return jnp.where(take > 0, own.astype(f32), other.astype(f32)).astype(bf16)


def choose(flag, ref, place, own, other):
    @pl.when(flag)
    def _():
        ref[place] = own()

    @pl.when(jnp.logical_not(flag))
    def _():
        ref[place] = other()


def pack_bases(ba, bg, va, vg, act, sent, keep, every, sem):
    half = ba.shape[1] // 2
    core = lax.axis_index("c")
    place = lax.broadcasted_iota(jnp.int32, (VALS, ba.shape[2]), 0)
    vals = jnp.where(place == 0, va[...].astype(f32), 0.0)
    for j in range(2):
        row = vg[0].astype(f32)[j : j + 1]
        vals = jnp.where(place == 1 + j, row, vals)
    copies = []
    for side, (ref, who) in enumerate(((sent, 1 - core), (keep, core))):
        rows = pl.ds(pl.multiple_of(who * half, half), half)
        for i in range(3):
            source = ba.at[0, rows] if i == 0 else bg.at[0, i - 1, rows]
            copies.append(
                pltpu.make_async_copy(source, ref.at[i * half : (i + 1) * half], sem.at[side, i])
            )
            copies[-1].start()
    sent[3 * half :] = vals.astype(bf16)
    keep[3 * half :] = vals.astype(bf16)
    for k in range(every.shape[0]):
        every[k] = act[...]
    for copy in copies:
        copy.wait()


def select_core(owners, own, got, sent, keep):
    half = (own.shape[0] - VALS) // 3
    core, xl = lax.axis_index("c"), lax.axis_index("xl")
    flags = [owners[i] % 2 == core for i in range(3)]

    def fill(ref, slot, i):
        start = pl.multiple_of(i * half, half)
        choose(
            owners[i] % 2 == core,
            ref,
            slice(slot * half, (slot + 1) * half),
            lambda: own[pl.ds(start, half)],
            lambda: got[pl.ds(start, half)],
        )

    vals = value_rows(flags, own[3 * half :], got[3 * half :])
    for ref, block in ((sent, 2 - xl), (keep, 1 + xl)):
        fill(ref, 0, 0)
        fill(ref, 1, block)
        ref[2 * half :] = vals


def grad_terms(cot, act, sent, keep, flat):
    blocks, half, slab = keep.shape
    tok, _, full = cot.shape
    nt = full // slab
    scale = 1.0 / (tok * lax.axis_size("z") * 4)
    core = lax.axis_index("c")
    flat[...] = cot[...].reshape(tok, blocks * full)
    for j in range(blocks):
        term = dot(flat[:, j * full : (j + 1) * full], act[...], ((0,), (0,))) * scale
        term = term.reshape(nt, 2, slab // 2, slab)
        for c in range(2):
            part = term[:, c].reshape(half, slab)

            @pl.when(core == c)
            def _():
                keep[j] = part

            @pl.when(core != c)
            def _():
                sent[j] = part.astype(bf16)


def add_core(keep, got, sent, rest):
    xl = lax.axis_index("xl")
    sent[...] = (keep[1 - xl] + got[1 - xl].astype(f32)).astype(bf16)
    rest[...] = keep[xl] + got[xl].astype(f32)


def pack_z(owners, keep, got, own, other, sent, vals):
    nz, _, slab = sent.shape
    half = (own.shape[0] - VALS) // 2
    per = half // nz
    xl = lax.axis_index("xl")
    total = (keep[...] + got[...].astype(f32)).astype(bf16)
    sent[:, 0:per] = total.reshape(nz, per, slab)
    here = [(owners[i] // 2) % 2 == xl for i in range(3)]
    flags = (here[0], (owners[1 + xl] // 2) % 2 == xl)
    for i, flag in enumerate(flags):
        rows = slice(i * half, (i + 1) * half)
        choose(
            flag,
            sent,
            (slice(None), slice((1 + i) * per, (2 + i) * per)),
            lambda: own[rows].reshape(nz, per, slab),
            lambda: other[rows].reshape(nz, per, slab),
        )
    vals[...] = value_rows(here, own[2 * half :], other[2 * half :])


def halve(bit, total, vals, sent, rest):
    count, height, slab = total.shape
    total = total.reshape(count // 2, 2, height, slab)
    rows = count // 2 * height
    mine = (lax.axis_index("z") // bit) % 2
    for side in range(2):

        @pl.when(mine == side)
        def _():
            rest[...] = total[:, side]
            sent[0:rows] = total[:, 1 - side].astype(bf16).reshape(rows, slab)

    sent[rows:] = vals


def join(bit, owners, keep, got, vals):
    count, height, slab = keep.shape
    rows = count * height
    z = lax.axis_index("z")
    flags = [(owners[i] // 4 // bit) % 2 == (z // bit) % 2 for i in range(3)]
    total = keep[...] + got[0:rows].astype(f32).reshape(count, height, slab)
    return total, value_rows(flags, vals[...], got[rows:])


def factor_z(bit, owners, keep, got, vals, sent, rest, chosen):
    total, chosen[...] = join(bit // 2, owners, keep, got, vals)
    halve(bit, total, chosen[...], sent, rest)


def factor_first(keep, got, vals, sent, rest):
    halve(1, keep[...] + got[...].astype(f32), vals[...], sent, rest)


def reduce_z(owners, got, keep, f_got, vals, sent, f_sent, f_rest, chosen):
    nz, height, _ = sent.shape
    per = height // 3
    xl = lax.axis_index("xl")
    total = got[0, 0:per].astype(f32)
    for k in range(1, nz):
        total = total + got[k, 0:per].astype(f32)
    parts = [total.astype(bf16)]
    for i, owner in enumerate((owners[0], owners[1 + xl])):
        parts.append(got[owner // 4, (1 + i) * per : (2 + i) * per])
    for i, part in enumerate(parts):
        for k in range(nz):
            sent[k, i * per : (i + 1) * per] = part
    factor_z(2, owners, keep, f_got, vals, f_sent, f_rest, chosen)


def factor_terms(cot, act, whole, sent, keep, flat, both):
    nz, _, height, slab = keep.shape
    group = height // 3
    tok, blocks, full = cot.shape
    nt = full // slab
    scale = 1.0 / (tok * nz * 4)
    core, t = lax.axis_index("c"), lax.axis_index("t")
    flat[...] = cot[...].reshape(tok, blocks * full)
    for j in range(blocks):
        own = flat[:, pl.ds(pl.multiple_of(j * full + t * slab, slab), slab)]
        both[j] = dot(flat[:, j * full : (j + 1) * full], own, ((0,), (0,))) * scale
    for k in range(nt):
        both[blocks, k * slab : (k + 1) * slab] = dot(whole[k], act[...], ((0,), (0,))) * scale
    for i in range(blocks + 1):
        term = both[i].reshape(nz, 2, 2, group, slab)
        rows = slice(i * group, (i + 1) * group)
        for c in range(2):

            @pl.when(core == c)
            def _():
                keep[:, :, rows] = term[:, :, c]

            @pl.when(core != c)
            def _():
                sent[:, :, rows] = term[:, :, c].astype(bf16)


def factor_core(keep, got, sent, rest):
    xl = lax.axis_index("xl")
    sent[...] = (keep[:, 1 - xl] + got[:, 1 - xl].astype(f32)).astype(bf16)
    rest[...] = keep[:, xl] + got[:, xl].astype(f32)


def pack_t(owners, got, keep, f_got, vals, sent, f_sent, f_rest, chosen):
    nz, height, slab = got.shape
    nt = sent.shape[0]
    per = height // 3
    half = nz * per
    piece = half // nt
    for k in range(nt):
        for i in range(2):
            rows = got[:, (1 + i) * per : (2 + i) * per].reshape(half, slab)
            sent[k, i * half : (i + 1) * half] = rows
    sent[:, 2 * half :] = got[:, 0:per].reshape(nt, piece, slab)
    factor_z(4, owners, keep, f_got, vals, f_sent, f_rest, chosen)


def factor_out(bit, owners, keep, got, vals, factor_a, factor_g, chosen):
    group = factor_a.shape[0]
    total, chosen[...] = join(bit, owners, keep, got, vals)
    for j in range(2):
        factor_g[:, j] = total[0, j * group : (j + 1) * group]
    factor_a[...] = total[0, 2 * group :]


def rotate(own, other, own_grad, other_grad, vals, sent, grad):
    nt, half, slab = own.shape
    piece = slab // 2
    core = lax.axis_index("c")
    mine = pl.multiple_of(core * piece, piece)
    theirs = pl.multiple_of((1 - core) * piece, piece)
    for k in range(nt):
        grad[pl.ds(mine, piece), k * slab : (k + 1) * slab] = own_grad[k]
        grad[pl.ds(theirs, piece), k * slab : (k + 1) * slab] = other_grad[k]
    near = grad[:, pl.ds(pl.multiple_of(core * half, half), half)]
    far = grad[:, pl.ds(pl.multiple_of((1 - core) * half, half), half)]
    for i in range(nt // 2):
        k = core * (nt // 2) + i
        turned = dot(near, own[k]) + dot(far, other[k])
        turned = turned.T.astype(bf16)
        sent[2 * i, 0:piece] = turned[0:piece]
        sent[2 * i + 1, 0:piece] = turned[piece:]
    for k in range(nt):
        sent[k, piece:] = vals[...]


def scale_rows(rows, own, other, sent, rot, scaled, column):
    nt, height, slab = rows.shape
    piece = height - VALS
    half = own.shape[1]
    core, xl, t = lax.axis_index("c"), lax.axis_index("xl"), lax.axis_index("t")
    row = rows[core * (nt // 2) + t // 2, piece:].astype(f32)[0:1]
    column[...] = jnp.broadcast_to(row, (slab, slab)).T
    la = column[pl.ds(pl.multiple_of((t % 2) * piece, piece), piece)]
    for k in range(nt):
        rot[:, k * slab : (k + 1) * slab] = rows[k, 0:piece]
    near = rot[:, pl.ds(pl.multiple_of(core * half, half), half)]
    far = rot[:, pl.ds(pl.multiple_of((1 - core) * half, half), half)]
    for k in range(nt):
        spectral = dot(near, own[k]) + dot(far, other[k])
        values = rows[k, piece:].astype(f32)
        lg = jnp.where(xl == 0, values[1:2], values[2:3])
        scaled[k] = (spectral / (la * lg + damping)).astype(bf16)
    for side, ref in ((core, own), (1 - core, other)):
        mixed = dot(scaled[0], ref[0], ((1,), (1,)))
        for k in range(1, nt):
            mixed = mixed + dot(scaled[k], ref[k], ((1,), (1,)))
        mixed = mixed.astype(bf16)
        for i in range(nt // 2):
            for copy in range(2):
                sent[copy, side * (nt // 2) + i] = mixed[:, i * slab : (i + 1) * slab]


def finish(groups, own, other, own_mixed, other_mixed, pre, worker):
    blocks, nt, piece, slab = own_mixed.shape
    half = own.shape[1]
    core = lax.axis_index("c")
    replica = (lax.axis_index("z") * 2 + lax.axis_index("xl")) * 2 + core
    group = groups[replica]
    for side, ref in ((core, own), (1 - core, other)):
        total = jnp.zeros((half, blocks * slab), f32)
        for part, mixed in ((core, own_mixed), (1 - core, other_mixed)):
            for i in range(nt // 4):
                k = part * (nt // 2) + 2 * i
                left = jnp.concatenate([ref[k], ref[k + 1]], 1)
                right = jnp.concatenate(
                    [mixed[j, 4 * i : 4 * i + 4].reshape(4 * piece, slab) for j in range(blocks)], 1
                )
                total = total + dot(left, right)
        total = total.astype(bf16)
        place = pl.ds(pl.multiple_of(side * half, half), half)
        pre[place] = total.reshape(half, blocks, slab)
        choose(
            group == 0,
            worker,
            (0, place),
            lambda: total[:, :slab],
            lambda: total[:, slab:],
        )


def input_grad(cot, weight, grad):
    tok, blocks, full = cot.shape
    left = cot[...].reshape(tok, blocks * full)
    right = weight[...].reshape(weight.shape[0], blocks * full)
    grad[...] = dot(left, right, ((1,), (1,))).astype(bf16)


def local(act, cot, weight, owners, worker_group, basis_a, values_a, basis_g, values_g):
    tok, slab = act.shape
    blocks, full = cot.shape[1:]
    nz, nt = lax.axis_size("z"), lax.axis_size("t")
    group = full // (nz * 4)
    half, piece = full // 2, slab // 2
    per = half // nz

    shape = (3 * half + VALS, slab)
    sent, keep, every = call(
        pack_bases,
        [out(shape), out(shape), out((nt, tok, slab))],
        [],
        [basis_a, basis_g, values_a, values_g, act],
        [pl.ANY, pl.ANY, None, None, None],
        scratch=[pltpu.SemaphoreType.DMA((2, 3))],
        limit=56,
    )
    got = swap(sent, "c")
    whole_act = exchange(every, "t")
    shape = (2 * half + VALS, slab)
    sent, base = call(select_core, [out(shape), out(shape)], [owners], [keep, got])
    base_got = swap(sent, "xl")

    flat = pltpu.VMEM((tok, blocks * full), bf16)
    shape = (blocks, half, slab)
    sent, keep = call(
        grad_terms,
        [out(shape), out(shape, f32)],
        [],
        [cot, act],
        scratch=[flat],
        flops=4 * tok * full * slab,
    )
    got = swap(sent, "c")
    sent, keep = call(add_core, [out(shape[1:]), out(shape[1:], f32)], [], [keep, got])
    got = swap(sent, "xl")

    sent, vals = call(
        pack_z,
        [out((nz, 3 * per, slab)), out((VALS, slab))],
        [owners],
        [keep, got, base, base_got],
    )
    got = exchange(follow(sent, whole_act, 56), "z")

    height = (blocks + 1) * group
    shape = (nz, 2, height, slab)
    sent, f_keep = call(
        factor_terms,
        [out(shape), out(shape, f32)],
        [],
        [cot, act, whole_act],
        scratch=[flat, pltpu.VMEM((blocks + 1, full, slab), f32)],
        flops=6 * tok * full * slab,
        limit=56,
    )
    f_got = swap(sent, "c")
    shape = (nz, height, slab)
    sent, f_keep = call(factor_core, [out(shape), out(shape, f32)], [], [f_keep, f_got])
    f_got = swap(sent, "xl")

    def step_outs(count):
        return [out((count * height + VALS, slab)), out((count, height, slab), f32)]

    f_sent, f_keep = call(factor_first, step_outs(nz // 2), [], [f_keep, f_got, vals])
    f_got = across(f_sent, "z", 1)

    chosen = out((VALS, slab))
    sent, f_sent, f_keep, vals = call(
        reduce_z,
        [out((nz, 3 * per, slab))] + step_outs(nz // 4) + [chosen],
        [owners],
        [got, f_keep, f_got, vals],
    )
    got = exchange(sent, "z")
    f_got = across(f_sent, "z", 2)

    sent, f_sent, f_keep, vals = call(
        pack_t,
        [out((nt, 2 * half + piece, slab))] + step_outs(nz // 8) + [chosen],
        [owners],
        [got, f_keep, f_got, vals],
    )
    own = exchange(sent, "t")
    f_got = across(f_sent, "z", 4)
    f_sent, f_keep, vals = call(
        functools.partial(factor_z, 8),
        step_outs(nz // 16) + [chosen],
        [owners],
        [f_keep, f_got, vals],
    )
    f_got = across(f_sent, "z", 8)
    factor_a, factor_g, vals = call(
        functools.partial(factor_out, nz // 2),
        [out((group, slab), f32), out((group, blocks, slab), f32), chosen],
        [owners],
        [f_keep, f_got, vals],
    )
    own = follow(own, vals, 20)
    other = swap(own, "c")
    qa, qa_other = (own, half, 0), (other, half, 0)
    qg, qg_other = (own, half, 1), (other, half, 1)
    columns, columns_other = (own, piece, 2 * half // piece), (other, piece, 2 * half // piece)
    (sent,) = call(
        rotate,
        [out((nt, piece + VALS, slab))],
        [],
        [qa, qa_other, columns, columns_other, vals],
        scratch=[pltpu.VMEM((slab, full), bf16)],
        flops=2 * slab * full * half,
    )
    rows = exchange(sent, "t")
    (sent,) = call(
        scale_rows,
        [out((blocks, nt, piece, slab))],
        [],
        [rows, qg, qg_other],
        scratch=[
            pltpu.VMEM((piece, full), bf16),
            pltpu.VMEM((nt, piece, slab), bf16),
            pltpu.VMEM((slab, slab), f32),
        ],
        flops=4 * piece * full * full,
    )
    own_mixed = exchange(sent.reshape(blocks * nt, piece, slab), ("xl", "t"))
    own_mixed = own_mixed.reshape(blocks, nt, piece, slab)
    other_mixed = swap(own_mixed, "c")
    pre, worker = call(
        finish,
        [out((full, blocks, slab)), out((1, full, slab))],
        [worker_group],
        [qa, qa_other, own_mixed, other_mixed],
        flops=4 * full * full * slab,
    )

    (grad_input,) = call(
        input_grad, [out((tok, slab))], [], [cot, weight], flops=4 * tok * full * slab
    )
    return grad_input, factor_a, factor_g, pre, worker


def solution(mesh):
    dp, tensor = mesh.devices.shape
    fine = Mesh(mesh.devices.reshape(dp // 4, 2, 2, tensor), ("z", "xl", "c", "t"))
    dp = ("z", "xl", "c")
    return jax.shard_map(
        local,
        mesh=fine,
        in_specs=(
            P(dp, "t"),
            P(dp, None, None),
            P("t", None, None),
            P(),
            P(),
            P(dp, None, "t"),
            P(dp, "t"),
            P(dp, None, None, "t"),
            P(dp, None, "t"),
        ),
        out_specs=(
            P(dp, "t"),
            P(dp, "t"),
            P(dp, None, "t"),
            P(None, None, "t"),
            P(dp, None, "t"),
        ),
        check_vma=False,
    )
```

```python
import functools

import jax
import jax.numpy as jnp
from jax import lax
from jax.experimental import pallas as pl
from jax.experimental.pallas import tpu as pltpu
from jax.sharding import Mesh, PartitionSpec as P

damping = 0.001
f32 = jnp.float32
bf16 = jnp.bfloat16
VALS = 16


def exchange(array, axis):
    return lax.all_to_all(array, axis, 0, 0, tiled=True)


def swap(array, axis):
    return lax.ppermute(array, axis, [(0, 1), (1, 0)])


def across(array, axis, step):
    pairs = [(i, i ^ step) for i in range(lax.axis_size(axis))]
    return lax.ppermute(array, axis, pairs)


def full_block(array):
    return pl.BlockSpec(array.shape, lambda i: (0,) * array.ndim)


def call(body, outs, scalars, args, places=None, scratch=(), flops=0, limit=20):
    specs, arrays = [], []
    for arg, place in zip(args, places or [None] * len(args)):
        if isinstance(arg, tuple):
            array, rows, block = arg
            shape = (array.shape[0], rows, array.shape[2])
            specs.append(pl.BlockSpec(shape, functools.partial(lambda k, i: (0, k, 0), block)))
        else:
            array = arg
            specs.append(pl.BlockSpec(memory_space=place) if place else full_block(array))
        arrays.append(array)
    bytes_all = sum(a.size * a.dtype.itemsize for a in arrays + list(outs))
    return pl.pallas_call(
        body,
        grid=(1,),
        out_shape=outs,
        in_specs=[pl.BlockSpec(memory_space=pltpu.SMEM)] * len(scalars) + specs,
        out_specs=[full_block(o) for o in outs],
        scratch_shapes=list(scratch),
        compiler_params=pltpu.CompilerParams(vmem_limit_bytes=limit * 1024 * 1024),
        cost_estimate=pl.CostEstimate(flops=flops, bytes_accessed=bytes_all, transcendentals=0),
    )(*scalars, *arrays)


def follow(array, after, limit):
    return pl.pallas_call(
        lambda *refs: None,
        out_shape=jax.ShapeDtypeStruct(array.shape, array.dtype),
        in_specs=[pl.BlockSpec(memory_space=pl.ANY)] * 2,
        out_specs=pl.BlockSpec(memory_space=pl.ANY),
        input_output_aliases={0: 0},
        compiler_params=pltpu.CompilerParams(vmem_limit_bytes=limit * 1024 * 1024),
    )(array, after)


def out(shape, dtype=bf16):
    return jax.ShapeDtypeStruct(shape, dtype)


def dot(left, right, dims=((1,), (0,))):
    return lax.dot_general(left, right, (dims, ((), ())), preferred_element_type=f32)


def value_rows(flags, own, other):
    place = lax.broadcasted_iota(jnp.int32, own.shape, 0)
    take = jnp.zeros(own.shape, jnp.int32)
    for row, flag in enumerate(flags):
        take = jnp.where(place == row, flag.astype(jnp.int32), take)
    return jnp.where(take > 0, own.astype(f32), other.astype(f32)).astype(bf16)


def choose(flag, ref, place, own, other):
    @pl.when(flag)
    def _():
        ref[place] = own()

    @pl.when(jnp.logical_not(flag))
    def _():
        ref[place] = other()


def pack_bases(ba, bg, va, vg, act, sent, keep, every, sem):
    half = ba.shape[1] // 2
    core = lax.axis_index("c")
    place = lax.broadcasted_iota(jnp.int32, (VALS, ba.shape[2]), 0)
    vals = jnp.where(place == 0, va[...].astype(f32), 0.0)
    for j in range(2):
        row = vg[0].astype(f32)[j : j + 1]
        vals = jnp.where(place == 1 + j, row, vals)
    copies = []
    for side, (ref, who) in enumerate(((sent, 1 - core), (keep, core))):
        rows = pl.ds(pl.multiple_of(who * half, half), half)
        for i in range(3):
            source = ba.at[0, rows] if i == 0 else bg.at[0, i - 1, rows]
            copies.append(
                pltpu.make_async_copy(source, ref.at[i * half : (i + 1) * half], sem.at[side, i])
            )
            copies[-1].start()
    sent[3 * half :] = vals.astype(bf16)
    keep[3 * half :] = vals.astype(bf16)
    for k in range(every.shape[0]):
        every[k] = act[...]
    for copy in copies:
        copy.wait()


def select_core(owners, own, got, sent, keep):
    half = (own.shape[0] - VALS) // 3
    core, xl = lax.axis_index("c"), lax.axis_index("xl")
    flags = [owners[i] % 2 == core for i in range(3)]

    def fill(ref, slot, i):
        start = pl.multiple_of(i * half, half)
        choose(
            owners[i] % 2 == core,
            ref,
            slice(slot * half, (slot + 1) * half),
            lambda: own[pl.ds(start, half)],
            lambda: got[pl.ds(start, half)],
        )

    vals = value_rows(flags, own[3 * half :], got[3 * half :])
    for ref, block in ((sent, 2 - xl), (keep, 1 + xl)):
        fill(ref, 0, 0)
        fill(ref, 1, block)
        ref[2 * half :] = vals


def grad_terms(cot, act, sent, keep, flat):
    blocks, half, slab = keep.shape
    tok, _, full = cot.shape
    nt = full // slab
    scale = 1.0 / (tok * lax.axis_size("z") * 4)
    core = lax.axis_index("c")
    flat[...] = cot[...].reshape(tok, blocks * full)
    for j in range(blocks):
        term = dot(flat[:, j * full : (j + 1) * full], act[...], ((0,), (0,))) * scale
        term = term.reshape(nt, 2, slab // 2, slab)
        for c in range(2):
            part = term[:, c].reshape(half, slab)

            @pl.when(core == c)
            def _():
                keep[j] = part

            @pl.when(core != c)
            def _():
                sent[j] = part.astype(bf16)


def add_core(keep, got, sent, rest):
    xl = lax.axis_index("xl")
    sent[...] = (keep[1 - xl] + got[1 - xl].astype(f32)).astype(bf16)
    rest[...] = keep[xl] + got[xl].astype(f32)


def pack_z(owners, keep, got, own, other, sent, vals):
    nz, _, slab = sent.shape
    half = (own.shape[0] - VALS) // 2
    per = half // nz
    xl = lax.axis_index("xl")
    total = (keep[...] + got[...].astype(f32)).astype(bf16)
    sent[:, 0:per] = total.reshape(nz, per, slab)
    here = [(owners[i] // 2) % 2 == xl for i in range(3)]
    flags = (here[0], (owners[1 + xl] // 2) % 2 == xl)
    for i, flag in enumerate(flags):
        rows = slice(i * half, (i + 1) * half)
        choose(
            flag,
            sent,
            (slice(None), slice((1 + i) * per, (2 + i) * per)),
            lambda: own[rows].reshape(nz, per, slab),
            lambda: other[rows].reshape(nz, per, slab),
        )
    vals[...] = value_rows(here, own[2 * half :], other[2 * half :])


def halve(bit, total, vals, sent, rest):
    count, height, slab = total.shape
    total = total.reshape(count // 2, 2, height, slab)
    rows = count // 2 * height
    mine = (lax.axis_index("z") // bit) % 2
    for side in range(2):

        @pl.when(mine == side)
        def _():
            rest[...] = total[:, side]
            sent[0:rows] = total[:, 1 - side].astype(bf16).reshape(rows, slab)

    sent[rows:] = vals


def join(bit, owners, keep, got, vals):
    count, height, slab = keep.shape
    rows = count * height
    z = lax.axis_index("z")
    flags = [(owners[i] // 4 // bit) % 2 == (z // bit) % 2 for i in range(3)]
    total = keep[...] + got[0:rows].astype(f32).reshape(count, height, slab)
    return total, value_rows(flags, vals[...], got[rows:])


def factor_z(bit, owners, keep, got, vals, sent, rest, chosen):
    total, chosen[...] = join(bit // 2, owners, keep, got, vals)
    halve(bit, total, chosen[...], sent, rest)


def factor_first(keep, got, vals, sent, rest):
    halve(1, keep[...] + got[...].astype(f32), vals[...], sent, rest)


def reduce_z(owners, got, keep, f_got, vals, sent, f_sent, f_rest, chosen):
    nz, height, _ = sent.shape
    per = height // 3
    xl = lax.axis_index("xl")
    total = got[0, 0:per].astype(f32)
    for k in range(1, nz):
        total = total + got[k, 0:per].astype(f32)
    parts = [total.astype(bf16)]
    for i, owner in enumerate((owners[0], owners[1 + xl])):
        parts.append(got[owner // 4, (1 + i) * per : (2 + i) * per])
    for i, part in enumerate(parts):
        for k in range(nz):
            sent[k, i * per : (i + 1) * per] = part
    factor_z(2, owners, keep, f_got, vals, f_sent, f_rest, chosen)


def factor_terms(cot, act, whole, sent, keep, flat, both):
    nz, _, height, slab = keep.shape
    group = height // 3
    tok, blocks, full = cot.shape
    nt = full // slab
    scale = 1.0 / (tok * nz * 4)
    core, t = lax.axis_index("c"), lax.axis_index("t")
    flat[...] = cot[...].reshape(tok, blocks * full)
    for j in range(blocks):
        own = flat[:, pl.ds(pl.multiple_of(j * full + t * slab, slab), slab)]
        both[j] = dot(flat[:, j * full : (j + 1) * full], own, ((0,), (0,))) * scale
    for k in range(nt):
        both[blocks, k * slab : (k + 1) * slab] = dot(whole[k], act[...], ((0,), (0,))) * scale
    for i in range(blocks + 1):
        term = both[i].reshape(nz, 2, 2, group, slab)
        rows = slice(i * group, (i + 1) * group)
        for c in range(2):

            @pl.when(core == c)
            def _():
                keep[:, :, rows] = term[:, :, c]

            @pl.when(core != c)
            def _():
                sent[:, :, rows] = term[:, :, c].astype(bf16)


def factor_core(keep, got, sent, rest):
    xl = lax.axis_index("xl")
    sent[...] = (keep[:, 1 - xl] + got[:, 1 - xl].astype(f32)).astype(bf16)
    rest[...] = keep[:, xl] + got[:, xl].astype(f32)


def pack_t(owners, got, keep, f_got, vals, sent, f_sent, f_rest, chosen):
    nz, height, slab = got.shape
    nt = sent.shape[0]
    per = height // 3
    half = nz * per
    piece = half // nt
    for k in range(nt):
        for i in range(2):
            rows = got[:, (1 + i) * per : (2 + i) * per].reshape(half, slab)
            sent[k, i * half : (i + 1) * half] = rows
    sent[:, 2 * half :] = got[:, 0:per].reshape(nt, piece, slab)
    factor_z(4, owners, keep, f_got, vals, f_sent, f_rest, chosen)


def factor_out(bit, owners, keep, got, vals, factor_a, factor_g, chosen):
    group = factor_a.shape[0]
    total, chosen[...] = join(bit, owners, keep, got, vals)
    for j in range(2):
        factor_g[:, j] = total[0, j * group : (j + 1) * group]
    factor_a[...] = total[0, 2 * group :]


def rotate(own, other, own_grad, other_grad, vals, sent, grad):
    nt, half, slab = own.shape
    piece = slab // 2
    core = lax.axis_index("c")
    mine = pl.multiple_of(core * piece, piece)
    theirs = pl.multiple_of((1 - core) * piece, piece)
    for k in range(nt):
        grad[pl.ds(mine, piece), k * slab : (k + 1) * slab] = own_grad[k]
        grad[pl.ds(theirs, piece), k * slab : (k + 1) * slab] = other_grad[k]
    near = grad[:, pl.ds(pl.multiple_of(core * half, half), half)]
    far = grad[:, pl.ds(pl.multiple_of((1 - core) * half, half), half)]
    for i in range(nt // 2):
        k = core * (nt // 2) + i
        turned = dot(near, own[k]) + dot(far, other[k])
        turned = turned.T.astype(bf16)
        sent[2 * i, 0:piece] = turned[0:piece]
        sent[2 * i + 1, 0:piece] = turned[piece:]
    for k in range(nt):
        sent[k, piece:] = vals[...]


def scale_rows(rows, own, other, sent, rot, scaled, column):
    nt, height, slab = rows.shape
    piece = height - VALS
    half = own.shape[1]
    core, xl, t = lax.axis_index("c"), lax.axis_index("xl"), lax.axis_index("t")
    row = rows[core * (nt // 2) + t // 2, piece:].astype(f32)[0:1]
    column[...] = jnp.broadcast_to(row, (slab, slab)).T
    la = column[pl.ds(pl.multiple_of((t % 2) * piece, piece), piece)]
    for k in range(nt):
        rot[:, k * slab : (k + 1) * slab] = rows[k, 0:piece]
    near = rot[:, pl.ds(pl.multiple_of(core * half, half), half)]
    far = rot[:, pl.ds(pl.multiple_of((1 - core) * half, half), half)]
    for k in range(nt):
        spectral = dot(near, own[k]) + dot(far, other[k])
        values = rows[k, piece:].astype(f32)
        lg = jnp.where(xl == 0, values[1:2], values[2:3])
        scaled[k] = (spectral / (la * lg + damping)).astype(bf16)
    for side, ref in ((core, own), (1 - core, other)):
        mixed = dot(scaled[0], ref[0], ((1,), (1,)))
        for k in range(1, nt):
            mixed = mixed + dot(scaled[k], ref[k], ((1,), (1,)))
        mixed = mixed.astype(bf16)
        for i in range(nt // 2):
            for copy in range(2):
                sent[copy, side * (nt // 2) + i] = mixed[:, i * slab : (i + 1) * slab]


def finish(groups, own, other, own_mixed, other_mixed, pre, worker):
    blocks, nt, piece, slab = own_mixed.shape
    half = own.shape[1]
    core = lax.axis_index("c")
    replica = (lax.axis_index("z") * 2 + lax.axis_index("xl")) * 2 + core
    group = groups[replica]
    for side, ref in ((core, own), (1 - core, other)):
        total = jnp.zeros((half, blocks * slab), f32)
        for part, mixed in ((core, own_mixed), (1 - core, other_mixed)):
            for i in range(nt // 4):
                k = part * (nt // 2) + 2 * i
                left = jnp.concatenate([ref[k], ref[k + 1]], 1)
                right = jnp.concatenate(
                    [mixed[j, 4 * i : 4 * i + 4].reshape(4 * piece, slab) for j in range(blocks)], 1
                )
                total = total + dot(left, right)
        total = total.astype(bf16)
        place = pl.ds(pl.multiple_of(side * half, half), half)
        pre[place] = total.reshape(half, blocks, slab)
        choose(
            group == 0,
            worker,
            (0, place),
            lambda: total[:, :slab],
            lambda: total[:, slab:],
        )


def input_grad(cot, weight, grad):
    tok, blocks, full = cot.shape
    left = cot[...].reshape(tok, blocks * full)
    right = weight[...].reshape(weight.shape[0], blocks * full)
    grad[...] = dot(left, right, ((1,), (1,))).astype(bf16)


def local(act, cot, weight, owners, worker_group, basis_a, values_a, basis_g, values_g):
    tok, slab = act.shape
    blocks, full = cot.shape[1:]
    nz, nt = lax.axis_size("z"), lax.axis_size("t")
    group = full // (nz * 4)
    half, piece = full // 2, slab // 2
    per = half // nz

    shape = (3 * half + VALS, slab)
    sent, keep, every = call(
        pack_bases,
        [out(shape), out(shape), out((nt, tok, slab))],
        [],
        [basis_a, basis_g, values_a, values_g, act],
        [pl.ANY, pl.ANY, None, None, None],
        scratch=[pltpu.SemaphoreType.DMA((2, 3))],
        limit=56,
    )
    got = swap(sent, "c")
    whole_act = exchange(every, "t")
    shape = (2 * half + VALS, slab)
    sent, base = call(select_core, [out(shape), out(shape)], [owners], [keep, got])
    base_got = swap(sent, "xl")

    flat = pltpu.VMEM((tok, blocks * full), bf16)
    shape = (blocks, half, slab)
    sent, keep = call(
        grad_terms,
        [out(shape), out(shape, f32)],
        [],
        [cot, act],
        scratch=[flat],
        flops=4 * tok * full * slab,
    )
    got = swap(sent, "c")
    sent, keep = call(add_core, [out(shape[1:]), out(shape[1:], f32)], [], [keep, got])
    got = swap(sent, "xl")

    sent, vals = call(
        pack_z,
        [out((nz, 3 * per, slab)), out((VALS, slab))],
        [owners],
        [keep, got, base, base_got],
    )
    got = exchange(sent, "z")

    height = (blocks + 1) * group
    shape = (nz, 2, height, slab)
    sent, f_keep = call(
        factor_terms,
        [out(shape), out(shape, f32)],
        [],
        [cot, act, whole_act],
        scratch=[flat, pltpu.VMEM((blocks + 1, full, slab), f32)],
        flops=6 * tok * full * slab,
    )
    f_got = swap(sent, "c")
    shape = (nz, height, slab)
    sent, f_keep = call(factor_core, [out(shape), out(shape, f32)], [], [f_keep, f_got])
    f_got = swap(sent, "xl")

    def step_outs(count):
        return [out((count * height + VALS, slab)), out((count, height, slab), f32)]

    f_sent, f_keep = call(factor_first, step_outs(nz // 2), [], [f_keep, f_got, vals])
    f_got = across(f_sent, "z", 1)

    chosen = out((VALS, slab))
    sent, f_sent, f_keep, vals = call(
        reduce_z,
        [out((nz, 3 * per, slab))] + step_outs(nz // 4) + [chosen],
        [owners],
        [got, f_keep, f_got, vals],
    )
    got = exchange(sent, "z")
    f_got = across(f_sent, "z", 2)

    sent, f_sent, f_keep, vals = call(
        pack_t,
        [out((nt, 2 * half + piece, slab))] + step_outs(nz // 8) + [chosen],
        [owners],
        [got, f_keep, f_got, vals],
    )
    own = exchange(sent, "t")
    f_got = across(f_sent, "z", 4)
    f_sent, f_keep, vals = call(
        functools.partial(factor_z, 8),
        step_outs(nz // 16) + [chosen],
        [owners],
        [f_keep, f_got, vals],
    )
    f_got = across(f_sent, "z", 8)
    factor_a, factor_g, vals = call(
        functools.partial(factor_out, nz // 2),
        [out((group, slab), f32), out((group, blocks, slab), f32), chosen],
        [owners],
        [f_keep, f_got, vals],
    )
    own = follow(own, vals, 20)
    other = swap(own, "c")
    qa, qa_other = (own, half, 0), (other, half, 0)
    qg, qg_other = (own, half, 1), (other, half, 1)
    columns, columns_other = (own, piece, 2 * half // piece), (other, piece, 2 * half // piece)
    (sent,) = call(
        rotate,
        [out((nt, piece + VALS, slab))],
        [],
        [qa, qa_other, columns, columns_other, vals],
        scratch=[pltpu.VMEM((slab, full), bf16)],
        flops=2 * slab * full * half,
    )
    rows = exchange(sent, "t")
    (sent,) = call(
        scale_rows,
        [out((blocks, nt, piece, slab))],
        [],
        [rows, qg, qg_other],
        scratch=[
            pltpu.VMEM((piece, full), bf16),
            pltpu.VMEM((nt, piece, slab), bf16),
            pltpu.VMEM((slab, slab), f32),
        ],
        flops=4 * piece * full * full,
    )
    own_mixed = exchange(sent.reshape(blocks * nt, piece, slab), ("xl", "t"))
    own_mixed = own_mixed.reshape(blocks, nt, piece, slab)
    other_mixed = swap(own_mixed, "c")
    pre, worker = call(
        finish,
        [out((full, blocks, slab)), out((1, full, slab))],
        [worker_group],
        [qa, qa_other, own_mixed, other_mixed],
        flops=4 * full * full * slab,
    )

    (grad_input,) = call(
        input_grad, [out((tok, slab))], [], [cot, weight], flops=4 * tok * full * slab
    )
    return grad_input, factor_a, factor_g, pre, worker


def solution(mesh):
    dp, tensor = mesh.devices.shape
    fine = Mesh(mesh.devices.reshape(dp // 4, 2, 2, tensor), ("z", "xl", "c", "t"))
    dp = ("z", "xl", "c")
    return jax.shard_map(
        local,
        mesh=fine,
        in_specs=(
            P(dp, "t"),
            P(dp, None, None),
            P("t", None, None),
            P(),
            P(),
            P(dp, None, "t"),
            P(dp, "t"),
            P(dp, None, None, "t"),
            P(dp, None, "t"),
        ),
        out_specs=(
            P(dp, "t"),
            P(dp, "t"),
            P(dp, None, "t"),
            P(None, None, "t"),
            P(dp, None, "t"),
        ),
        check_vma=False,
    )
```
